32 devices in a mesh: dp: 2 (over y), tensor: 4 (over x, core), context: 4 (over z).
Axes of the slice: x: 2, y: 2, z: 4, core: 2. Of those that a mesh axis runs over, the one named last changes fastest.
Arguments:
- q_in: bfloat16 [2, 512, 4096], P('dp', 'context', 'tensor'), may hold values from -44 to 44
- k_in: bfloat16 [2, 512, 4096], P('dp', 'context', 'tensor'), may hold values from -6 to 6
- v_in: bfloat16 [2, 512, 4096], P('dp', 'context', 'tensor'), may hold values from -6 to 6
- short_filt: float32 [3, 7, 4096], P(None, None, 'tensor'), may hold values from -2 to 2
- long_filt: float32 [512, 4096], P('context', 'tensor'), may hold values from -1.1 to 1.1
- norm_gain: float32 [4096], P('tensor'), may hold values from 0.1 to 1.9
- grad_out: bfloat16 [2, 512, 4096], P('dp', 'context', 'tensor'), may hold values from -6 to 6
Outputs:
- mixed: bfloat16 [2, 512, 4096], P('dp', 'context', 'tensor')
- grad_inputs: bfloat16 [3, 2, 512, 4096], P(None, 'dp', 'context', 'tensor')
- grad_long: float32 [512, 4096], P('context', 'tensor')
- grad_short: float32 [3, 7, 4096], P(None, None, 'tensor')
The draws below stay inside these ranges and needn't reach their ends.
All inputs are finite; a program needn't handle non-finite values.
Results may differ from the reference program's by a relative error of at most 0.00225.
Values may be sent and summed in bfloat16 or wider, within the bound.
A program may use at most 128 MiB of HBM per device.

```python
import math
import jax
import jax.numpy as jnp
from jax import lax

D = 4096
FILT = 7
REPL = 2
SEQ = 512


def draw_q_in(key, part):
    first, second, third = jax.random.split(jax.random.fold_in(key, 11), 3)
    column = jnp.exp(jax.random.uniform(first, (D,)) * math.log(10.0) * 0.6 + math.log(3.0) * jnp.arange(D, dtype=jnp.float32) / D) / (2.0 * math.sqrt(3.0))
    row_scale = jnp.exp(jax.random.uniform(second, (REPL, SEQ, 1)) * math.log(10.0)) / math.sqrt(10.0)
    noise = jax.random.truncated_normal(third, -4.0, 4.0, (REPL, SEQ, D))
    return (noise * row_scale * column).astype(jnp.bfloat16)


def draw_long_filt(key, part):
    first, second = jax.random.split(jax.random.fold_in(key, 23), 2)
    decay = jnp.exp(jax.random.uniform(first, (D,), minval=math.log(30.0), maxval=math.log(4.0 * SEQ)))
    noise = jax.random.truncated_normal(second, -4.0, 4.0, (SEQ, D))
    position = jnp.arange(SEQ, dtype=jnp.float32)[:, None]
    amplitude = jnp.sqrt(1.0 - jnp.exp(-2.0 / decay))
    return (noise * amplitude * jnp.exp(-position / decay)).astype(jnp.float32)


def steps_of(own_key, extent, pieces, low, high):
    gain = 1.0
    for dim, parts in pieces:
        draws = jax.random.uniform(jax.random.fold_in(jax.random.fold_in(own_key, 6), dim), (parts,), jnp.float32, low / len(pieces), high / len(pieces))
        gain = gain * jnp.repeat(jnp.exp(draws), extent[dim] // parts).reshape((-1,) + (1,) * (len(extent) - 1 - dim))
    return gain


def gaussian(rng, dims, scale, reach, cuts=(), held_as=jnp.bfloat16):
    result = jax.random.normal(rng, dims, jnp.float32) * scale
    if len(cuts) > 0:
        result = steps_of(rng, dims, cuts, -0.22, 0.18) * result
    return jnp.clip(result, min=-reach, max=reach).astype(held_as)


def setup_inputs(seed: int = 0) -> dict:
    key_list = jax.random.split(jax.random.key(seed), 8)
    return {
        "q_in": draw_q_in(jax.random.fold_in(key_list[7], 71), 0),
        "k_in": gaussian(key_list[1], (REPL, SEQ, D), 1.0, 6.0, ((0, 2), (1, 4), (2, 4))),
        "v_in": gaussian(key_list[2], (REPL, SEQ, D), 1.0, 6.0, ((0, 2), (1, 4), (2, 4))),
        "short_filt": gaussian(key_list[3], (3, FILT, D), FILT ** -0.5, 2.0, ((2, 4),), jnp.float32),
        "long_filt": draw_long_filt(jax.random.fold_in(key_list[7], 71), 0),
        "norm_gain": jnp.clip(1.0 + 0.18 * jax.random.normal(key_list[5], (D,), jnp.float32), 0.1, 1.9),
        "grad_out": gaussian(key_list[6], (REPL, SEQ, D), 1.0, 6.0, ((0, 2), (1, 4), (2, 4))),
    }


EPS = 1e-06

def causal_short(seq, filt):
    padded = jnp.pad(seq, ((0, 0), (FILT - 1, 0), (0, 0)))
    total = jnp.zeros(seq.shape, jnp.float32)
    for lag in range(FILT):
        total = total + filt[lag] * padded[:, FILT - 1 - lag:FILT - 1 - lag + SEQ]
    return (total, padded)

def back_short(grads, filt):
    padded = jnp.pad(grads, ((0, 0), (0, FILT - 1), (0, 0)))
    total = jnp.zeros(grads.shape, jnp.float32)
    for lag in range(FILT):
        total = total + filt[lag] * padded[:, lag:lag + SEQ]
    return total

def filter_grads(grads, padded):
    return jnp.stack([lax.optimization_barrier(jnp.sum(grads * padded[:, FILT - 1 - lag:FILT - 1 - lag + SEQ], axis=(0, 1))) for lag in range(FILT)])

def to_blocks(values, width):
    return values.reshape(values.shape[0], SEQ, D // width, width).transpose(2, 0, 1, 3)

def from_blocks(values):
    return values.transpose(1, 2, 0, 3).reshape(values.shape[1], SEQ, D)

def conv_pair(pair):
    kv_block, filt_block = pair
    length = 2 * SEQ
    spec = jnp.fft.rfft(kv_block, n=length, axis=1) * jnp.fft.rfft(filt_block, n=length, axis=0)[None]
    return jnp.fft.irfft(spec, n=length, axis=1)[:, :SEQ]

def back_triple(triple):
    grad_block, kv_block, filt_block = triple
    length = 2 * SEQ
    grad_spec = jnp.fft.rfft(grad_block, n=length, axis=1)
    kv_spec = jnp.fft.rfft(kv_block, n=length, axis=1)
    filt_spec = jnp.fft.rfft(filt_block, n=length, axis=0)[None]
    dkv = jnp.fft.irfft(jnp.conj(filt_spec) * grad_spec, n=length, axis=1)[:, :SEQ]
    dfilt = lax.optimization_barrier(jnp.sum(jnp.fft.irfft(jnp.conj(kv_spec) * grad_spec, n=length, axis=1)[:, :SEQ], axis=0))
    return (dkv, dfilt)

def reference(q_in, k_in, v_in, short_filt, long_filt, norm_gain, grad_out):
    width = math.gcd(D, 256)
    q_short, q_pad = causal_short(q_in.astype(jnp.float32), short_filt[0])
    k_short, k_pad = causal_short(k_in.astype(jnp.float32), short_filt[1])
    v_short, v_pad = causal_short(v_in.astype(jnp.float32), short_filt[2])
    kv = k_short * v_short
    filt_blocks = long_filt.reshape(SEQ, D // width, width).transpose(1, 0, 2)
    conv = from_blocks(lax.map(conv_pair, (to_blocks(kv, width), filt_blocks)))
    y_out = q_short * conv
    rms = jnp.sqrt(lax.optimization_barrier(jnp.mean(y_out * y_out, axis=-1, keepdims=True)) + EPS)
    mixed = (y_out / rms * norm_gain).astype(jnp.bfloat16)
    grad_z = grad_out.astype(jnp.float32) * norm_gain
    prods = lax.optimization_barrier(jnp.sum(grad_z * y_out, axis=-1, keepdims=True))
    grad_y = grad_z / rms - y_out * prods / (D * rms ** 3)
    dconv = grad_y * q_short
    grad_q = grad_y * conv
    dkv_blocks, dfilt_blocks = lax.map(back_triple, (to_blocks(dconv, width), to_blocks(kv, width), filt_blocks))
    dkv = from_blocks(dkv_blocks)
    dfilt = dfilt_blocks.transpose(1, 0, 2).reshape(SEQ, D)
    grad_k = dkv * v_short
    grad_v = dkv * k_short
    scale = 1.0 / math.sqrt(REPL * SEQ)
    grad_inputs = jnp.stack([back_short(grad_q, short_filt[0]), back_short(grad_k, short_filt[1]), back_short(grad_v, short_filt[2])]).astype(jnp.bfloat16)
    grad_short = jnp.stack([filter_grads(grad_q, q_pad), filter_grads(grad_k, k_pad), filter_grads(grad_v, v_pad)]) * scale
    return (mixed, grad_inputs, dfilt * scale, grad_short)
```

```python
import functools
import math

import jax
import jax.numpy as jnp
import numpy as np
from jax import lax
from jax.experimental import pallas as pl
from jax.experimental.pallas import tpu as pltpu
from jax.sharding import PartitionSpec as P

D = 4096
FILT = 7


EPS = 1e-06
HIGH = lax.Precision.HIGHEST


def passed_along(shard, axis, by):
    peers = lax.axis_size(axis)
    pairs = [(i, i + by) for i in range(peers) if 0 <= i + by < peers]
    return lax.ppermute(shard, axis, pairs)


def phases(first, second, modulus):
    product = first[:, None] * second[None, :] % modulus
    return product.astype(jnp.float32) * (2.0 * math.pi / modulus)


def block_table(block_len, sign):
    index = jnp.arange(block_len, dtype=jnp.int32)
    angle = phases(index, index, block_len)
    cosine = jnp.cos(angle)
    sine = jnp.sin(angle) * sign
    return jnp.stack([jnp.stack([cosine, sine]), jnp.stack([-sine, cosine])])


def forward_rows(values, modulus):
    count, block_len, width = values.shape
    ctx_size = lax.axis_size("context")
    sub_len = block_len // ctx_size
    spread = lax.all_to_all(
        values.reshape(count, 1, block_len, width),
        "context",
        split_axis=2,
        concat_axis=1,
        tiled=True,
    )
    freq = jnp.arange(2 * ctx_size, dtype=jnp.int32)
    place = (
        jnp.arange(ctx_size, dtype=jnp.int32)[:, None] * block_len
        + lax.axis_index("context") * sub_len
        + jnp.arange(sub_len, dtype=jnp.int32)[None, :]
    )
    angle = (freq[:, None, None] * place[None] % modulus).astype(jnp.float32) * (
        2.0 * math.pi / modulus
    )
    table = jnp.stack([jnp.cos(angle), -jnp.sin(angle)])
    turned = jnp.einsum("pkcs,ncsx->npksx", table, spread, precision=HIGH)
    moved = lax.all_to_all(turned, "context", split_axis=2, concat_axis=3, tiled=True)
    return jnp.einsum("pqmb,nqjbx->npjmx", block_table(block_len, 1.0), moved, precision=HIGH)


def inverse_rows(spec, modulus):
    rows = spec.shape[2]
    block_len = spec.shape[3]
    ctx_size = lax.axis_size("context")
    index = jnp.arange(block_len, dtype=jnp.int32)
    freq = 2 * lax.axis_index("context") + jnp.arange(rows, dtype=jnp.int32)
    total = freq[:, None, None] + 2 * ctx_size * index[None, :, None]
    angle = (total * index[None, None, :] % modulus).astype(jnp.float32) * (2.0 * math.pi / modulus)
    cosine = jnp.cos(angle)
    sine = jnp.sin(angle)
    table = jnp.stack([jnp.stack([cosine, -sine]), jnp.stack([sine, cosine])])
    turned = jnp.einsum("pqjmb,nqjmx->npjbx", table, spec, precision=HIGH)
    moved = lax.all_to_all(turned, "context", split_axis=3, concat_axis=2, tiled=True)
    outer = phases(
        jnp.arange(ctx_size, dtype=jnp.int32),
        jnp.arange(2 * ctx_size, dtype=jnp.int32),
        2 * ctx_size,
    )
    real_table = jnp.stack([jnp.cos(outer), -jnp.sin(outer)])
    values = jnp.einsum("qck,nqksx->ncsx", real_table, moved, precision=HIGH) / modulus
    back = lax.all_to_all(values, "context", split_axis=1, concat_axis=2, tiled=True)
    return back.reshape(back.shape[0], back.shape[2], back.shape[3])


def shards(q_in, k_in, v_in, short_filt, long_filt, norm_gain, grad_out):
    block_len = q_in.shape[1]
    channels = q_in.shape[2]
    edge_rows = FILT - 1
    modulus = 2 * lax.axis_size("context") * block_len
    branches = jnp.stack([q_in[0], k_in[0], v_in[0]])
    before = passed_along(branches[:, block_len - edge_rows :], "context", 1)
    inputs = jnp.concatenate([before, branches], 1).astype(jnp.float32)
    shorts = jnp.zeros((3, block_len, channels), jnp.float32)
    for lag in range(FILT):
        shorts = (
            shorts
            + short_filt[:, lag][:, None, :]
            * inputs[:, edge_rows - lag : edge_rows - lag + block_len]
        )
    q_short = shorts[0]
    k_short = shorts[1]
    v_short = shorts[2]
    kv_prod = k_short * v_short
    spectra = forward_rows(jnp.stack([kv_prod, long_filt]), modulus)
    kv_real, kv_imag = (spectra[0, 0], spectra[0, 1])
    filt_real, filt_imag = (spectra[1, 0], spectra[1, 1])
    conv_spec = jnp.stack(
        [kv_real * filt_real - kv_imag * filt_imag, kv_real * filt_imag + kv_imag * filt_real]
    )[None]
    conv = inverse_rows(conv_spec, modulus)[0]
    y_out = q_short * conv
    squares = lax.psum(jnp.sum(y_out * y_out, axis=-1), "tensor")
    rms = jnp.sqrt(squares / D + EPS)[:, None]
    mixed = (y_out / rms * norm_gain).astype(jnp.bfloat16)[None]
    grad_z = grad_out[0].astype(jnp.float32) * norm_gain
    prods = lax.psum(jnp.sum(grad_z * y_out, axis=-1), "tensor")[:, None]
    grad_y = grad_z / rms - y_out * prods / (D * rms**3)
    dconv = grad_y * q_short
    grad_q = grad_y * conv
    grad_spec = forward_rows(dconv[None], modulus)[0]
    grad_real = grad_spec[0]
    grad_imag = grad_spec[1]
    dkv_spec = jnp.stack(
        [
            filt_real * grad_real + filt_imag * grad_imag,
            filt_real * grad_imag - filt_imag * grad_real,
        ]
    )
    dfilt_spec = jnp.stack(
        [kv_real * grad_real + kv_imag * grad_imag, kv_real * grad_imag - kv_imag * grad_real]
    )
    results = inverse_rows(jnp.stack([dkv_spec, dfilt_spec]), modulus)
    dkv = results[0]
    dfilt_local = results[1]
    grads = jnp.stack([grad_q, dkv * v_short, dkv * k_short])
    after = passed_along(grads[:, :edge_rows].astype(jnp.bfloat16), "context", -1).astype(
        jnp.float32
    )
    extended = jnp.concatenate([grads, after], 1)
    grad_inputs = jnp.zeros((3, block_len, channels), jnp.float32)
    for lag in range(FILT):
        grad_inputs = (
            grad_inputs + short_filt[:, lag][:, None, :] * extended[:, lag : lag + block_len]
        )
    short_local = jnp.stack(
        [
            jnp.sum(grads * inputs[:, edge_rows - lag : edge_rows - lag + block_len], axis=1)
            for lag in range(FILT)
        ],
        1,
    )
    scale = 1.0 / math.sqrt(lax.axis_size("dp") * block_len * lax.axis_size("context"))
    grad_long = lax.psum(dfilt_local, "dp") * scale
    grad_short = lax.psum(short_local, ("dp", "context")) * scale
    return (mixed, grad_inputs.astype(jnp.bfloat16)[:, None], grad_long, grad_short)

MESH = pl.DeviceIdType.MESH
F32 = jnp.float32
BF16 = jnp.bfloat16
PAD = 16
ROWS = 32


def split_table(table):
    high = table.astype(jnp.bfloat16)
    low = (table - high.astype(np.float64)).astype(jnp.bfloat16)
    return high, low


def odd_tables(seq):
    freq = 2 * np.arange(seq)[:, None] + 1
    angle = (freq * np.arange(seq)[None, :] % (4 * seq)) * (np.pi / (2 * seq))
    forward = np.concatenate([np.cos(angle), -np.sin(angle)], 0)
    return split_table(forward) + split_table(np.ascontiguousarray(forward.T) / seq)


def halves(values):
    high = values.astype(BF16)
    return high, (values - high.astype(F32)).astype(BF16)


def dot(a, b):
    return jnp.dot(a, b, preferred_element_type=F32)


def dot3(ah, al, bh, bl):
    return dot(ah, bh) + (dot(ah, bl) + dot(al, bh))


def operator_kernel(
    model_width,
    total_rows,
    q_in,
    k_in,
    v_in,
    g_in,
    f_in,
    short_filt,
    gain_in,
    wh_in,
    wl_in,
    vh_in,
    vl_in,
    mixed,
    grad_inputs,
    grad_long,
    grad_short,
    branch,
    filt,
    wh,
    wl,
    vh,
    vl,
    shorts,
    op_h,
    op_l,
    spec_kv,
    spec_f,
    spec_g,
    prod_h,
    prod_l,
    conv,
    y_buf,
    sums,
    stats,
    grads,
    dfilt,
    dfilt_in,
    dfilt_sum,
    short_sum,
    sent,
    in_send,
    in_recv,
    in_local,
    hop_send,
    hop_recv,
    tab_sem,
    st_send,
    st_recv,
    out_send,
    out_recv,
    out_local,
    df_send,
    df_recv,
    gl_send,
    gl_recv,
    gl_local,
    fw_send,
    fw_recv,
    sh_send,
    sh_recv,
    gs_send,
    gs_recv,
    gs_local,
):
    ctx = lax.axis_size("context")
    tens = lax.axis_size("tensor")
    dp = lax.axis_index("dp")
    me = lax.axis_index("context")
    row = lax.axis_index("tensor")
    block = q_in.shape[0]
    seq = block * ctx
    width = branch.shape[2]
    half = width // 2
    taps = short_filt.shape[1]
    other = {"dp": 1 - dp}

    def peer(off):
        return lax.rem(me + off, ctx)

    def source(off):
        return lax.rem(me + ctx - off, ctx)

    def rows_of(p):
        return pl.ds(pl.multiple_of(p * block, block), block)

    def cols_of(p):
        return pl.ds(pl.multiple_of(p * width, width), width)

    def half_cols(p, h):
        return pl.ds(pl.multiple_of(p * width + h * half, half), half)

    def remote(src, dst, send, recv, device):
        copy = pltpu.make_async_remote_copy(
            src_ref=src, dst_ref=dst, send_sem=send, recv_sem=recv, device_id=device, device_id_type=MESH
        )
        copy.start()
        return copy

    def local(src, dst, sem):
        copy = pltpu.make_async_copy(src, dst, sem)
        copy.start()
        return copy

    tables = [
        local(src, dst, tab_sem.at[n])
        for n, (src, dst) in enumerate([(wh_in, wh), (wl_in, wl), (vh_in, vh), (vl_in, vl)])
    ]

    barrier = pltpu.get_barrier_semaphore()
    near = [(a, b) for a in range(tens) for b in range(ctx) if a + b > 0]
    for a, b in near:
        pl.semaphore_signal(
            barrier,
            inc=1,
            device_id={"tensor": lax.rem(row + a, tens), "context": peer(b)},
            device_id_type=MESH,
        )
    pl.semaphore_signal(barrier, inc=1, device_id=other, device_id_type=MESH)
    pl.semaphore_wait(barrier, len(near) + 1)

    f_copies = [
        remote(
            f_in.at[:, half_cols(peer(off), dp)],
            filt.at[dp, rows_of(me), :],
            in_send.at[4, off],
            in_recv.at[4, off],
            {"context": peer(off)},
        )
        for off in range(1, ctx)
    ]
    f_own = local(f_in.at[:, half_cols(me, dp)], filt.at[dp, rows_of(me), :], in_local.at[4])
    land = pl.ds(pl.multiple_of(PAD + me * block, PAD), block)
    arrivals = {}
    for n, ref in ((1, k_in), (2, v_in), (0, q_in), (3, g_in)):
        arrivals[n] = [
            remote(
                ref.at[:, cols_of(peer(off))],
                branch.at[n, land, :],
                in_send.at[n, off],
                in_recv.at[n, off],
                {"context": peer(off)},
            )
            for off in range(1, ctx)
        ]
        arrivals[n].append(local(ref.at[:, cols_of(me)], branch.at[n, land, :], in_local.at[n]))

    def arrived(n):
        for copy in arrivals[n][:-1]:
            copy.wait_recv()
        arrivals[n][-1].wait()

    branch[:, :PAD, :] = jnp.zeros((4, PAD, width), BF16)
    grads[:, seq:, :] = jnp.zeros((3, 8, width), F32)
    short_sum[...] = jnp.zeros_like(short_sum)

    def taps_of(n):
        return [short_filt[n, j : j + 1, cols_of(me)] for j in range(taps)]

    gain = gain_in[:, cols_of(me)]

    def at(i, rows=ROWS):
        return pl.ds(pl.multiple_of(i * rows, rows), rows)

    def short_conv(n, i, weights):
        piece = branch[n, pl.ds(pl.multiple_of(i * ROWS, ROWS), ROWS + PAD), :].astype(F32)
        total = weights[0] * piece[PAD : PAD + ROWS]
        for j in range(1, taps):
            total = total + weights[j] * piece[PAD - j : PAD - j + ROWS]
        return total

    def forward(spec):
        @pl.loop(0, 2 * seq // 256)
        def _(m):
            rows = at(m, 256)
            spec[rows, :] = dot3(wh[rows, :], wl[rows, :], op_h[...], op_l[...])

    def inverse(store):
        @pl.loop(0, seq // 256)
        def _(m):
            rows = at(m, 256)
            store(rows, dot3(vh[rows, :], vl[rows, :], prod_h[...], prod_l[...]))

    def multiply(left, right, sign):
        @pl.loop(0, seq // ROWS)
        def _(i):
            re = at(i)
            im = pl.ds(pl.multiple_of(seq + i * ROWS, ROWS), ROWS)
            a, b = left[re, :], left[im, :] * sign
            c, d = right[re, :], right[im, :]
            prod_h[re, :], prod_l[re, :] = halves(a * c - b * d)
            prod_h[im, :], prod_l[im, :] = halves(a * d + b * c)

    for copy in f_copies:
        copy.wait_recv()
    f_own.wait()
    f_hop = remote(filt.at[dp], filt.at[dp], hop_send, hop_recv, other)

    arrived(1)
    arrived(2)
    k_taps = taps_of(1)
    v_taps = taps_of(2)

    @pl.loop(0, seq // ROWS)
    def _(i):
        ks = short_conv(1, i, k_taps)
        vs = short_conv(2, i, v_taps)
        shorts[1, at(i), :] = ks
        shorts[2, at(i), :] = vs
        op_h[at(i), :], op_l[at(i), :] = halves(ks * vs)

    for copy in tables:
        copy.wait()
    forward(spec_kv)

    f_hop.wait_recv()

    @pl.loop(0, seq // ROWS)
    def _(i):
        op_h[at(i), :half], op_l[at(i), :half] = halves(filt[0, at(i), :])
        op_h[at(i), half:], op_l[at(i), half:] = halves(filt[1, at(i), :])

    forward(spec_f)
    multiply(spec_kv, spec_f, 1.0)

    def store_conv(rows, values):
        conv[rows, :] = values

    inverse(store_conv)

    arrived(0)
    arrived(3)
    q_taps = taps_of(0)

    def folded(values):
        total = values[:, :128]
        for n in range(1, width // 128):
            total = total + values[:, n * 128 : (n + 1) * 128]
        return total

    @pl.loop(0, seq // ROWS)
    def _(i):
        qs = short_conv(0, i, q_taps)
        shorts[0, at(i), :] = qs
        y = qs * conv[at(i), :]
        y_buf[at(i), :] = y
        gz = branch[3, pl.ds(pl.multiple_of(PAD + i * ROWS, PAD), ROWS), :].astype(F32) * gain
        sums[0, at(i), :] = folded(y * y)
        sums[1, at(i), :] = folded(gz * y)

    groups = seq // 128
    lane = lax.broadcasted_iota(jnp.int32, (128, 128), 1)
    columns = jnp.zeros((128, 128), F32)
    for n in range(2):
        for b in range(groups):
            part = jnp.sum(sums[n, b * 128 : (b + 1) * 128, :], axis=1, keepdims=True)
            columns = jnp.where(lane == n * groups + b, part, columns)
    stats[0] = columns.T[: 2 * groups]
    st_copies = [
        remote(
            stats.at[0],
            stats.at[a * ctx + b],
            st_send.at[a * ctx + b],
            st_recv.at[a * ctx + b],
            {"tensor": lax.rem(row + a, tens), "context": peer(b)},
        )
        for a, b in near
    ]
    for copy in st_copies:
        copy.wait_recv()
    total = stats[0]
    for n in range(1, tens * ctx):
        total = total + stats[n]
    inv = 1.0 / jnp.sqrt(total[:groups] / model_width + EPS)
    coef = total[groups:] * (inv * inv * inv / model_width)
    spread = jnp.concatenate([inv, coef, jnp.zeros((128 - 2 * groups, 128), F32)], 0).T

    for b in range(groups):
        sums[0, b * 128 : (b + 1) * 128, :] = jnp.broadcast_to(spread[:, b : b + 1], (128, 128))
        sums[1, b * 128 : (b + 1) * 128, :] = jnp.broadcast_to(
            spread[:, groups + b : groups + b + 1], (128, 128)
        )

    def wide(n, i):
        return jnp.concatenate([sums[n, at(i), :]] * (width // 128), 1)

    @pl.loop(0, seq // ROWS)
    def _(i):
        sent[3, at(i), :] = (y_buf[at(i), :] * wide(0, i) * gain).astype(BF16)

    def send_back(n, target):
        copies = [
            remote(
                sent.at[n, rows_of(peer(off)), :],
                target,
                out_send.at[n, off],
                out_recv.at[n, off],
                {"context": peer(off)},
            )
            for off in range(1, ctx)
        ]
        return copies, local(sent.at[n, rows_of(me), :], target, out_local.at[n])

    back = [send_back(3, mixed.at[0, :, cols_of(me)])]

    @pl.loop(0, seq // ROWS)
    def _(i):
        gz = branch[3, pl.ds(pl.multiple_of(PAD + i * ROWS, PAD), ROWS), :].astype(F32) * gain
        dy = gz * wide(0, i) - y_buf[at(i), :] * wide(1, i)
        op_h[at(i), :], op_l[at(i), :] = halves(dy * shorts[0, at(i), :])
        grads[0, at(i), :] = dy * conv[at(i), :]

    scale = 1.0 / math.sqrt(total_rows)

    def back_short(n):
        weights = taps_of(n)

        def body(i, acc):
            piece = grads[n, pl.ds(pl.multiple_of(i * ROWS, ROWS), ROWS + 8), :]
            total = weights[0] * piece[:ROWS]
            for j in range(1, taps):
                total = total + weights[j] * piece[j : j + ROWS]
            sent[n, at(i), :] = total.astype(BF16)
            inputs = branch[n, pl.ds(pl.multiple_of(i * ROWS, ROWS), ROWS + PAD), :].astype(F32)
            own = piece[:ROWS]
            out = []
            for j in range(taps):
                prod = own * inputs[PAD - j : PAD - j + ROWS]
                part = acc[j]
                for r in range(ROWS // 8):
                    part = part + prod[r * 8 : (r + 1) * 8]
                out.append(part)
            return tuple(out)

        acc = lax.fori_loop(0, seq // ROWS, body, tuple(jnp.zeros((8, width), F32) for _ in range(taps)))
        back.append(send_back(n, grad_inputs.at[n, 0, :, cols_of(me)]))
        for j in range(taps):
            short_sum[0, n, j : j + 1, :] = jnp.sum(acc[j], axis=0, keepdims=True) * scale

    back_short(0)

    forward(spec_g)
    multiply(spec_kv, spec_g, -1.0)

    def store_dfilt(rows, values):
        dfilt[0, rows, :] = values[:, :half] * scale
        dfilt[1, rows, :] = values[:, half:] * scale

    inverse(store_dfilt)
    df_copy = remote(dfilt.at[1 - dp], dfilt_in, df_send, df_recv, other)

    multiply(spec_f, spec_g, -1.0)

    def store_dkv(rows, values):
        grads[1, rows, :] = values * shorts[2, rows, :]
        grads[2, rows, :] = values * shorts[1, rows, :]

    inverse(store_dkv)

    df_copy.wait_recv()
    dfilt_sum[...] = dfilt[dp] + dfilt_in[...]
    gl_target = grad_long.at[:, half_cols(me, dp)]
    gl_copies = [
        remote(
            dfilt_sum.at[rows_of(peer(off)), :],
            gl_target,
            gl_send.at[off],
            gl_recv.at[off],
            {"context": peer(off)},
        )
        for off in range(1, ctx)
    ]
    gl_own = local(dfilt_sum.at[rows_of(me), :], gl_target, gl_local)
    forwards = [remote(dfilt_sum.at[rows_of(me), :], gl_target, fw_send.at[0], fw_recv.at[0], other)]

    back_short(1)
    back_short(2)

    sh_copy = remote(short_sum.at[0], short_sum.at[1], sh_send, sh_recv, other)
    for off in range(1, ctx):
        gl_copies[off - 1].wait_recv()
        piece = grad_long.at[:, half_cols(source(off), dp)]
        forwards.append(remote(piece, piece, fw_send.at[off], fw_recv.at[off], other))
    sh_copy.wait_recv()
    short_sum[2] = short_sum[0] + short_sum[1]
    gs_target = grad_short.at[:, :, cols_of(me)]
    gs_copies = [
        remote(short_sum.at[2], gs_target, gs_send.at[off], gs_recv.at[off], {"context": peer(off)})
        for off in range(1, ctx)
    ]
    gs_own = local(short_sum.at[2], gs_target, gs_local)

    for copies, own in back:
        own.wait()
        for copy in copies:
            copy.wait()
    gl_own.wait()
    for copy in gl_copies:
        copy.wait_send()
    for copy in forwards:
        copy.wait()
    gs_own.wait()
    for copy in gs_copies:
        copy.wait()
    sh_copy.wait_send()
    df_copy.wait_send()
    f_hop.wait_send()
    for copy in f_copies + st_copies:
        copy.wait_send()
    for n in range(4):
        for copy in arrivals[n][:-1]:
            copy.wait_send()


def fused(q_in, k_in, v_in, short_filt, long_filt, norm_gain, grad_out):
    _, block, channels = q_in.shape
    ctx = lax.axis_size("context")
    tens = lax.axis_size("tensor")
    seq = block * ctx
    width = channels // ctx
    tables = [jnp.asarray(t) for t in odd_tables(seq)]
    dma = pltpu.SemaphoreType.DMA
    anywhere = pl.BlockSpec(memory_space=pl.ANY)
    in_vmem = pl.BlockSpec(memory_space=pltpu.VMEM)
    outs = pl.pallas_call(
        functools.partial(operator_kernel, D, lax.axis_size("dp") * seq),
        out_shape=(
            jax.ShapeDtypeStruct((1, block, channels), BF16),
            jax.ShapeDtypeStruct((3, 1, block, channels), BF16),
            jax.ShapeDtypeStruct((block, channels), F32),
            jax.ShapeDtypeStruct((3, 8, channels), F32),
        ),
        in_specs=[anywhere] * 5 + [in_vmem] * 2 + [anywhere] * 4,
        out_specs=(anywhere,) * 4,
        scratch_shapes=[
            pltpu.VMEM((4, PAD + seq, width), BF16),
            pltpu.VMEM((2, seq, width // 2), F32),
            pltpu.VMEM((2 * seq, seq), BF16),
            pltpu.VMEM((2 * seq, seq), BF16),
            pltpu.VMEM((seq, 2 * seq), BF16),
            pltpu.VMEM((seq, 2 * seq), BF16),
            pltpu.VMEM((3, seq, width), F32),
            pltpu.VMEM((seq, width), BF16),
            pltpu.VMEM((seq, width), BF16),
            pltpu.VMEM((2 * seq, width), F32),
            pltpu.VMEM((2 * seq, width), F32),
            pltpu.VMEM((2 * seq, width), F32),
            pltpu.VMEM((2 * seq, width), BF16),
            pltpu.VMEM((2 * seq, width), BF16),
            pltpu.VMEM((seq, width), F32),
            pltpu.VMEM((seq, width), F32),
            pltpu.VMEM((2, seq, 128), F32),
            pltpu.VMEM((tens * ctx, 2 * seq // 128, 128), F32),
            pltpu.VMEM((3, seq + 8, width), F32),
            pltpu.VMEM((2, seq, width // 2), F32),
            pltpu.VMEM((seq, width // 2), F32),
            pltpu.VMEM((seq, width // 2), F32),
            pltpu.VMEM((3, 3, 8, width), F32),
            pltpu.VMEM((4, seq, width), BF16),
            dma((5, ctx)),
            dma((5, ctx)),
            dma((5,)),
            dma,
            dma,
            dma((4,)),
            dma((tens * ctx,)),
            dma((tens * ctx,)),
            dma((4, ctx)),
            dma((4, ctx)),
            dma((4,)),
            dma,
            dma,
            dma((ctx,)),
            dma((ctx,)),
            dma,
            dma((ctx,)),
            dma((ctx,)),
            dma,
            dma,
            dma((ctx,)),
            dma((ctx,)),
            dma,
        ],
        compiler_params=pltpu.CompilerParams(
            collective_id=0, has_side_effects=True, vmem_limit_bytes=48 * 2**20
        ),
    )(
        q_in[0],
        k_in[0],
        v_in[0],
        grad_out[0],
        long_filt,
        short_filt,
        norm_gain[None],
        *tables,
    )
    mixed, grad_inputs, grad_long, short = outs
    return mixed, grad_inputs, grad_long, short[:, : short_filt.shape[1]]


def operator(q_in, k_in, v_in, short_filt, long_filt, norm_gain, grad_out):
    _, block, channels = q_in.shape
    ctx = lax.axis_size("context")
    dense = block * ctx <= 1024 and block % 128 == 0 and channels % (256 * ctx) == 0
    form = fused if dense and lax.axis_size("dp") == 2 else shards
    return form(q_in, k_in, v_in, short_filt, long_filt, norm_gain, grad_out)


def solution(mesh):
    in_specs = (
        P("dp", "context", "tensor"),
        P("dp", "context", "tensor"),
        P("dp", "context", "tensor"),
        P(None, None, "tensor"),
        P("context", "tensor"),
        P("tensor"),
        P("dp", "context", "tensor"),
    )
    out_specs = (
        P("dp", "context", "tensor"),
        P(None, "dp", "context", "tensor"),
        P("context", "tensor"),
        P(None, None, "tensor"),
    )
    return jax.shard_map(operator, mesh=mesh, in_specs=in_specs, out_specs=out_specs, check_vma=False)
```

```python
import functools
import math

import jax
import jax.numpy as jnp
import numpy as np
from jax import lax
from jax.experimental import pallas as pl
from jax.experimental.pallas import tpu as pltpu
from jax.sharding import PartitionSpec as P

D = 4096
FILT = 7


EPS = 1e-06
HIGH = lax.Precision.HIGHEST


def passed_along(shard, axis, by):
    peers = lax.axis_size(axis)
    pairs = [(i, i + by) for i in range(peers) if 0 <= i + by < peers]
    return lax.ppermute(shard, axis, pairs)


def phases(first, second, modulus):
    product = first[:, None] * second[None, :] % modulus
    return product.astype(jnp.float32) * (2.0 * math.pi / modulus)


def block_table(block_len, sign):
    index = jnp.arange(block_len, dtype=jnp.int32)
    angle = phases(index, index, block_len)
    cosine = jnp.cos(angle)
    sine = jnp.sin(angle) * sign
    return jnp.stack([jnp.stack([cosine, sine]), jnp.stack([-sine, cosine])])


def forward_rows(values, modulus):
    count, block_len, width = values.shape
    ctx_size = lax.axis_size("context")
    sub_len = block_len // ctx_size
    spread = lax.all_to_all(
        values.reshape(count, 1, block_len, width),
        "context",
        split_axis=2,
        concat_axis=1,
        tiled=True,
    )
    freq = jnp.arange(2 * ctx_size, dtype=jnp.int32)
    place = (
        jnp.arange(ctx_size, dtype=jnp.int32)[:, None] * block_len
        + lax.axis_index("context") * sub_len
        + jnp.arange(sub_len, dtype=jnp.int32)[None, :]
    )
    angle = (freq[:, None, None] * place[None] % modulus).astype(jnp.float32) * (
        2.0 * math.pi / modulus
    )
    table = jnp.stack([jnp.cos(angle), -jnp.sin(angle)])
    turned = jnp.einsum("pkcs,ncsx->npksx", table, spread, precision=HIGH)
    moved = lax.all_to_all(turned, "context", split_axis=2, concat_axis=3, tiled=True)
    return jnp.einsum("pqmb,nqjbx->npjmx", block_table(block_len, 1.0), moved, precision=HIGH)


def inverse_rows(spec, modulus):
    rows = spec.shape[2]
    block_len = spec.shape[3]
    ctx_size = lax.axis_size("context")
    index = jnp.arange(block_len, dtype=jnp.int32)
    freq = 2 * lax.axis_index("context") + jnp.arange(rows, dtype=jnp.int32)
    total = freq[:, None, None] + 2 * ctx_size * index[None, :, None]
    angle = (total * index[None, None, :] % modulus).astype(jnp.float32) * (2.0 * math.pi / modulus)
    cosine = jnp.cos(angle)
    sine = jnp.sin(angle)
    table = jnp.stack([jnp.stack([cosine, -sine]), jnp.stack([sine, cosine])])
    turned = jnp.einsum("pqjmb,nqjmx->npjbx", table, spec, precision=HIGH)
    moved = lax.all_to_all(turned, "context", split_axis=3, concat_axis=2, tiled=True)
    outer = phases(
        jnp.arange(ctx_size, dtype=jnp.int32),
        jnp.arange(2 * ctx_size, dtype=jnp.int32),
        2 * ctx_size,
    )
    real_table = jnp.stack([jnp.cos(outer), -jnp.sin(outer)])
    values = jnp.einsum("qck,nqksx->ncsx", real_table, moved, precision=HIGH) / modulus
    back = lax.all_to_all(values, "context", split_axis=1, concat_axis=2, tiled=True)
    return back.reshape(back.shape[0], back.shape[2], back.shape[3])


def shards(q_in, k_in, v_in, short_filt, long_filt, norm_gain, grad_out):
    block_len = q_in.shape[1]
    channels = q_in.shape[2]
    edge_rows = FILT - 1
    modulus = 2 * lax.axis_size("context") * block_len
    branches = jnp.stack([q_in[0], k_in[0], v_in[0]])
    before = passed_along(branches[:, block_len - edge_rows :], "context", 1)
    inputs = jnp.concatenate([before, branches], 1).astype(jnp.float32)
    shorts = jnp.zeros((3, block_len, channels), jnp.float32)
    for lag in range(FILT):
        shorts = (
            shorts
            + short_filt[:, lag][:, None, :]
            * inputs[:, edge_rows - lag : edge_rows - lag + block_len]
        )
    q_short = shorts[0]
    k_short = shorts[1]
    v_short = shorts[2]
    kv_prod = k_short * v_short
    spectra = forward_rows(jnp.stack([kv_prod, long_filt]), modulus)
    kv_real, kv_imag = (spectra[0, 0], spectra[0, 1])
    filt_real, filt_imag = (spectra[1, 0], spectra[1, 1])
    conv_spec = jnp.stack(
        [kv_real * filt_real - kv_imag * filt_imag, kv_real * filt_imag + kv_imag * filt_real]
    )[None]
    conv = inverse_rows(conv_spec, modulus)[0]
    y_out = q_short * conv
    squares = lax.psum(jnp.sum(y_out * y_out, axis=-1), "tensor")
    rms = jnp.sqrt(squares / D + EPS)[:, None]
    mixed = (y_out / rms * norm_gain).astype(jnp.bfloat16)[None]
    grad_z = grad_out[0].astype(jnp.float32) * norm_gain
    prods = lax.psum(jnp.sum(grad_z * y_out, axis=-1), "tensor")[:, None]
    grad_y = grad_z / rms - y_out * prods / (D * rms**3)
    dconv = grad_y * q_short
    grad_q = grad_y * conv
    grad_spec = forward_rows(dconv[None], modulus)[0]
    grad_real = grad_spec[0]
    grad_imag = grad_spec[1]
    dkv_spec = jnp.stack(
        [
            filt_real * grad_real + filt_imag * grad_imag,
            filt_real * grad_imag - filt_imag * grad_real,
        ]
    )
    dfilt_spec = jnp.stack(
        [kv_real * grad_real + kv_imag * grad_imag, kv_real * grad_imag - kv_imag * grad_real]
    )
    results = inverse_rows(jnp.stack([dkv_spec, dfilt_spec]), modulus)
    dkv = results[0]
    dfilt_local = results[1]
    grads = jnp.stack([grad_q, dkv * v_short, dkv * k_short])
    after = passed_along(grads[:, :edge_rows].astype(jnp.bfloat16), "context", -1).astype(
        jnp.float32
    )
    extended = jnp.concatenate([grads, after], 1)
    grad_inputs = jnp.zeros((3, block_len, channels), jnp.float32)
    for lag in range(FILT):
        grad_inputs = (
            grad_inputs + short_filt[:, lag][:, None, :] * extended[:, lag : lag + block_len]
        )
    short_local = jnp.stack(
        [
            jnp.sum(grads * inputs[:, edge_rows - lag : edge_rows - lag + block_len], axis=1)
            for lag in range(FILT)
        ],
        1,
    )
    scale = 1.0 / math.sqrt(lax.axis_size("dp") * block_len * lax.axis_size("context"))
    grad_long = lax.psum(dfilt_local, "dp") * scale
    grad_short = lax.psum(short_local, ("dp", "context")) * scale
    return (mixed, grad_inputs.astype(jnp.bfloat16)[:, None], grad_long, grad_short)

MESH = pl.DeviceIdType.MESH
F32 = jnp.float32
BF16 = jnp.bfloat16
PAD = 16
ROWS = 32


def split_table(table):
    high = table.astype(jnp.bfloat16)
    low = (table - high.astype(np.float64)).astype(jnp.bfloat16)
    return high, low


def odd_tables(seq):
    freq = 2 * np.arange(seq)[:, None] + 1
    angle = (freq * np.arange(seq)[None, :] % (4 * seq)) * (np.pi / (2 * seq))
    forward = np.concatenate([np.cos(angle), -np.sin(angle)], 0)
    return split_table(forward) + split_table(np.ascontiguousarray(forward.T) / seq)


def halves(values):
    high = values.astype(BF16)
    return high, (values - high.astype(F32)).astype(BF16)


def dot(a, b):
    return jnp.dot(a, b, preferred_element_type=F32)


def dot3(ah, al, bh, bl):
    return dot(ah, bh) + (dot(ah, bl) + dot(al, bh))


def operator_kernel(
    model_width,
    total_rows,
    q_in,
    k_in,
    v_in,
    g_in,
    f_in,
    short_in,
    gains_in,
    wh_in,
    wl_in,
    vh_in,
    vl_in,
    mixed,
    grad_inputs,
    grad_long,
    grad_short,
    branch,
    filt,
    wh,
    wl,
    vh,
    vl,
    short_filt,
    gain_in,
    shorts,
    op_h,
    op_l,
    spec_kv,
    spec_f,
    spec_g,
    prod_h,
    prod_l,
    conv,
    y_buf,
    sums,
    stats,
    grads,
    dfilt,
    dfilt_in,
    dfilt_sum,
    short_sum,
    sent,
    in_send,
    in_recv,
    in_local,
    hop_send,
    hop_recv,
    tab_sem,
    st_send,
    st_recv,
    out_send,
    out_recv,
    out_local,
    df_send,
    df_recv,
    gl_send,
    gl_recv,
    gl_local,
    fw_send,
    fw_recv,
    sh_send,
    sh_recv,
    gs_send,
    gs_recv,
    gs_local,
):
    ctx = lax.axis_size("context")
    tens = lax.axis_size("tensor")
    dp = lax.axis_index("dp")
    me = lax.axis_index("context")
    row = lax.axis_index("tensor")
    block = q_in.shape[0]
    seq = block * ctx
    width = branch.shape[2]
    half = width // 2
    taps = short_filt.shape[1]
    other = {"dp": 1 - dp}

    def peer(off):
        return lax.rem(me + off, ctx)

    def source(off):
        return lax.rem(me + ctx - off, ctx)

    def rows_of(p):
        return pl.ds(pl.multiple_of(p * block, block), block)

    def cols_of(p):
        return pl.ds(pl.multiple_of(p * width, width), width)

    def half_cols(p, h):
        return pl.ds(pl.multiple_of(p * width + h * half, half), half)

    def remote(src, dst, send, recv, device):
        copy = pltpu.make_async_remote_copy(
            src_ref=src, dst_ref=dst, send_sem=send, recv_sem=recv, device_id=device, device_id_type=MESH
        )
        copy.start()
        return copy

    def local(src, dst, sem):
        copy = pltpu.make_async_copy(src, dst, sem)
        copy.start()
        return copy

    barrier = pltpu.get_barrier_semaphore()
    near = [(a, b) for a in range(tens) for b in range(ctx) if a + b > 0]
    for a, b in near:
        pl.semaphore_signal(
            barrier,
            inc=1,
            device_id={"tensor": lax.rem(row + a, tens), "context": peer(b)},
            device_id_type=MESH,
        )
    pl.semaphore_signal(barrier, inc=1, device_id=other, device_id_type=MESH)
    pl.semaphore_wait(barrier, len(near) + 1)

    f_copies = [
        remote(
            f_in.at[:, half_cols(peer(off), dp)],
            filt.at[dp, rows_of(me), :],
            in_send.at[4, off],
            in_recv.at[4, off],
            {"context": peer(off)},
        )
        for off in range(1, ctx)
    ]
    f_own = local(f_in.at[:, half_cols(me, dp)], filt.at[dp, rows_of(me), :], in_local.at[4])
    land = pl.ds(pl.multiple_of(PAD + me * block, PAD), block)
    arrivals = {}
    for n, ref in ((1, k_in), (2, v_in), (0, q_in), (3, g_in)):
        arrivals[n] = [
            remote(
                ref.at[:, cols_of(peer(off))],
                branch.at[n, land, :],
                in_send.at[n, off],
                in_recv.at[n, off],
                {"context": peer(off)},
            )
            for off in range(1, ctx)
        ]
        arrivals[n].append(local(ref.at[:, cols_of(me)], branch.at[n, land, :], in_local.at[n]))

    small = [local(short_in, short_filt, tab_sem.at[4]), local(gains_in, gain_in, tab_sem.at[5])]
    tables = [
        local(src, dst, tab_sem.at[n])
        for n, (src, dst) in enumerate([(wh_in, wh), (wl_in, wl), (vh_in, vh), (vl_in, vl)])
    ]

    def arrived(n):
        for copy in arrivals[n][:-1]:
            copy.wait_recv()
        arrivals[n][-1].wait()

    branch[:, :PAD, :] = jnp.zeros((4, PAD, width), BF16)
    grads[:, seq:, :] = jnp.zeros((3, 8, width), F32)
    short_sum[...] = jnp.zeros_like(short_sum)

    for copy in small:
        copy.wait()

    def taps_of(n):
        return [short_filt[n, j : j + 1, cols_of(me)] for j in range(taps)]

    gain = gain_in[:, cols_of(me)]

    def at(i, rows=ROWS):
        return pl.ds(pl.multiple_of(i * rows, rows), rows)

    def short_conv(n, i, weights):
        piece = branch[n, pl.ds(pl.multiple_of(i * ROWS, ROWS), ROWS + PAD), :].astype(F32)
        total = weights[0] * piece[PAD : PAD + ROWS]
        for j in range(1, taps):
            total = total + weights[j] * piece[PAD - j : PAD - j + ROWS]
        return total

    def forward(spec):
        @pl.loop(0, 2 * seq // 256)
        def _(m):
            rows = at(m, 256)
            spec[rows, :] = dot3(wh[rows, :], wl[rows, :], op_h[...], op_l[...])

    def inverse(store):
        @pl.loop(0, seq // 256)
        def _(m):
            rows = at(m, 256)
            store(rows, dot3(vh[rows, :], vl[rows, :], prod_h[...], prod_l[...]))

    def multiply(left, right, sign):
        @pl.loop(0, seq // ROWS)
        def _(i):
            re = at(i)
            im = pl.ds(pl.multiple_of(seq + i * ROWS, ROWS), ROWS)
            a, b = left[re, :], left[im, :] * sign
            c, d = right[re, :], right[im, :]
            prod_h[re, :], prod_l[re, :] = halves(a * c - b * d)
            prod_h[im, :], prod_l[im, :] = halves(a * d + b * c)

    for copy in f_copies:
        copy.wait_recv()
    f_own.wait()
    f_hop = remote(filt.at[dp], filt.at[dp], hop_send, hop_recv, other)

    arrived(1)
    k_taps = taps_of(1)

    @pl.loop(0, seq // ROWS)
    def _(i):
        shorts[1, at(i), :] = short_conv(1, i, k_taps)

    for copy in tables:
        copy.wait()
    f_hop.wait_recv()

    @pl.loop(0, seq // ROWS)
    def _(i):
        op_h[at(i), :half], op_l[at(i), :half] = halves(filt[0, at(i), :])
        op_h[at(i), half:], op_l[at(i), half:] = halves(filt[1, at(i), :])

    forward(spec_f)

    arrived(2)
    v_taps = taps_of(2)

    @pl.loop(0, seq // ROWS)
    def _(i):
        vs = short_conv(2, i, v_taps)
        shorts[2, at(i), :] = vs
        op_h[at(i), :], op_l[at(i), :] = halves(shorts[1, at(i), :] * vs)

    forward(spec_kv)
    multiply(spec_kv, spec_f, 1.0)

    def store_conv(rows, values):
        conv[rows, :] = values

    inverse(store_conv)

    arrived(0)
    q_taps = taps_of(0)

    def folded(values):
        total = values[:, :128]
        for n in range(1, width // 128):
            total = total + values[:, n * 128 : (n + 1) * 128]
        return total

    @pl.loop(0, seq // ROWS)
    def _(i):
        qs = short_conv(0, i, q_taps)
        shorts[0, at(i), :] = qs
        y = qs * conv[at(i), :]
        y_buf[at(i), :] = y
        sums[0, at(i), :] = folded(y * y)

    groups = seq // 128
    lane = lax.broadcasted_iota(jnp.int32, (128, 128), 1)

    def share(n):
        columns = jnp.zeros((128, 128), F32)
        for b in range(groups):
            part = jnp.sum(sums[n, b * 128 : (b + 1) * 128, :], axis=1, keepdims=True)
            columns = jnp.where(lane == b, part, columns)
        stats[n, 0] = columns.T[:8]
        return [
            remote(
                stats.at[n, 0],
                stats.at[n, a * ctx + b],
                st_send.at[n, a * ctx + b],
                st_recv.at[n, a * ctx + b],
                {"tensor": lax.rem(row + a, tens), "context": peer(b)},
            )
            for a, b in near
        ]

    def gathered(n, copies):
        for copy in copies:
            copy.wait_recv()
        total = stats[n, 0]
        for r in range(1, tens * ctx):
            total = total + stats[n, r]
        return total

    def widen(n, values):
        spread = jnp.concatenate([values, jnp.zeros((120, 128), F32)], 0).T
        for b in range(groups):
            sums[n, b * 128 : (b + 1) * 128, :] = jnp.broadcast_to(spread[:, b : b + 1], (128, 128))

    st_copies = share(0)
    arrived(3)

    @pl.loop(0, seq // ROWS)
    def _(i):
        gz = branch[3, pl.ds(pl.multiple_of(PAD + i * ROWS, PAD), ROWS), :].astype(F32) * gain
        sums[1, at(i), :] = folded(gz * y_buf[at(i), :])

    prod_copies = share(1)
    inv = 1.0 / jnp.sqrt(gathered(0, st_copies) / model_width + EPS)
    widen(0, inv)

    def wide(n, i):
        return jnp.concatenate([sums[n, at(i), :]] * (width // 128), 1)

    @pl.loop(0, seq // ROWS)
    def _(i):
        sent[3, at(i), :] = (y_buf[at(i), :] * wide(0, i) * gain).astype(BF16)

    def send_back(n, target):
        copies = [
            remote(
                sent.at[n, rows_of(peer(off)), :],
                target,
                out_send.at[n, off],
                out_recv.at[n, off],
                {"context": peer(off)},
            )
            for off in range(1, ctx)
        ]
        return copies, local(sent.at[n, rows_of(me), :], target, out_local.at[n])

    back = [send_back(3, mixed.at[0, :, cols_of(me)])]
    widen(1, gathered(1, prod_copies) * (inv * inv * inv / model_width))

    @pl.loop(0, seq // ROWS)
    def _(i):
        gz = branch[3, pl.ds(pl.multiple_of(PAD + i * ROWS, PAD), ROWS), :].astype(F32) * gain
        dy = gz * wide(0, i) - y_buf[at(i), :] * wide(1, i)
        op_h[at(i), :], op_l[at(i), :] = halves(dy * shorts[0, at(i), :])
        grads[0, at(i), :] = dy * conv[at(i), :]

    scale = 1.0 / math.sqrt(total_rows)

    def back_short(n):
        weights = taps_of(n)

        @pl.loop(0, seq // ROWS)
        def _(i):
            piece = grads[n, pl.ds(pl.multiple_of(i * ROWS, ROWS), ROWS + 8), :]
            total = weights[0] * piece[:ROWS]
            for j in range(1, taps):
                total = total + weights[j] * piece[j : j + ROWS]
            sent[n, at(i), :] = total.astype(BF16)

        back.append(send_back(n, grad_inputs.at[n, 0, :, cols_of(me)]))

    def short_grads(n):
        def body(i, acc):
            own = grads[n, at(i), :]
            inputs = branch[n, pl.ds(pl.multiple_of(i * ROWS, ROWS), ROWS + PAD), :].astype(F32)
            out = []
            for j in range(taps):
                prod = own * inputs[PAD - j : PAD - j + ROWS]
                part = acc[j]
                for r in range(ROWS // 8):
                    part = part + prod[r * 8 : (r + 1) * 8]
                out.append(part)
            return tuple(out)

        acc = lax.fori_loop(0, seq // ROWS, body, tuple(jnp.zeros((8, width), F32) for _ in range(taps)))
        for j in range(taps):
            short_sum[0, n, j : j + 1, :] = jnp.sum(acc[j], axis=0, keepdims=True) * scale

    back_short(0)

    forward(spec_g)
    multiply(spec_f, spec_g, -1.0)

    def store_dkv(rows, values):
        grads[1, rows, :] = values * shorts[2, rows, :]
        grads[2, rows, :] = values * shorts[1, rows, :]

    inverse(store_dkv)
    back_short(1)
    back_short(2)

    multiply(spec_kv, spec_g, -1.0)

    def store_dfilt(rows, values):
        dfilt[0, rows, :] = values[:, :half] * scale
        dfilt[1, rows, :] = values[:, half:] * scale

    inverse(store_dfilt)
    df_copy = remote(dfilt.at[1 - dp], dfilt_in, df_send, df_recv, other)

    for n in range(3):
        short_grads(n)
    sh_copy = remote(short_sum.at[0], short_sum.at[1], sh_send, sh_recv, other)

    df_copy.wait_recv()
    dfilt_sum[...] = dfilt[dp] + dfilt_in[...]
    gl_target = grad_long.at[:, half_cols(me, dp)]
    gl_copies = [
        remote(
            dfilt_sum.at[rows_of(peer(off)), :],
            gl_target,
            gl_send.at[off],
            gl_recv.at[off],
            {"context": peer(off)},
        )
        for off in range(1, ctx)
    ]
    gl_own = local(dfilt_sum.at[rows_of(me), :], gl_target, gl_local)
    forwards = [remote(dfilt_sum.at[rows_of(me), :], gl_target, fw_send.at[0], fw_recv.at[0], other)]

    sh_copy.wait_recv()
    short_sum[2] = short_sum[0] + short_sum[1]
    gs_target = grad_short.at[:, :, cols_of(me)]
    gs_copies = [
        remote(short_sum.at[2], gs_target, gs_send.at[off], gs_recv.at[off], {"context": peer(off)})
        for off in range(1, ctx)
    ]
    gs_own = local(short_sum.at[2], gs_target, gs_local)
    for off in range(1, ctx):
        gl_copies[off - 1].wait_recv()
        piece = grad_long.at[:, half_cols(source(off), dp)]
        forwards.append(remote(piece, piece, fw_send.at[off], fw_recv.at[off], other))

    for copies, own in back:
        own.wait()
        for copy in copies:
            copy.wait()
    gl_own.wait()
    for copy in gl_copies:
        copy.wait_send()
    for copy in forwards:
        copy.wait()
    gs_own.wait()
    for copy in gs_copies:
        copy.wait()
    sh_copy.wait_send()
    df_copy.wait_send()
    f_hop.wait_send()
    for copy in f_copies + st_copies + prod_copies:
        copy.wait_send()
    for n in range(4):
        for copy in arrivals[n][:-1]:
            copy.wait_send()


def fused(q_in, k_in, v_in, short_filt, long_filt, norm_gain, grad_out):
    _, block, channels = q_in.shape
    ctx = lax.axis_size("context")
    tens = lax.axis_size("tensor")
    seq = block * ctx
    width = channels // ctx
    tables = [jnp.asarray(t) for t in odd_tables(seq)]
    dma = pltpu.SemaphoreType.DMA
    anywhere = pl.BlockSpec(memory_space=pl.ANY)
    in_hbm = pl.BlockSpec(memory_space=pltpu.HBM)
    outs = pl.pallas_call(
        functools.partial(operator_kernel, D, lax.axis_size("dp") * seq),
        out_shape=(
            jax.ShapeDtypeStruct((1, block, channels), BF16),
            jax.ShapeDtypeStruct((3, 1, block, channels), BF16),
            jax.ShapeDtypeStruct((block, channels), F32),
            jax.ShapeDtypeStruct((3, 8, channels), F32),
        ),
        in_specs=[in_hbm] * 11,
        out_specs=(anywhere,) * 4,
        scratch_shapes=[
            pltpu.VMEM((4, PAD + seq, width), BF16),
            pltpu.VMEM((2, seq, width // 2), F32),
            pltpu.VMEM((2 * seq, seq), BF16),
            pltpu.VMEM((2 * seq, seq), BF16),
            pltpu.VMEM((seq, 2 * seq), BF16),
            pltpu.VMEM((seq, 2 * seq), BF16),
            pltpu.VMEM(short_filt.shape, F32),
            pltpu.VMEM((1, channels), F32),
            pltpu.VMEM((3, seq, width), F32),
            pltpu.VMEM((seq, width), BF16),
            pltpu.VMEM((seq, width), BF16),
            pltpu.VMEM((2 * seq, width), F32),
            pltpu.VMEM((2 * seq, width), F32),
            pltpu.VMEM((2 * seq, width), F32),
            pltpu.VMEM((2 * seq, width), BF16),
            pltpu.VMEM((2 * seq, width), BF16),
            pltpu.VMEM((seq, width), F32),
            pltpu.VMEM((seq, width), F32),
            pltpu.VMEM((2, seq, 128), F32),
            pltpu.VMEM((2, tens * ctx, 8, 128), F32),
            pltpu.VMEM((3, seq + 8, width), F32),
            pltpu.VMEM((2, seq, width // 2), F32),
            pltpu.VMEM((seq, width // 2), F32),
            pltpu.VMEM((seq, width // 2), F32),
            pltpu.VMEM((3, 3, 8, width), F32),
            pltpu.VMEM((4, seq, width), BF16),
            dma((5, ctx)),
            dma((5, ctx)),
            dma((5,)),
            dma,
            dma,
            dma((6,)),
            dma((2, tens * ctx)),
            dma((2, tens * ctx)),
            dma((4, ctx)),
            dma((4, ctx)),
            dma((4,)),
            dma,
            dma,
            dma((ctx,)),
            dma((ctx,)),
            dma,
            dma((ctx,)),
            dma((ctx,)),
            dma,
            dma,
            dma((ctx,)),
            dma((ctx,)),
            dma,
        ],
        compiler_params=pltpu.CompilerParams(
            collective_id=0, has_side_effects=True, vmem_limit_bytes=60 * 2**20
        ),
    )(
        q_in[0],
        k_in[0],
        v_in[0],
        grad_out[0],
        long_filt,
        short_filt,
        norm_gain[None],
        *tables,
    )
    mixed, grad_inputs, grad_long, short = outs
    return mixed, grad_inputs, grad_long, short[:, : short_filt.shape[1]]


def operator(q_in, k_in, v_in, short_filt, long_filt, norm_gain, grad_out):
    _, block, channels = q_in.shape
    ctx = lax.axis_size("context")
    dense = block * ctx <= 1024 and block % 128 == 0 and channels % (256 * ctx) == 0
    form = fused if dense and lax.axis_size("dp") == 2 else shards
    return form(q_in, k_in, v_in, short_filt, long_filt, norm_gain, grad_out)


def solution(mesh):
    in_specs = (
        P("dp", "context", "tensor"),
        P("dp", "context", "tensor"),
        P("dp", "context", "tensor"),
        P(None, None, "tensor"),
        P("context", "tensor"),
        P("tensor"),
        P("dp", "context", "tensor"),
    )
    out_specs = (
        P("dp", "context", "tensor"),
        P(None, "dp", "context", "tensor"),
        P("context", "tensor"),
        P(None, None, "tensor"),
    )
    return jax.shard_map(operator, mesh=mesh, in_specs=in_specs, out_specs=out_specs, check_vma=False)
```

```python
import functools
import math

import jax
import jax.numpy as jnp
import numpy as np
from jax import lax
from jax.experimental import pallas as pl
from jax.experimental.pallas import tpu as pltpu
from jax.sharding import PartitionSpec as P

D = 4096
FILT = 7


EPS = 1e-06
HIGH = lax.Precision.HIGHEST


def passed_along(shard, axis, by):
    peers = lax.axis_size(axis)
    pairs = [(i, i + by) for i in range(peers) if 0 <= i + by < peers]
    return lax.ppermute(shard, axis, pairs)


def phases(first, second, modulus):
    product = first[:, None] * second[None, :] % modulus
    return product.astype(jnp.float32) * (2.0 * math.pi / modulus)


def block_table(block_len, sign):
    index = jnp.arange(block_len, dtype=jnp.int32)
    angle = phases(index, index, block_len)
    cosine = jnp.cos(angle)
    sine = jnp.sin(angle) * sign
    return jnp.stack([jnp.stack([cosine, sine]), jnp.stack([-sine, cosine])])


def forward_rows(values, modulus):
    count, block_len, width = values.shape
    ctx_size = lax.axis_size("context")
    sub_len = block_len // ctx_size
    spread = lax.all_to_all(
        values.reshape(count, 1, block_len, width),
        "context",
        split_axis=2,
        concat_axis=1,
        tiled=True,
    )
    freq = jnp.arange(2 * ctx_size, dtype=jnp.int32)
    place = (
        jnp.arange(ctx_size, dtype=jnp.int32)[:, None] * block_len
        + lax.axis_index("context") * sub_len
        + jnp.arange(sub_len, dtype=jnp.int32)[None, :]
    )
    angle = (freq[:, None, None] * place[None] % modulus).astype(jnp.float32) * (
        2.0 * math.pi / modulus
    )
    table = jnp.stack([jnp.cos(angle), -jnp.sin(angle)])
    turned = jnp.einsum("pkcs,ncsx->npksx", table, spread, precision=HIGH)
    moved = lax.all_to_all(turned, "context", split_axis=2, concat_axis=3, tiled=True)
    return jnp.einsum("pqmb,nqjbx->npjmx", block_table(block_len, 1.0), moved, precision=HIGH)


def inverse_rows(spec, modulus):
    rows = spec.shape[2]
    block_len = spec.shape[3]
    ctx_size = lax.axis_size("context")
    index = jnp.arange(block_len, dtype=jnp.int32)
    freq = 2 * lax.axis_index("context") + jnp.arange(rows, dtype=jnp.int32)
    total = freq[:, None, None] + 2 * ctx_size * index[None, :, None]
    angle = (total * index[None, None, :] % modulus).astype(jnp.float32) * (2.0 * math.pi / modulus)
    cosine = jnp.cos(angle)
    sine = jnp.sin(angle)
    table = jnp.stack([jnp.stack([cosine, -sine]), jnp.stack([sine, cosine])])
    turned = jnp.einsum("pqjmb,nqjmx->npjbx", table, spec, precision=HIGH)
    moved = lax.all_to_all(turned, "context", split_axis=3, concat_axis=2, tiled=True)
    outer = phases(
        jnp.arange(ctx_size, dtype=jnp.int32),
        jnp.arange(2 * ctx_size, dtype=jnp.int32),
        2 * ctx_size,
    )
    real_table = jnp.stack([jnp.cos(outer), -jnp.sin(outer)])
    values = jnp.einsum("qck,nqksx->ncsx", real_table, moved, precision=HIGH) / modulus
    back = lax.all_to_all(values, "context", split_axis=1, concat_axis=2, tiled=True)
    return back.reshape(back.shape[0], back.shape[2], back.shape[3])


def shards(q_in, k_in, v_in, short_filt, long_filt, norm_gain, grad_out):
    block_len = q_in.shape[1]
    channels = q_in.shape[2]
    edge_rows = FILT - 1
    modulus = 2 * lax.axis_size("context") * block_len
    branches = jnp.stack([q_in[0], k_in[0], v_in[0]])
    before = passed_along(branches[:, block_len - edge_rows :], "context", 1)
    inputs = jnp.concatenate([before, branches], 1).astype(jnp.float32)
    shorts = jnp.zeros((3, block_len, channels), jnp.float32)
    for lag in range(FILT):
        shorts = (
            shorts
            + short_filt[:, lag][:, None, :]
            * inputs[:, edge_rows - lag : edge_rows - lag + block_len]
        )
    q_short = shorts[0]
    k_short = shorts[1]
    v_short = shorts[2]
    kv_prod = k_short * v_short
    spectra = forward_rows(jnp.stack([kv_prod, long_filt]), modulus)
    kv_real, kv_imag = (spectra[0, 0], spectra[0, 1])
    filt_real, filt_imag = (spectra[1, 0], spectra[1, 1])
    conv_spec = jnp.stack(
        [kv_real * filt_real - kv_imag * filt_imag, kv_real * filt_imag + kv_imag * filt_real]
    )[None]
    conv = inverse_rows(conv_spec, modulus)[0]
    y_out = q_short * conv
    squares = lax.psum(jnp.sum(y_out * y_out, axis=-1), "tensor")
    rms = jnp.sqrt(squares / D + EPS)[:, None]
    mixed = (y_out / rms * norm_gain).astype(jnp.bfloat16)[None]
    grad_z = grad_out[0].astype(jnp.float32) * norm_gain
    prods = lax.psum(jnp.sum(grad_z * y_out, axis=-1), "tensor")[:, None]
    grad_y = grad_z / rms - y_out * prods / (D * rms**3)
    dconv = grad_y * q_short
    grad_q = grad_y * conv
    grad_spec = forward_rows(dconv[None], modulus)[0]
    grad_real = grad_spec[0]
    grad_imag = grad_spec[1]
    dkv_spec = jnp.stack(
        [
            filt_real * grad_real + filt_imag * grad_imag,
            filt_real * grad_imag - filt_imag * grad_real,
        ]
    )
    dfilt_spec = jnp.stack(
        [kv_real * grad_real + kv_imag * grad_imag, kv_real * grad_imag - kv_imag * grad_real]
    )
    results = inverse_rows(jnp.stack([dkv_spec, dfilt_spec]), modulus)
    dkv = results[0]
    dfilt_local = results[1]
    grads = jnp.stack([grad_q, dkv * v_short, dkv * k_short])
    after = passed_along(grads[:, :edge_rows].astype(jnp.bfloat16), "context", -1).astype(
        jnp.float32
    )
    extended = jnp.concatenate([grads, after], 1)
    grad_inputs = jnp.zeros((3, block_len, channels), jnp.float32)
    for lag in range(FILT):
        grad_inputs = (
            grad_inputs + short_filt[:, lag][:, None, :] * extended[:, lag : lag + block_len]
        )
    short_local = jnp.stack(
        [
            jnp.sum(grads * inputs[:, edge_rows - lag : edge_rows - lag + block_len], axis=1)
            for lag in range(FILT)
        ],
        1,
    )
    scale = 1.0 / math.sqrt(lax.axis_size("dp") * block_len * lax.axis_size("context"))
    grad_long = lax.psum(dfilt_local, "dp") * scale
    grad_short = lax.psum(short_local, ("dp", "context")) * scale
    return (mixed, grad_inputs.astype(jnp.bfloat16)[:, None], grad_long, grad_short)

MESH = pl.DeviceIdType.MESH
F32 = jnp.float32
BF16 = jnp.bfloat16
PAD = 16
ROWS = 32


def split_table(table):
    high = table.astype(jnp.bfloat16)
    low = (table - high.astype(np.float64)).astype(jnp.bfloat16)
    return high, low


def odd_tables(seq):
    freq = 2 * np.arange(seq)[:, None] + 1
    angle = (freq * np.arange(seq)[None, :] % (4 * seq)) * (np.pi / (2 * seq))
    forward = np.concatenate([np.cos(angle), -np.sin(angle)], 0)
    return split_table(forward) + split_table(np.ascontiguousarray(forward.T) / seq)


def halves(values):
    high = values.astype(BF16)
    return high, (values - high.astype(F32)).astype(BF16)


def dot(a, b):
    return jnp.dot(a, b, preferred_element_type=F32)


def dot3(ah, al, bh, bl):
    return dot(ah, bh) + (dot(ah, bl) + dot(al, bh))


def operator_kernel(
    model_width,
    total_rows,
    q_in,
    k_in,
    v_in,
    g_in,
    f_in,
    short_in,
    gains_in,
    wh_in,
    wl_in,
    vh_in,
    vl_in,
    mixed,
    grad_inputs,
    grad_long,
    grad_short,
    branch,
    filt,
    wh,
    wl,
    vh,
    vl,
    short_filt,
    gain_in,
    shorts,
    op_h,
    op_l,
    spec_kv,
    spec_f,
    spec_g,
    prod_h,
    prod_l,
    conv,
    y_buf,
    sums,
    stats,
    grads,
    dfilt,
    dfilt_in,
    dfilt_sum,
    short_sum,
    sent,
    in_send,
    in_recv,
    in_local,
    hop_send,
    hop_recv,
    tab_sem,
    st_send,
    st_recv,
    out_send,
    out_recv,
    out_local,
    df_send,
    df_recv,
    gl_send,
    gl_recv,
    gl_local,
    fw_send,
    fw_recv,
    sh_send,
    sh_recv,
    gs_send,
    gs_recv,
    gs_local,
):
    ctx = lax.axis_size("context")
    tens = lax.axis_size("tensor")
    dp = lax.axis_index("dp")
    me = lax.axis_index("context")
    row = lax.axis_index("tensor")
    block = q_in.shape[0]
    seq = block * ctx
    width = branch.shape[2]
    half = width // 2
    taps = short_filt.shape[1]
    other = {"dp": 1 - dp}

    def peer(off):
        return lax.rem(me + off, ctx)

    def source(off):
        return lax.rem(me + ctx - off, ctx)

    def rows_of(p):
        return pl.ds(pl.multiple_of(p * block, block), block)

    def cols_of(p):
        return pl.ds(pl.multiple_of(p * width, width), width)

    def half_cols(p, h):
        return pl.ds(pl.multiple_of(p * width + h * half, half), half)

    def remote(src, dst, send, recv, device):
        copy = pltpu.make_async_remote_copy(
            src_ref=src, dst_ref=dst, send_sem=send, recv_sem=recv, device_id=device, device_id_type=MESH
        )
        copy.start()
        return copy

    def local(src, dst, sem):
        copy = pltpu.make_async_copy(src, dst, sem)
        copy.start()
        return copy

    barrier = pltpu.get_barrier_semaphore()
    near = [(a, b) for a in range(tens) for b in range(ctx) if a + b > 0]
    for a, b in near:
        pl.semaphore_signal(
            barrier,
            inc=1,
            device_id={"tensor": lax.rem(row + a, tens), "context": peer(b)},
            device_id_type=MESH,
        )
    pl.semaphore_signal(barrier, inc=1, device_id=other, device_id_type=MESH)
    pl.semaphore_wait(barrier, len(near) + 1)

    f_copies = [
        remote(
            f_in.at[:, half_cols(peer(off), dp)],
            filt.at[dp, rows_of(me), :],
            in_send.at[4, off],
            in_recv.at[4, off],
            {"context": peer(off)},
        )
        for off in range(1, ctx)
    ]
    f_own = local(f_in.at[:, half_cols(me, dp)], filt.at[dp, rows_of(me), :], in_local.at[4])
    land = pl.ds(pl.multiple_of(PAD + me * block, PAD), block)
    arrivals = {}
    branch_refs = (q_in, k_in, v_in, g_in)

    def fetch(n):
        ref = branch_refs[n]
        arrivals[n] = [
            remote(
                ref.at[:, cols_of(peer(off))],
                branch.at[n, land, :],
                in_send.at[n, off],
                in_recv.at[n, off],
                {"context": peer(off)},
            )
            for off in range(1, ctx)
        ]
        arrivals[n].append(local(ref.at[:, cols_of(me)], branch.at[n, land, :], in_local.at[n]))

    fetch(1)
    small = [local(short_in, short_filt, tab_sem.at[4]), local(gains_in, gain_in, tab_sem.at[5])]
    tables = [
        local(src, dst, tab_sem.at[n])
        for n, (src, dst) in enumerate([(wh_in, wh), (wl_in, wl), (vh_in, vh), (vl_in, vl)])
    ]

    def arrived(n):
        for copy in arrivals[n][:-1]:
            copy.wait_recv()
        arrivals[n][-1].wait()

    branch[:, :PAD, :] = jnp.zeros((4, PAD, width), BF16)
    grads[:, seq:, :] = jnp.zeros((3, 8, width), F32)

    for copy in small:
        copy.wait()

    def taps_of(n):
        return [short_filt[n, j : j + 1, cols_of(me)] for j in range(taps)]

    gain = gain_in[:, cols_of(me)]

    def at(i, rows=ROWS):
        return pl.ds(pl.multiple_of(i * rows, rows), rows)

    def short_conv(n, i, weights):
        piece = branch[n, pl.ds(pl.multiple_of(i * ROWS, ROWS), ROWS + PAD), :].astype(F32)
        total = weights[0] * piece[PAD : PAD + ROWS]
        for j in range(1, taps):
            total = total + weights[j] * piece[PAD - j : PAD - j + ROWS]
        return total

    def forward(spec):
        @pl.loop(0, 2 * seq // 256)
        def _(m):
            rows = at(m, 256)
            spec[rows, :] = dot3(wh[rows, :], wl[rows, :], op_h[...], op_l[...])

    def inverse(store):
        @pl.loop(0, seq // 256)
        def _(m):
            rows = at(m, 256)
            store(rows, dot3(vh[rows, :], vl[rows, :], prod_h[...], prod_l[...]))

    def multiply(left, right, sign):
        @pl.loop(0, seq // ROWS)
        def _(i):
            re = at(i)
            im = pl.ds(pl.multiple_of(seq + i * ROWS, ROWS), ROWS)
            a, b = left[re, :], left[im, :] * sign
            c, d = right[re, :], right[im, :]
            prod_h[re, :], prod_l[re, :] = halves(a * c - b * d)
            prod_h[im, :], prod_l[im, :] = halves(a * d + b * c)

    for copy in f_copies:
        copy.wait_recv()
    f_own.wait()
    f_hop = remote(filt.at[dp], filt.at[dp], hop_send, hop_recv, other)
    fetch(2)

    arrived(1)
    fetch(0)
    k_taps = taps_of(1)

    @pl.loop(0, seq // ROWS)
    def _(i):
        shorts[1, at(i), :] = short_conv(1, i, k_taps)

    for copy in tables:
        copy.wait()
    f_hop.wait_recv()

    @pl.loop(0, seq // ROWS)
    def _(i):
        op_h[at(i), :half], op_l[at(i), :half] = halves(filt[0, at(i), :])
        op_h[at(i), half:], op_l[at(i), half:] = halves(filt[1, at(i), :])

    forward(spec_f)

    arrived(2)
    fetch(3)
    v_taps = taps_of(2)

    @pl.loop(0, seq // ROWS)
    def _(i):
        vs = short_conv(2, i, v_taps)
        shorts[2, at(i), :] = vs
        op_h[at(i), :], op_l[at(i), :] = halves(shorts[1, at(i), :] * vs)

    forward(spec_kv)
    multiply(spec_kv, spec_f, 1.0)

    def store_conv(rows, values):
        conv[rows, :] = values

    inverse(store_conv)

    arrived(0)
    q_taps = taps_of(0)

    def folded(values):
        total = values[:, :128]
        for n in range(1, width // 128):
            total = total + values[:, n * 128 : (n + 1) * 128]
        return total

    @pl.loop(0, seq // ROWS)
    def _(i):
        qs = short_conv(0, i, q_taps)
        shorts[0, at(i), :] = qs
        y = qs * conv[at(i), :]
        y_buf[at(i), :] = y
        sums[0, at(i), :] = folded(y * y)

    groups = seq // 128
    lane = lax.broadcasted_iota(jnp.int32, (128, 128), 1)

    def share(n):
        columns = jnp.zeros((128, 128), F32)
        for b in range(groups):
            part = jnp.sum(sums[n, b * 128 : (b + 1) * 128, :], axis=1, keepdims=True)
            columns = jnp.where(lane == b, part, columns)
        stats[n, 0] = columns.T[:8]
        return [
            remote(
                stats.at[n, 0],
                stats.at[n, a * ctx + b],
                st_send.at[n, a * ctx + b],
                st_recv.at[n, a * ctx + b],
                {"tensor": lax.rem(row + a, tens), "context": peer(b)},
            )
            for a, b in near
        ]

    def gathered(n, copies):
        for copy in copies:
            copy.wait_recv()
        total = stats[n, 0]
        for r in range(1, tens * ctx):
            total = total + stats[n, r]
        return total

    def widen(n, values):
        spread = jnp.concatenate([values, jnp.zeros((120, 128), F32)], 0).T
        for b in range(groups):
            sums[n, b * 128 : (b + 1) * 128, :] = jnp.broadcast_to(spread[:, b : b + 1], (128, 128))

    st_copies = share(0)
    arrived(3)

    @pl.loop(0, seq // ROWS)
    def _(i):
        gz = branch[3, pl.ds(pl.multiple_of(PAD + i * ROWS, PAD), ROWS), :].astype(F32) * gain
        sums[1, at(i), :] = folded(gz * y_buf[at(i), :])

    prod_copies = share(1)
    inv = 1.0 / jnp.sqrt(gathered(0, st_copies) / model_width + EPS)
    widen(0, inv)

    def wide(n, i):
        return jnp.concatenate([sums[n, at(i), :]] * (width // 128), 1)

    @pl.loop(0, seq // ROWS)
    def _(i):
        sent[3, at(i), :] = (y_buf[at(i), :] * wide(0, i) * gain).astype(BF16)

    def send_back(n, target):
        copies = [
            remote(
                sent.at[n, rows_of(peer(off)), :],
                target,
                out_send.at[n, off],
                out_recv.at[n, off],
                {"context": peer(off)},
            )
            for off in range(1, ctx)
        ]
        return copies, local(sent.at[n, rows_of(me), :], target, out_local.at[n])

    back = [send_back(3, mixed.at[0, :, cols_of(me)])]
    widen(1, gathered(1, prod_copies) * (inv * inv * inv / model_width))

    @pl.loop(0, seq // ROWS)
    def _(i):
        gz = branch[3, pl.ds(pl.multiple_of(PAD + i * ROWS, PAD), ROWS), :].astype(F32) * gain
        dy = gz * wide(0, i) - y_buf[at(i), :] * wide(1, i)
        op_h[at(i), :], op_l[at(i), :] = halves(dy * shorts[0, at(i), :])
        grads[0, at(i), :] = dy * conv[at(i), :]

    scale = 1.0 / math.sqrt(total_rows)

    def back_short(n):
        weights = taps_of(n)

        @pl.loop(0, seq // ROWS)
        def _(i):
            piece = grads[n, pl.ds(pl.multiple_of(i * ROWS, ROWS), ROWS + 8), :]
            total = weights[0] * piece[:ROWS]
            for j in range(1, taps):
                total = total + weights[j] * piece[j : j + ROWS]
            sent[n, at(i), :] = total.astype(BF16)

        back.append(send_back(n, grad_inputs.at[n, 0, :, cols_of(me)]))

    def short_grads(n):
        def body(i, acc):
            own = grads[n, at(i), :]
            inputs = branch[n, pl.ds(pl.multiple_of(i * ROWS, ROWS), ROWS + PAD), :].astype(F32)
            out = []
            for j in range(taps):
                prod = own * inputs[PAD - j : PAD - j + ROWS]
                part = acc[j]
                for r in range(ROWS // 8):
                    part = part + prod[r * 8 : (r + 1) * 8]
                out.append(part)
            return tuple(out)

        acc = lax.fori_loop(0, seq // ROWS, body, tuple(jnp.zeros((8, width), F32) for _ in range(taps)))
        for j in range(taps):
            short_sum[0, n, j : j + 1, :] = jnp.sum(acc[j], axis=0, keepdims=True) * scale

    back_short(0)

    forward(spec_g)
    multiply(spec_kv, spec_g, -1.0)

    def store_dfilt(rows, values):
        dfilt[0, rows, :] = values[:, :half] * scale
        dfilt[1, rows, :] = values[:, half:] * scale

    inverse(store_dfilt)
    df_copy = remote(dfilt.at[1 - dp], dfilt_in, df_send, df_recv, other)

    multiply(spec_f, spec_g, -1.0)

    def store_dkv(rows, values):
        grads[1, rows, :] = values * shorts[2, rows, :]
        grads[2, rows, :] = values * shorts[1, rows, :]

    inverse(store_dkv)
    back_short(1)
    df_copy.wait_recv()
    dfilt_sum[...] = (dfilt[dp] + dfilt_in[...]).astype(BF16)
    gl_target = grad_long.at[:, half_cols(me, dp)]
    gl_copies = [
        remote(
            dfilt_sum.at[rows_of(peer(off)), :],
            gl_target,
            gl_send.at[off],
            gl_recv.at[off],
            {"context": peer(off)},
        )
        for off in range(1, ctx)
    ]
    gl_own = local(dfilt_sum.at[rows_of(me), :], gl_target, gl_local)
    forwards = [remote(dfilt_sum.at[rows_of(me), :], gl_target, fw_send.at[0], fw_recv.at[0], other)]

    back_short(2)

    for n in range(3):
        short_grads(n)
    sh_copy = remote(short_sum.at[0], short_sum.at[1], sh_send, sh_recv, other)

    for off in range(1, ctx):
        gl_copies[off - 1].wait_recv()
        piece = grad_long.at[:, half_cols(source(off), dp)]
        forwards.append(remote(piece, piece, fw_send.at[off], fw_recv.at[off], other))
    sh_copy.wait_recv()
    short_sum[2] = short_sum[0] + short_sum[1]
    gs_target = grad_short.at[:, :, cols_of(me)]
    gs_copies = [
        remote(short_sum.at[2], gs_target, gs_send.at[off], gs_recv.at[off], {"context": peer(off)})
        for off in range(1, ctx)
    ]
    gs_own = local(short_sum.at[2], gs_target, gs_local)
    for copies, own in back:
        own.wait()
        for copy in copies:
            copy.wait()
    gl_own.wait()
    for copy in gl_copies:
        copy.wait_send()
    for copy in forwards:
        copy.wait()
    gs_own.wait()
    for copy in gs_copies:
        copy.wait()
    sh_copy.wait_send()
    df_copy.wait_send()
    f_hop.wait_send()
    for copy in f_copies + st_copies + prod_copies:
        copy.wait_send()
    for n in range(4):
        for copy in arrivals[n][:-1]:
            copy.wait_send()


def deliver_kernel(
    mixed, grad_inputs, grad_long, grad_short, mixed_out, inputs_out, long_out, short_out, narrow, wide, sem
):
    load = pltpu.make_async_copy(grad_long, narrow, sem.at[0])
    load.start()
    copies = [
        pltpu.make_async_copy(mixed, mixed_out, sem.at[1]),
        pltpu.make_async_copy(grad_short, short_out, sem.at[2]),
    ]
    for n in range(3):
        copies.append(pltpu.make_async_copy(grad_inputs.at[n], inputs_out.at[n], sem.at[3 + n]))
    for copy in copies:
        copy.start()
    load.wait()
    wide[...] = narrow[...].astype(F32)
    store = pltpu.make_async_copy(wide, long_out, sem.at[6])
    store.start()
    store.wait()
    for copy in copies:
        copy.wait()


def fused(q_in, k_in, v_in, short_filt, long_filt, norm_gain, grad_out):
    _, block, channels = q_in.shape
    ctx = lax.axis_size("context")
    tens = lax.axis_size("tensor")
    seq = block * ctx
    width = channels // ctx
    tables = [jnp.asarray(t) for t in odd_tables(seq)]
    dma = pltpu.SemaphoreType.DMA
    anywhere = pl.BlockSpec(memory_space=pl.ANY)
    in_hbm = pl.BlockSpec(memory_space=pltpu.HBM)
    outs = pl.pallas_call(
        functools.partial(operator_kernel, D, lax.axis_size("dp") * seq),
        out_shape=(
            jax.ShapeDtypeStruct((1, block, channels), BF16),
            jax.ShapeDtypeStruct((3, 1, block, channels), BF16),
            jax.ShapeDtypeStruct((block, channels), BF16),
            jax.ShapeDtypeStruct(short_filt.shape, F32),
        ),
        in_specs=[in_hbm] * 11,
        out_specs=(anywhere,) * 4,
        scratch_shapes=[
            pltpu.VMEM((4, PAD + seq, width), BF16),
            pltpu.VMEM((2, seq, width // 2), F32),
            pltpu.VMEM((2 * seq, seq), BF16),
            pltpu.VMEM((2 * seq, seq), BF16),
            pltpu.VMEM((seq, 2 * seq), BF16),
            pltpu.VMEM((seq, 2 * seq), BF16),
            pltpu.VMEM(short_filt.shape, F32),
            pltpu.VMEM((1, channels), F32),
            pltpu.VMEM((3, seq, width), F32),
            pltpu.VMEM((seq, width), BF16),
            pltpu.VMEM((seq, width), BF16),
            pltpu.VMEM((2 * seq, width), F32),
            pltpu.VMEM((2 * seq, width), F32),
            pltpu.VMEM((2 * seq, width), F32),
            pltpu.VMEM((2 * seq, width), BF16),
            pltpu.VMEM((2 * seq, width), BF16),
            pltpu.VMEM((seq, width), F32),
            pltpu.VMEM((seq, width), F32),
            pltpu.VMEM((2, seq, 128), F32),
            pltpu.VMEM((2, tens * ctx, 8, 128), F32),
            pltpu.VMEM((3, seq + 8, width), F32),
            pltpu.VMEM((2, seq, width // 2), F32),
            pltpu.VMEM((seq, width // 2), F32),
            pltpu.VMEM((seq, width // 2), BF16),
            pltpu.VMEM((3, 3, short_filt.shape[1], width), F32),
            pltpu.VMEM((4, seq, width), BF16),
            dma((5, ctx)),
            dma((5, ctx)),
            dma((5,)),
            dma,
            dma,
            dma((6,)),
            dma((2, tens * ctx)),
            dma((2, tens * ctx)),
            dma((4, ctx)),
            dma((4, ctx)),
            dma((4,)),
            dma,
            dma,
            dma((ctx,)),
            dma((ctx,)),
            dma,
            dma((ctx,)),
            dma((ctx,)),
            dma,
            dma,
            dma((ctx,)),
            dma((ctx,)),
            dma,
        ],
        compiler_params=pltpu.CompilerParams(
            collective_id=0, has_side_effects=True, vmem_limit_bytes=60 * 2**20
        ),
    )(
        q_in[0],
        k_in[0],
        v_in[0],
        grad_out[0],
        long_filt,
        short_filt,
        norm_gain[None],
        *tables,
    )
    return pl.pallas_call(
        deliver_kernel,
        out_shape=(
            jax.ShapeDtypeStruct((1, block, channels), BF16),
            jax.ShapeDtypeStruct((3, 1, block, channels), BF16),
            jax.ShapeDtypeStruct((block, channels), F32),
            jax.ShapeDtypeStruct(short_filt.shape, F32),
        ),
        in_specs=[anywhere] * 4,
        out_specs=(anywhere,) * 4,
        scratch_shapes=[
            pltpu.VMEM((block, channels), BF16),
            pltpu.VMEM((block, channels), F32),
            dma((7,)),
        ],
        compiler_params=pltpu.CompilerParams(vmem_limit_bytes=60 * 2**20),
    )(*outs)


def operator(q_in, k_in, v_in, short_filt, long_filt, norm_gain, grad_out):
    _, block, channels = q_in.shape
    ctx = lax.axis_size("context")
    dense = block * ctx <= 1024 and block % 128 == 0 and channels % (256 * ctx) == 0
    form = fused if dense and lax.axis_size("dp") == 2 else shards
    return form(q_in, k_in, v_in, short_filt, long_filt, norm_gain, grad_out)


def solution(mesh):
    in_specs = (
        P("dp", "context", "tensor"),
        P("dp", "context", "tensor"),
        P("dp", "context", "tensor"),
        P(None, None, "tensor"),
        P("context", "tensor"),
        P("tensor"),
        P("dp", "context", "tensor"),
    )
    out_specs = (
        P("dp", "context", "tensor"),
        P(None, "dp", "context", "tensor"),
        P("context", "tensor"),
        P(None, None, "tensor"),
    )
    return jax.shard_map(operator, mesh=mesh, in_specs=in_specs, out_specs=out_specs, check_vma=False)
```

```python
import functools
import math

import jax
import jax.numpy as jnp
import numpy as np
from jax import lax
from jax.experimental import pallas as pl
from jax.experimental.pallas import tpu as pltpu
from jax.sharding import PartitionSpec as P

D = 4096
FILT = 7


EPS = 1e-06
HIGH = lax.Precision.HIGHEST


def passed_along(shard, axis, by):
    peers = lax.axis_size(axis)
    pairs = [(i, i + by) for i in range(peers) if 0 <= i + by < peers]
    return lax.ppermute(shard, axis, pairs)


def phases(first, second, modulus):
    product = first[:, None] * second[None, :] % modulus
    return product.astype(jnp.float32) * (2.0 * math.pi / modulus)


def block_table(block_len, sign):
    index = jnp.arange(block_len, dtype=jnp.int32)
    angle = phases(index, index, block_len)
    cosine = jnp.cos(angle)
    sine = jnp.sin(angle) * sign
    return jnp.stack([jnp.stack([cosine, sine]), jnp.stack([-sine, cosine])])


def forward_rows(values, modulus):
    count, block_len, width = values.shape
    ctx_size = lax.axis_size("context")
    sub_len = block_len // ctx_size
    spread = lax.all_to_all(
        values.reshape(count, 1, block_len, width),
        "context",
        split_axis=2,
        concat_axis=1,
        tiled=True,
    )
    freq = jnp.arange(2 * ctx_size, dtype=jnp.int32)
    place = (
        jnp.arange(ctx_size, dtype=jnp.int32)[:, None] * block_len
        + lax.axis_index("context") * sub_len
        + jnp.arange(sub_len, dtype=jnp.int32)[None, :]
    )
    angle = (freq[:, None, None] * place[None] % modulus).astype(jnp.float32) * (
        2.0 * math.pi / modulus
    )
    table = jnp.stack([jnp.cos(angle), -jnp.sin(angle)])
    turned = jnp.einsum("pkcs,ncsx->npksx", table, spread, precision=HIGH)
    moved = lax.all_to_all(turned, "context", split_axis=2, concat_axis=3, tiled=True)
    return jnp.einsum("pqmb,nqjbx->npjmx", block_table(block_len, 1.0), moved, precision=HIGH)


def inverse_rows(spec, modulus):
    rows = spec.shape[2]
    block_len = spec.shape[3]
    ctx_size = lax.axis_size("context")
    index = jnp.arange(block_len, dtype=jnp.int32)
    freq = 2 * lax.axis_index("context") + jnp.arange(rows, dtype=jnp.int32)
    total = freq[:, None, None] + 2 * ctx_size * index[None, :, None]
    angle = (total * index[None, None, :] % modulus).astype(jnp.float32) * (2.0 * math.pi / modulus)
    cosine = jnp.cos(angle)
    sine = jnp.sin(angle)
    table = jnp.stack([jnp.stack([cosine, -sine]), jnp.stack([sine, cosine])])
    turned = jnp.einsum("pqjmb,nqjmx->npjbx", table, spec, precision=HIGH)
    moved = lax.all_to_all(turned, "context", split_axis=3, concat_axis=2, tiled=True)
    outer = phases(
        jnp.arange(ctx_size, dtype=jnp.int32),
        jnp.arange(2 * ctx_size, dtype=jnp.int32),
        2 * ctx_size,
    )
    real_table = jnp.stack([jnp.cos(outer), -jnp.sin(outer)])
    values = jnp.einsum("qck,nqksx->ncsx", real_table, moved, precision=HIGH) / modulus
    back = lax.all_to_all(values, "context", split_axis=1, concat_axis=2, tiled=True)
    return back.reshape(back.shape[0], back.shape[2], back.shape[3])


def shards(q_in, k_in, v_in, short_filt, long_filt, norm_gain, grad_out):
    block_len = q_in.shape[1]
    channels = q_in.shape[2]
    edge_rows = FILT - 1
    modulus = 2 * lax.axis_size("context") * block_len
    branches = jnp.stack([q_in[0], k_in[0], v_in[0]])
    before = passed_along(branches[:, block_len - edge_rows :], "context", 1)
    inputs = jnp.concatenate([before, branches], 1).astype(jnp.float32)
    shorts = jnp.zeros((3, block_len, channels), jnp.float32)
    for lag in range(FILT):
        shorts = (
            shorts
            + short_filt[:, lag][:, None, :]
            * inputs[:, edge_rows - lag : edge_rows - lag + block_len]
        )
    q_short = shorts[0]
    k_short = shorts[1]
    v_short = shorts[2]
    kv_prod = k_short * v_short
    spectra = forward_rows(jnp.stack([kv_prod, long_filt]), modulus)
    kv_real, kv_imag = (spectra[0, 0], spectra[0, 1])
    filt_real, filt_imag = (spectra[1, 0], spectra[1, 1])
    conv_spec = jnp.stack(
        [kv_real * filt_real - kv_imag * filt_imag, kv_real * filt_imag + kv_imag * filt_real]
    )[None]
    conv = inverse_rows(conv_spec, modulus)[0]
    y_out = q_short * conv
    squares = lax.psum(jnp.sum(y_out * y_out, axis=-1), "tensor")
    rms = jnp.sqrt(squares / D + EPS)[:, None]
    mixed = (y_out / rms * norm_gain).astype(jnp.bfloat16)[None]
    grad_z = grad_out[0].astype(jnp.float32) * norm_gain
    prods = lax.psum(jnp.sum(grad_z * y_out, axis=-1), "tensor")[:, None]
    grad_y = grad_z / rms - y_out * prods / (D * rms**3)
    dconv = grad_y * q_short
    grad_q = grad_y * conv
    grad_spec = forward_rows(dconv[None], modulus)[0]
    grad_real = grad_spec[0]
    grad_imag = grad_spec[1]
    dkv_spec = jnp.stack(
        [
            filt_real * grad_real + filt_imag * grad_imag,
            filt_real * grad_imag - filt_imag * grad_real,
        ]
    )
    dfilt_spec = jnp.stack(
        [kv_real * grad_real + kv_imag * grad_imag, kv_real * grad_imag - kv_imag * grad_real]
    )
    results = inverse_rows(jnp.stack([dkv_spec, dfilt_spec]), modulus)
    dkv = results[0]
    dfilt_local = results[1]
    grads = jnp.stack([grad_q, dkv * v_short, dkv * k_short])
    after = passed_along(grads[:, :edge_rows].astype(jnp.bfloat16), "context", -1).astype(
        jnp.float32
    )
    extended = jnp.concatenate([grads, after], 1)
    grad_inputs = jnp.zeros((3, block_len, channels), jnp.float32)
    for lag in range(FILT):
        grad_inputs = (
            grad_inputs + short_filt[:, lag][:, None, :] * extended[:, lag : lag + block_len]
        )
    short_local = jnp.stack(
        [
            jnp.sum(grads * inputs[:, edge_rows - lag : edge_rows - lag + block_len], axis=1)
            for lag in range(FILT)
        ],
        1,
    )
    scale = 1.0 / math.sqrt(lax.axis_size("dp") * block_len * lax.axis_size("context"))
    grad_long = lax.psum(dfilt_local, "dp") * scale
    grad_short = lax.psum(short_local, ("dp", "context")) * scale
    return (mixed, grad_inputs.astype(jnp.bfloat16)[:, None], grad_long, grad_short)

MESH = pl.DeviceIdType.MESH
F32 = jnp.float32
BF16 = jnp.bfloat16
PAD = 16
ROWS = 32


def split_table(table):
    high = table.astype(jnp.bfloat16)
    low = (table - high.astype(np.float64)).astype(jnp.bfloat16)
    return high, low


def odd_tables(seq):
    freq = 2 * np.arange(seq)[:, None] + 1
    angle = (freq * np.arange(seq)[None, :] % (4 * seq)) * (np.pi / (2 * seq))
    forward = np.concatenate([np.cos(angle), -np.sin(angle)], 0)
    return split_table(forward) + split_table(np.ascontiguousarray(forward.T) / seq)


def halves(values):
    high = values.astype(BF16)
    return high, (values - high.astype(F32)).astype(BF16)


def dot(a, b):
    return jnp.dot(a, b, preferred_element_type=F32)


def dot3(ah, al, bh, bl):
    return dot(ah, bh) + (dot(ah, bl) + dot(al, bh))


def operator_kernel(
    model_width,
    total_rows,
    q_in,
    k_in,
    v_in,
    g_in,
    f_in,
    short_in,
    gains_in,
    wh_in,
    wl_in,
    vh_in,
    vl_in,
    mixed,
    grad_inputs,
    grad_long,
    grad_short,
    staged,
    f_staged,
    branch,
    filt,
    wh,
    wl,
    vh,
    vl,
    short_filt,
    gain_in,
    shorts,
    op_h,
    op_l,
    spec_kv,
    spec_f,
    spec_g,
    prod_h,
    prod_l,
    conv,
    y_buf,
    sums,
    stats,
    grads,
    dfilt,
    dfilt_in,
    dfilt_sum,
    long_buf,
    short_sum,
    sent,
    in_send,
    in_recv,
    in_local,
    stage_sem,
    hop_send,
    hop_recv,
    tab_sem,
    st_send,
    st_recv,
    out_send,
    out_recv,
    out_local,
    df_send,
    df_recv,
    gl_send,
    gl_recv,
    gl_local,
    fw_send,
    fw_recv,
    sh_send,
    sh_recv,
    gs_send,
    gs_recv,
    gs_local,
):
    ctx = lax.axis_size("context")
    tens = lax.axis_size("tensor")
    dp = lax.axis_index("dp")
    me = lax.axis_index("context")
    row = lax.axis_index("tensor")
    block = q_in.shape[0]
    seq = block * ctx
    width = branch.shape[2]
    half = width // 2
    taps = short_filt.shape[1]
    other = {"dp": 1 - dp}

    def peer(off):
        return lax.rem(me + off, ctx)

    def source(off):
        return lax.rem(me + ctx - off, ctx)

    def rows_of(p):
        return pl.ds(pl.multiple_of(p * block, block), block)

    def cols_of(p):
        return pl.ds(pl.multiple_of(p * width, width), width)

    def half_cols(p, h):
        return pl.ds(pl.multiple_of(p * width + h * half, half), half)

    def remote(src, dst, send, recv, device):
        copy = pltpu.make_async_remote_copy(
            src_ref=src, dst_ref=dst, send_sem=send, recv_sem=recv, device_id=device, device_id_type=MESH
        )
        copy.start()
        return copy

    def local(src, dst, sem):
        copy = pltpu.make_async_copy(src, dst, sem)
        copy.start()
        return copy

    f_load = local(f_in, f_staged, stage_sem.at[4])
    loads = {n: local(ref, staged.at[n], stage_sem.at[n]) for n, ref in ((1, k_in), (2, v_in), (0, q_in), (3, g_in))}

    barrier = pltpu.get_barrier_semaphore()
    near = [(a, b) for a in range(tens) for b in range(ctx) if a + b > 0]
    for a, b in near:
        pl.semaphore_signal(
            barrier,
            inc=1,
            device_id={"tensor": lax.rem(row + a, tens), "context": peer(b)},
            device_id_type=MESH,
        )
    pl.semaphore_signal(barrier, inc=1, device_id=other, device_id_type=MESH)
    pl.semaphore_wait(barrier, len(near) + 1)

    f_load.wait()
    f_copies = [
        remote(
            f_staged.at[:, half_cols(peer(off), dp)],
            filt.at[dp, rows_of(me), :],
            in_send.at[4, off],
            in_recv.at[4, off],
            {"context": peer(off)},
        )
        for off in range(1, ctx)
    ]
    f_own = local(f_staged.at[:, half_cols(me, dp)], filt.at[dp, rows_of(me), :], in_local.at[4])
    land = pl.ds(pl.multiple_of(PAD + me * block, PAD), block)
    arrivals = {}

    def fetch(n):
        loads[n].wait()
        ref = staged.at[n]
        arrivals[n] = [
            remote(
                ref.at[:, cols_of(peer(off))],
                branch.at[n, land, :],
                in_send.at[n, off],
                in_recv.at[n, off],
                {"context": peer(off)},
            )
            for off in range(1, ctx)
        ]
        arrivals[n].append(local(ref.at[:, cols_of(me)], branch.at[n, land, :], in_local.at[n]))

    fetch(1)
    small = [local(short_in, short_filt, tab_sem.at[4]), local(gains_in, gain_in, tab_sem.at[5])]
    tables = [
        local(src, dst, tab_sem.at[n])
        for n, (src, dst) in enumerate([(wh_in, wh), (wl_in, wl), (vh_in, vh), (vl_in, vl)])
    ]

    def arrived(n):
        for copy in arrivals[n][:-1]:
            copy.wait_recv()
        arrivals[n][-1].wait()

    branch[:, :PAD, :] = jnp.zeros((4, PAD, width), BF16)
    grads[:, seq:, :] = jnp.zeros((3, 8, width), F32)

    for copy in small:
        copy.wait()

    def taps_of(n):
        return [short_filt[n, j : j + 1, cols_of(me)] for j in range(taps)]

    gain = gain_in[:, cols_of(me)]

    def at(i, rows=ROWS):
        return pl.ds(pl.multiple_of(i * rows, rows), rows)

    def short_conv(n, i, weights):
        piece = branch[n, pl.ds(pl.multiple_of(i * ROWS, ROWS), ROWS + PAD), :].astype(F32)
        total = weights[0] * piece[PAD : PAD + ROWS]
        for j in range(1, taps):
            total = total + weights[j] * piece[PAD - j : PAD - j + ROWS]
        return total

    def forward(spec):
        @pl.loop(0, 2 * seq // 256)
        def _(m):
            rows = at(m, 256)
            spec[rows, :] = dot3(wh[rows, :], wl[rows, :], op_h[...], op_l[...])

    def inverse(store):
        @pl.loop(0, seq // 256)
        def _(m):
            rows = at(m, 256)
            store(rows, dot3(vh[rows, :], vl[rows, :], prod_h[...], prod_l[...]))

    def multiply(left, right, sign):
        @pl.loop(0, seq // ROWS)
        def _(i):
            re = at(i)
            im = pl.ds(pl.multiple_of(seq + i * ROWS, ROWS), ROWS)
            a, b = left[re, :], left[im, :] * sign
            c, d = right[re, :], right[im, :]
            prod_h[re, :], prod_l[re, :] = halves(a * c - b * d)
            prod_h[im, :], prod_l[im, :] = halves(a * d + b * c)

    for copy in f_copies:
        copy.wait_recv()
    f_own.wait()
    f_hop = remote(filt.at[dp], filt.at[dp], hop_send, hop_recv, other)
    fetch(2)

    arrived(1)
    fetch(0)
    k_taps = taps_of(1)

    @pl.loop(0, seq // ROWS)
    def _(i):
        shorts[1, at(i), :] = short_conv(1, i, k_taps)

    for copy in tables:
        copy.wait()
    f_hop.wait_recv()

    @pl.loop(0, seq // ROWS)
    def _(i):
        op_h[at(i), :half], op_l[at(i), :half] = halves(filt[0, at(i), :])
        op_h[at(i), half:], op_l[at(i), half:] = halves(filt[1, at(i), :])

    forward(spec_f)

    arrived(2)
    fetch(3)
    v_taps = taps_of(2)

    @pl.loop(0, seq // ROWS)
    def _(i):
        vs = short_conv(2, i, v_taps)
        shorts[2, at(i), :] = vs
        op_h[at(i), :], op_l[at(i), :] = halves(shorts[1, at(i), :] * vs)

    forward(spec_kv)
    multiply(spec_kv, spec_f, 1.0)

    def store_conv(rows, values):
        conv[rows, :] = values

    inverse(store_conv)

    arrived(0)
    q_taps = taps_of(0)

    def folded(values):
        total = values[:, :128]
        for n in range(1, width // 128):
            total = total + values[:, n * 128 : (n + 1) * 128]
        return total

    @pl.loop(0, seq // ROWS)
    def _(i):
        qs = short_conv(0, i, q_taps)
        shorts[0, at(i), :] = qs
        y = qs * conv[at(i), :]
        y_buf[at(i), :] = y
        sums[0, at(i), :] = folded(y * y)

    groups = seq // 128
    lane = lax.broadcasted_iota(jnp.int32, (128, 128), 1)

    def share(n):
        columns = jnp.zeros((128, 128), F32)
        for b in range(groups):
            part = jnp.sum(sums[n, b * 128 : (b + 1) * 128, :], axis=1, keepdims=True)
            columns = jnp.where(lane == b, part, columns)
        stats[n, 0] = columns.T[:8]
        return [
            remote(
                stats.at[n, 0],
                stats.at[n, a * ctx + b],
                st_send.at[n, a * ctx + b],
                st_recv.at[n, a * ctx + b],
                {"tensor": lax.rem(row + a, tens), "context": peer(b)},
            )
            for a, b in near
        ]

    def gathered(n, copies):
        for copy in copies:
            copy.wait_recv()
        total = stats[n, 0]
        for r in range(1, tens * ctx):
            total = total + stats[n, r]
        return total

    def widen(n, values):
        spread = jnp.concatenate([values, jnp.zeros((120, 128), F32)], 0).T
        for b in range(groups):
            sums[n, b * 128 : (b + 1) * 128, :] = jnp.broadcast_to(spread[:, b : b + 1], (128, 128))

    st_copies = share(0)
    inv = 1.0 / jnp.sqrt(gathered(0, st_copies) / model_width + EPS)
    widen(0, inv)

    def wide(n, i):
        return jnp.concatenate([sums[n, at(i), :]] * (width // 128), 1)

    @pl.loop(0, seq // ROWS)
    def _(i):
        sent[3, at(i), :] = (y_buf[at(i), :] * wide(0, i) * gain).astype(BF16)

    def send_back(n, target):
        copies = [
            remote(
                sent.at[n, rows_of(peer(off)), :],
                target,
                out_send.at[n, off],
                out_recv.at[n, off],
                {"context": peer(off)},
            )
            for off in range(1, ctx)
        ]
        return copies, local(sent.at[n, rows_of(me), :], target, out_local.at[n])

    back = [send_back(3, mixed.at[0, :, cols_of(me)])]
    arrived(3)

    @pl.loop(0, seq // ROWS)
    def _(i):
        gz = branch[3, pl.ds(pl.multiple_of(PAD + i * ROWS, PAD), ROWS), :].astype(F32) * gain
        sums[1, at(i), :] = folded(gz * y_buf[at(i), :])

    prod_copies = share(1)
    widen(1, gathered(1, prod_copies) * (inv * inv * inv / model_width))

    @pl.loop(0, seq // ROWS)
    def _(i):
        gz = branch[3, pl.ds(pl.multiple_of(PAD + i * ROWS, PAD), ROWS), :].astype(F32) * gain
        dy = gz * wide(0, i) - y_buf[at(i), :] * wide(1, i)
        op_h[at(i), :], op_l[at(i), :] = halves(dy * shorts[0, at(i), :])
        grads[0, at(i), :] = dy * conv[at(i), :]

    scale = 1.0 / math.sqrt(total_rows)

    def back_short(n):
        weights = taps_of(n)

        @pl.loop(0, seq // ROWS)
        def _(i):
            piece = grads[n, pl.ds(pl.multiple_of(i * ROWS, ROWS), ROWS + 8), :]
            total = weights[0] * piece[:ROWS]
            for j in range(1, taps):
                total = total + weights[j] * piece[j : j + ROWS]
            sent[n, at(i), :] = total.astype(BF16)

        back.append(send_back(n, grad_inputs.at[n, 0, :, cols_of(me)]))

    def short_grads(n):
        def body(i, acc):
            own = grads[n, at(i), :]
            inputs = branch[n, pl.ds(pl.multiple_of(i * ROWS, ROWS), ROWS + PAD), :].astype(F32)
            out = []
            for j in range(taps):
                prod = own * inputs[PAD - j : PAD - j + ROWS]
                part = acc[j]
                for r in range(ROWS // 8):
                    part = part + prod[r * 8 : (r + 1) * 8]
                out.append(part)
            return tuple(out)

        acc = lax.fori_loop(0, seq // ROWS, body, tuple(jnp.zeros((8, width), F32) for _ in range(taps)))
        for j in range(taps):
            short_sum[0, n, j : j + 1, :] = jnp.sum(acc[j], axis=0, keepdims=True) * scale

    back_short(0)

    forward(spec_g)
    multiply(spec_kv, spec_g, -1.0)

    def store_dfilt(rows, values):
        dfilt[0, rows, :] = values[:, :half] * scale
        dfilt[1, rows, :] = values[:, half:] * scale

    inverse(store_dfilt)
    df_copy = remote(dfilt.at[1 - dp], dfilt_in, df_send, df_recv, other)

    multiply(spec_f, spec_g, -1.0)

    def store_dkv(rows, values):
        grads[1, rows, :] = values * shorts[2, rows, :]
        grads[2, rows, :] = values * shorts[1, rows, :]

    inverse(store_dkv)
    back_short(1)
    df_copy.wait_recv()
    dfilt_sum[...] = (dfilt[dp] + dfilt_in[...]).astype(BF16)
    gl_target = grad_long.at[:, half_cols(me, dp)]
    gl_copies = [
        remote(
            dfilt_sum.at[rows_of(peer(off)), :],
            long_buf.at[off],
            gl_send.at[off],
            gl_recv.at[off],
            {"context": peer(off)},
        )
        for off in range(1, ctx)
    ]
    gl_own = [local(dfilt_sum.at[rows_of(me), :], gl_target, gl_local.at[0])]
    forwards = [remote(dfilt_sum.at[rows_of(me), :], gl_target, fw_send.at[0], fw_recv.at[0], other)]

    back_short(2)

    for n in range(3):
        short_grads(n)
    sh_copy = remote(short_sum.at[0], short_sum.at[1], sh_send, sh_recv, other)

    for off in range(1, ctx):
        gl_copies[off - 1].wait_recv()
        piece = grad_long.at[:, half_cols(source(off), dp)]
        forwards.append(remote(long_buf.at[off], piece, fw_send.at[off], fw_recv.at[off], other))
        gl_own.append(local(long_buf.at[off], piece, gl_local.at[off]))
    sh_copy.wait_recv()
    short_sum[2] = short_sum[0] + short_sum[1]
    gs_target = grad_short.at[:, :, cols_of(me)]
    gs_copies = [
        remote(short_sum.at[2], gs_target, gs_send.at[off], gs_recv.at[off], {"context": peer(off)})
        for off in range(1, ctx)
    ]
    gs_own = local(short_sum.at[2], gs_target, gs_local)
    for copies, own in back:
        own.wait()
        for copy in copies:
            copy.wait()
    for copy in gl_own:
        copy.wait()
    for copy in gl_copies:
        copy.wait_send()
    for copy in forwards:
        copy.wait()
    gs_own.wait()
    for copy in gs_copies:
        copy.wait()
    sh_copy.wait_send()
    df_copy.wait_send()
    f_hop.wait_send()
    for copy in f_copies + st_copies + prod_copies:
        copy.wait_send()
    for n in range(4):
        for copy in arrivals[n][:-1]:
            copy.wait_send()


def deliver_kernel(
    mixed, grad_inputs, grad_long, grad_short, mixed_out, inputs_out, long_out, short_out, held, narrow, wide, short, sem
):
    def move(n, src, dst):
        copy = pltpu.make_async_copy(src, dst, sem.at[n])
        copy.start()
        return copy

    loads = [move(0, grad_long, narrow), move(1, mixed.at[0], held.at[0])]
    loads += [move(2 + n, grad_inputs.at[n, 0], held.at[1 + n]) for n in range(3)]
    loads.append(move(5, grad_short, short))
    loads[0].wait()
    wide[...] = narrow[...].astype(F32)
    stores = [move(6, wide, long_out)]
    targets = [mixed_out.at[0]] + [inputs_out.at[n, 0] for n in range(3)]
    for n in range(4):
        loads[1 + n].wait()
        stores.append(move(7 + n, held.at[n], targets[n]))
    loads[5].wait()
    stores.append(move(11, short, short_out))
    for copy in stores:
        copy.wait()


def fused(q_in, k_in, v_in, short_filt, long_filt, norm_gain, grad_out):
    _, block, channels = q_in.shape
    ctx = lax.axis_size("context")
    tens = lax.axis_size("tensor")
    seq = block * ctx
    width = channels // ctx
    tables = [jnp.asarray(t) for t in odd_tables(seq)]
    dma = pltpu.SemaphoreType.DMA
    anywhere = pl.BlockSpec(memory_space=pl.ANY)
    in_hbm = pl.BlockSpec(memory_space=pltpu.HBM)
    outs = pl.pallas_call(
        functools.partial(operator_kernel, D, lax.axis_size("dp") * seq),
        out_shape=(
            jax.ShapeDtypeStruct((1, block, channels), BF16),
            jax.ShapeDtypeStruct((3, 1, block, channels), BF16),
            jax.ShapeDtypeStruct((block, channels), BF16),
            jax.ShapeDtypeStruct(short_filt.shape, F32),
        ),
        in_specs=[in_hbm] * 11,
        out_specs=(anywhere,) * 4,
        scratch_shapes=[
            pltpu.VMEM((4, block, channels), BF16),
            pltpu.VMEM((block, channels), F32),
            pltpu.VMEM((4, PAD + seq, width), BF16),
            pltpu.VMEM((2, seq, width // 2), F32),
            pltpu.VMEM((2 * seq, seq), BF16),
            pltpu.VMEM((2 * seq, seq), BF16),
            pltpu.VMEM((seq, 2 * seq), BF16),
            pltpu.VMEM((seq, 2 * seq), BF16),
            pltpu.VMEM(short_filt.shape, F32),
            pltpu.VMEM((1, channels), F32),
            pltpu.VMEM((3, seq, width), F32),
            pltpu.VMEM((seq, width), BF16),
            pltpu.VMEM((seq, width), BF16),
            pltpu.VMEM((2 * seq, width), F32),
            pltpu.VMEM((2 * seq, width), F32),
            pltpu.VMEM((2 * seq, width), F32),
            pltpu.VMEM((2 * seq, width), BF16),
            pltpu.VMEM((2 * seq, width), BF16),
            pltpu.VMEM((seq, width), F32),
            pltpu.VMEM((seq, width), F32),
            pltpu.VMEM((2, seq, 128), F32),
            pltpu.VMEM((2, tens * ctx, 8, 128), F32),
            pltpu.VMEM((3, seq + 8, width), F32),
            pltpu.VMEM((2, seq, width // 2), F32),
            pltpu.VMEM((seq, width // 2), F32),
            pltpu.VMEM((seq, width // 2), BF16),
            pltpu.VMEM((ctx, block, width // 2), BF16),
            pltpu.VMEM((3, 3, short_filt.shape[1], width), F32),
            pltpu.VMEM((4, seq, width), BF16),
            dma((5, ctx)),
            dma((5, ctx)),
            dma((5,)),
            dma((5,)),
            dma,
            dma,
            dma((6,)),
            dma((2, tens * ctx)),
            dma((2, tens * ctx)),
            dma((4, ctx)),
            dma((4, ctx)),
            dma((4,)),
            dma,
            dma,
            dma((ctx,)),
            dma((ctx,)),
            dma((ctx,)),
            dma((ctx,)),
            dma((ctx,)),
            dma,
            dma,
            dma((ctx,)),
            dma((ctx,)),
            dma,
        ],
        compiler_params=pltpu.CompilerParams(
            collective_id=0, has_side_effects=True, vmem_limit_bytes=60 * 2**20
        ),
    )(
        q_in[0],
        k_in[0],
        v_in[0],
        grad_out[0],
        long_filt,
        short_filt,
        norm_gain[None],
        *tables,
    )
    return pl.pallas_call(
        deliver_kernel,
        out_shape=(
            jax.ShapeDtypeStruct((1, block, channels), BF16),
            jax.ShapeDtypeStruct((3, 1, block, channels), BF16),
            jax.ShapeDtypeStruct((block, channels), F32),
            jax.ShapeDtypeStruct(short_filt.shape, F32),
        ),
        in_specs=[anywhere] * 4,
        out_specs=(anywhere,) * 4,
        scratch_shapes=[
            pltpu.VMEM((4, block, channels), BF16),
            pltpu.VMEM((block, channels), BF16),
            pltpu.VMEM((block, channels), F32),
            pltpu.VMEM(short_filt.shape, F32),
            dma((12,)),
        ],
        compiler_params=pltpu.CompilerParams(vmem_limit_bytes=60 * 2**20),
    )(*outs)


def operator(q_in, k_in, v_in, short_filt, long_filt, norm_gain, grad_out):
    _, block, channels = q_in.shape
    ctx = lax.axis_size("context")
    dense = block * ctx <= 1024 and block % 128 == 0 and channels % (256 * ctx) == 0
    form = fused if dense and lax.axis_size("dp") == 2 else shards
    return form(q_in, k_in, v_in, short_filt, long_filt, norm_gain, grad_out)


def solution(mesh):
    in_specs = (
        P("dp", "context", "tensor"),
        P("dp", "context", "tensor"),
        P("dp", "context", "tensor"),
        P(None, None, "tensor"),
        P("context", "tensor"),
        P("tensor"),
        P("dp", "context", "tensor"),
    )
    out_specs = (
        P("dp", "context", "tensor"),
        P(None, "dp", "context", "tensor"),
        P("context", "tensor"),
        P(None, None, "tensor"),
    )
    return jax.shard_map(operator, mesh=mesh, in_specs=in_specs, out_specs=out_specs, check_vma=False)
```

```python
import functools
import math

import jax
import jax.numpy as jnp
import numpy as np
from jax import lax
from jax.experimental import pallas as pl
from jax.experimental.pallas import tpu as pltpu
from jax.sharding import PartitionSpec as P

D = 4096
FILT = 7


EPS = 1e-06
HIGH = lax.Precision.HIGHEST


def passed_along(shard, axis, by):
    peers = lax.axis_size(axis)
    pairs = [(i, i + by) for i in range(peers) if 0 <= i + by < peers]
    return lax.ppermute(shard, axis, pairs)


def phases(first, second, modulus):
    product = first[:, None] * second[None, :] % modulus
    return product.astype(jnp.float32) * (2.0 * math.pi / modulus)


def block_table(block_len, sign):
    index = jnp.arange(block_len, dtype=jnp.int32)
    angle = phases(index, index, block_len)
    cosine = jnp.cos(angle)
    sine = jnp.sin(angle) * sign
    return jnp.stack([jnp.stack([cosine, sine]), jnp.stack([-sine, cosine])])


def forward_rows(values, modulus):
    count, block_len, width = values.shape
    ctx_size = lax.axis_size("context")
    sub_len = block_len // ctx_size
    spread = lax.all_to_all(
        values.reshape(count, 1, block_len, width),
        "context",
        split_axis=2,
        concat_axis=1,
        tiled=True,
    )
    freq = jnp.arange(2 * ctx_size, dtype=jnp.int32)
    place = (
        jnp.arange(ctx_size, dtype=jnp.int32)[:, None] * block_len
        + lax.axis_index("context") * sub_len
        + jnp.arange(sub_len, dtype=jnp.int32)[None, :]
    )
    angle = (freq[:, None, None] * place[None] % modulus).astype(jnp.float32) * (
        2.0 * math.pi / modulus
    )
    table = jnp.stack([jnp.cos(angle), -jnp.sin(angle)])
    turned = jnp.einsum("pkcs,ncsx->npksx", table, spread, precision=HIGH)
    moved = lax.all_to_all(turned, "context", split_axis=2, concat_axis=3, tiled=True)
    return jnp.einsum("pqmb,nqjbx->npjmx", block_table(block_len, 1.0), moved, precision=HIGH)


def inverse_rows(spec, modulus):
    rows = spec.shape[2]
    block_len = spec.shape[3]
    ctx_size = lax.axis_size("context")
    index = jnp.arange(block_len, dtype=jnp.int32)
    freq = 2 * lax.axis_index("context") + jnp.arange(rows, dtype=jnp.int32)
    total = freq[:, None, None] + 2 * ctx_size * index[None, :, None]
    angle = (total * index[None, None, :] % modulus).astype(jnp.float32) * (2.0 * math.pi / modulus)
    cosine = jnp.cos(angle)
    sine = jnp.sin(angle)
    table = jnp.stack([jnp.stack([cosine, -sine]), jnp.stack([sine, cosine])])
    turned = jnp.einsum("pqjmb,nqjmx->npjbx", table, spec, precision=HIGH)
    moved = lax.all_to_all(turned, "context", split_axis=3, concat_axis=2, tiled=True)
    outer = phases(
        jnp.arange(ctx_size, dtype=jnp.int32),
        jnp.arange(2 * ctx_size, dtype=jnp.int32),
        2 * ctx_size,
    )
    real_table = jnp.stack([jnp.cos(outer), -jnp.sin(outer)])
    values = jnp.einsum("qck,nqksx->ncsx", real_table, moved, precision=HIGH) / modulus
    back = lax.all_to_all(values, "context", split_axis=1, concat_axis=2, tiled=True)
    return back.reshape(back.shape[0], back.shape[2], back.shape[3])


def shards(q_in, k_in, v_in, short_filt, long_filt, norm_gain, grad_out):
    block_len = q_in.shape[1]
    channels = q_in.shape[2]
    edge_rows = FILT - 1
    modulus = 2 * lax.axis_size("context") * block_len
    branches = jnp.stack([q_in[0], k_in[0], v_in[0]])
    before = passed_along(branches[:, block_len - edge_rows :], "context", 1)
    inputs = jnp.concatenate([before, branches], 1).astype(jnp.float32)
    shorts = jnp.zeros((3, block_len, channels), jnp.float32)
    for lag in range(FILT):
        shorts = (
            shorts
            + short_filt[:, lag][:, None, :]
            * inputs[:, edge_rows - lag : edge_rows - lag + block_len]
        )
    q_short = shorts[0]
    k_short = shorts[1]
    v_short = shorts[2]
    kv_prod = k_short * v_short
    spectra = forward_rows(jnp.stack([kv_prod, long_filt]), modulus)
    kv_real, kv_imag = (spectra[0, 0], spectra[0, 1])
    filt_real, filt_imag = (spectra[1, 0], spectra[1, 1])
    conv_spec = jnp.stack(
        [kv_real * filt_real - kv_imag * filt_imag, kv_real * filt_imag + kv_imag * filt_real]
    )[None]
    conv = inverse_rows(conv_spec, modulus)[0]
    y_out = q_short * conv
    squares = lax.psum(jnp.sum(y_out * y_out, axis=-1), "tensor")
    rms = jnp.sqrt(squares / D + EPS)[:, None]
    mixed = (y_out / rms * norm_gain).astype(jnp.bfloat16)[None]
    grad_z = grad_out[0].astype(jnp.float32) * norm_gain
    prods = lax.psum(jnp.sum(grad_z * y_out, axis=-1), "tensor")[:, None]
    grad_y = grad_z / rms - y_out * prods / (D * rms**3)
    dconv = grad_y * q_short
    grad_q = grad_y * conv
    grad_spec = forward_rows(dconv[None], modulus)[0]
    grad_real = grad_spec[0]
    grad_imag = grad_spec[1]
    dkv_spec = jnp.stack(
        [
            filt_real * grad_real + filt_imag * grad_imag,
            filt_real * grad_imag - filt_imag * grad_real,
        ]
    )
    dfilt_spec = jnp.stack(
        [kv_real * grad_real + kv_imag * grad_imag, kv_real * grad_imag - kv_imag * grad_real]
    )
    results = inverse_rows(jnp.stack([dkv_spec, dfilt_spec]), modulus)
    dkv = results[0]
    dfilt_local = results[1]
    grads = jnp.stack([grad_q, dkv * v_short, dkv * k_short])
    after = passed_along(grads[:, :edge_rows].astype(jnp.bfloat16), "context", -1).astype(
        jnp.float32
    )
    extended = jnp.concatenate([grads, after], 1)
    grad_inputs = jnp.zeros((3, block_len, channels), jnp.float32)
    for lag in range(FILT):
        grad_inputs = (
            grad_inputs + short_filt[:, lag][:, None, :] * extended[:, lag : lag + block_len]
        )
    short_local = jnp.stack(
        [
            jnp.sum(grads * inputs[:, edge_rows - lag : edge_rows - lag + block_len], axis=1)
            for lag in range(FILT)
        ],
        1,
    )
    scale = 1.0 / math.sqrt(lax.axis_size("dp") * block_len * lax.axis_size("context"))
    grad_long = lax.psum(dfilt_local, "dp") * scale
    grad_short = lax.psum(short_local, ("dp", "context")) * scale
    return (mixed, grad_inputs.astype(jnp.bfloat16)[:, None], grad_long, grad_short)

MESH = pl.DeviceIdType.MESH
F32 = jnp.float32
BF16 = jnp.bfloat16
PAD = 16
ROWS = 32


def split_table(table):
    high = table.astype(jnp.bfloat16)
    low = (table - high.astype(np.float64)).astype(jnp.bfloat16)
    return high, low


def odd_tables(seq):
    freq = 2 * np.arange(seq)[:, None] + 1
    angle = (freq * np.arange(seq)[None, :] % (4 * seq)) * (np.pi / (2 * seq))
    forward = np.concatenate([np.cos(angle), -np.sin(angle)], 0)
    return split_table(forward) + split_table(np.ascontiguousarray(forward.T) / seq)


def halves(values):
    high = values.astype(BF16)
    return high, (values - high.astype(F32)).astype(BF16)


def dot(a, b):
    return jnp.dot(a, b, preferred_element_type=F32)


def dot3(ah, al, bh, bl):
    return dot(ah, bh) + (dot(ah, bl) + dot(al, bh))


def operator_kernel(
    model_width,
    total_rows,
    q_in,
    k_in,
    v_in,
    g_in,
    f_in,
    short_in,
    gains_in,
    wh_in,
    wl_in,
    vh_in,
    vl_in,
    mixed,
    grad_inputs,
    grad_long,
    grad_short,
    staged,
    f_staged,
    branch,
    filt,
    wh,
    wl,
    vh,
    vl,
    short_filt,
    gain_in,
    shorts,
    op_h,
    op_l,
    spec_kv,
    spec_f,
    spec_g,
    prod_h,
    prod_l,
    conv,
    y_buf,
    sums,
    stats,
    grads,
    dfilt,
    dfilt_in,
    dfilt_sum,
    long_buf,
    short_sum,
    sent,
    in_send,
    in_recv,
    in_local,
    stage_sem,
    hop_send,
    hop_recv,
    tab_sem,
    st_send,
    st_recv,
    out_send,
    out_recv,
    out_local,
    df_send,
    df_recv,
    gl_send,
    gl_recv,
    gl_local,
    fw_send,
    fw_recv,
    sh_send,
    sh_recv,
    gs_send,
    gs_recv,
    gs_local,
):
    ctx = lax.axis_size("context")
    tens = lax.axis_size("tensor")
    dp = lax.axis_index("dp")
    me = lax.axis_index("context")
    row = lax.axis_index("tensor")
    block = q_in.shape[0]
    seq = block * ctx
    width = branch.shape[2]
    half = width // 2
    taps = short_filt.shape[1]
    other = {"dp": 1 - dp}

    def peer(off):
        return lax.rem(me + off, ctx)

    def source(off):
        return lax.rem(me + ctx - off, ctx)

    def rows_of(p):
        return pl.ds(pl.multiple_of(p * block, block), block)

    def cols_of(p):
        return pl.ds(pl.multiple_of(p * width, width), width)

    def half_cols(p, h):
        return pl.ds(pl.multiple_of(p * width + h * half, half), half)

    def remote(src, dst, send, recv, device):
        copy = pltpu.make_async_remote_copy(
            src_ref=src, dst_ref=dst, send_sem=send, recv_sem=recv, device_id=device, device_id_type=MESH
        )
        copy.start()
        return copy

    def local(src, dst, sem):
        copy = pltpu.make_async_copy(src, dst, sem)
        copy.start()
        return copy

    f_load = local(f_in, f_staged, stage_sem.at[4])
    loads = {n: local(ref, staged.at[n], stage_sem.at[n]) for n, ref in ((1, k_in), (2, v_in), (0, q_in), (3, g_in))}

    barrier = pltpu.get_barrier_semaphore()
    near = [(a, b) for a in range(tens) for b in range(ctx) if a + b > 0]
    for a, b in near:
        pl.semaphore_signal(
            barrier,
            inc=1,
            device_id={"tensor": lax.rem(row + a, tens), "context": peer(b)},
            device_id_type=MESH,
        )
    pl.semaphore_signal(barrier, inc=1, device_id=other, device_id_type=MESH)
    pl.semaphore_wait(barrier, len(near) + 1)

    f_load.wait()
    f_copies = [
        remote(
            f_staged.at[:, half_cols(peer(off), dp)],
            filt.at[dp, rows_of(me), :],
            in_send.at[4, off],
            in_recv.at[4, off],
            {"context": peer(off)},
        )
        for off in range(1, ctx)
    ]
    f_own = local(f_staged.at[:, half_cols(me, dp)], filt.at[dp, rows_of(me), :], in_local.at[4])
    land = pl.ds(pl.multiple_of(PAD + me * block, PAD), block)
    arrivals = {}

    def fetch(n):
        loads[n].wait()
        ref = staged.at[n]
        arrivals[n] = [
            remote(
                ref.at[:, cols_of(peer(off))],
                branch.at[n, land, :],
                in_send.at[n, off],
                in_recv.at[n, off],
                {"context": peer(off)},
            )
            for off in range(1, ctx)
        ]
        arrivals[n].append(local(ref.at[:, cols_of(me)], branch.at[n, land, :], in_local.at[n]))

    fetch(1)
    small = [local(short_in, short_filt, tab_sem.at[4]), local(gains_in, gain_in, tab_sem.at[5])]
    tables = [
        local(src, dst, tab_sem.at[n])
        for n, (src, dst) in enumerate([(wh_in, wh), (wl_in, wl), (vh_in, vh), (vl_in, vl)])
    ]

    def arrived(n):
        for copy in arrivals[n][:-1]:
            copy.wait_recv()
        arrivals[n][-1].wait()

    branch[:, :PAD, :] = jnp.zeros((4, PAD, width), BF16)
    grads[:, seq:, :] = jnp.zeros((3, 8, width), F32)

    for copy in small:
        copy.wait()

    def taps_of(n):
        return [short_filt[n, j : j + 1, cols_of(me)] for j in range(taps)]

    gain = gain_in[:, cols_of(me)]

    def at(i, rows=ROWS):
        return pl.ds(pl.multiple_of(i * rows, rows), rows)

    def short_conv(n, i, weights):
        piece = branch[n, pl.ds(pl.multiple_of(i * ROWS, ROWS), ROWS + PAD), :].astype(F32)
        total = weights[0] * piece[PAD : PAD + ROWS]
        for j in range(1, taps):
            total = total + weights[j] * piece[PAD - j : PAD - j + ROWS]
        return total

    def forward(spec):
        @pl.loop(0, 2 * seq // 256)
        def _(m):
            rows = at(m, 256)
            spec[rows, :] = dot3(wh[rows, :], wl[rows, :], op_h[...], op_l[...])

    def inverse(store):
        @pl.loop(0, seq // 256)
        def _(m):
            rows = at(m, 256)
            store(rows, dot3(vh[rows, :], vl[rows, :], prod_h[...], prod_l[...]))

    def multiply(left, right, sign):
        @pl.loop(0, seq // ROWS)
        def _(i):
            re = at(i)
            im = pl.ds(pl.multiple_of(seq + i * ROWS, ROWS), ROWS)
            a, b = left[re, :], left[im, :] * sign
            c, d = right[re, :], right[im, :]
            prod_h[re, :], prod_l[re, :] = halves(a * c - b * d)
            prod_h[im, :], prod_l[im, :] = halves(a * d + b * c)

    for copy in f_copies:
        copy.wait_recv()
    f_own.wait()
    f_hop = remote(filt.at[dp], filt.at[dp], hop_send, hop_recv, other)
    fetch(2)

    arrived(1)
    fetch(0)
    k_taps = taps_of(1)

    @pl.loop(0, seq // ROWS)
    def _(i):
        shorts[1, at(i), :] = short_conv(1, i, k_taps)

    arrived(2)
    fetch(3)
    v_taps = taps_of(2)

    @pl.loop(0, seq // ROWS)
    def _(i):
        vs = short_conv(2, i, v_taps)
        shorts[2, at(i), :] = vs
        op_h[at(i), :], op_l[at(i), :] = halves(shorts[1, at(i), :] * vs)

    for copy in tables:
        copy.wait()
    forward(spec_kv)

    f_hop.wait_recv()

    @pl.loop(0, seq // ROWS)
    def _(i):
        op_h[at(i), :half], op_l[at(i), :half] = halves(filt[0, at(i), :])
        op_h[at(i), half:], op_l[at(i), half:] = halves(filt[1, at(i), :])

    forward(spec_f)
    multiply(spec_kv, spec_f, 1.0)

    def store_conv(rows, values):
        conv[rows, :] = values

    inverse(store_conv)

    arrived(0)
    q_taps = taps_of(0)

    def folded(values):
        total = values[:, :128]
        for n in range(1, width // 128):
            total = total + values[:, n * 128 : (n + 1) * 128]
        return total

    @pl.loop(0, seq // ROWS)
    def _(i):
        qs = short_conv(0, i, q_taps)
        shorts[0, at(i), :] = qs
        y = qs * conv[at(i), :]
        y_buf[at(i), :] = y
        sums[0, at(i), :] = folded(y * y)

    groups = seq // 128
    lane = lax.broadcasted_iota(jnp.int32, (128, 128), 1)

    def share(n):
        columns = jnp.zeros((128, 128), F32)
        for b in range(groups):
            part = jnp.sum(sums[n, b * 128 : (b + 1) * 128, :], axis=1, keepdims=True)
            columns = jnp.where(lane == b, part, columns)
        stats[n, 0] = columns.T[:8]
        return [
            remote(
                stats.at[n, 0],
                stats.at[n, a * ctx + b],
                st_send.at[n, a * ctx + b],
                st_recv.at[n, a * ctx + b],
                {"tensor": lax.rem(row + a, tens), "context": peer(b)},
            )
            for a, b in near
        ]

    def gathered(n, copies):
        for copy in copies:
            copy.wait_recv()
        total = stats[n, 0]
        for r in range(1, tens * ctx):
            total = total + stats[n, r]
        return total

    def widen(n, values):
        spread = jnp.concatenate([values, jnp.zeros((120, 128), F32)], 0).T
        for b in range(groups):
            sums[n, b * 128 : (b + 1) * 128, :] = jnp.broadcast_to(spread[:, b : b + 1], (128, 128))

    st_copies = share(0)
    arrived(3)

    @pl.loop(0, seq // ROWS)
    def _(i):
        gz = branch[3, pl.ds(pl.multiple_of(PAD + i * ROWS, PAD), ROWS), :].astype(F32) * gain
        sums[1, at(i), :] = folded(gz * y_buf[at(i), :])

    prod_copies = share(1)
    inv = 1.0 / jnp.sqrt(gathered(0, st_copies) / model_width + EPS)
    widen(0, inv)

    def wide(n, i):
        return jnp.concatenate([sums[n, at(i), :]] * (width // 128), 1)

    @pl.loop(0, seq // ROWS)
    def _(i):
        sent[3, at(i), :] = (y_buf[at(i), :] * wide(0, i) * gain).astype(BF16)

    def send_back(n, target):
        copies = [
            remote(
                sent.at[n, rows_of(peer(off)), :],
                target,
                out_send.at[n, off],
                out_recv.at[n, off],
                {"context": peer(off)},
            )
            for off in range(1, ctx)
        ]
        return copies, local(sent.at[n, rows_of(me), :], target, out_local.at[n])

    back = [send_back(3, mixed.at[0, :, cols_of(me)])]
    widen(1, gathered(1, prod_copies) * (inv * inv * inv / model_width))

    @pl.loop(0, seq // ROWS)
    def _(i):
        gz = branch[3, pl.ds(pl.multiple_of(PAD + i * ROWS, PAD), ROWS), :].astype(F32) * gain
        dy = gz * wide(0, i) - y_buf[at(i), :] * wide(1, i)
        op_h[at(i), :], op_l[at(i), :] = halves(dy * shorts[0, at(i), :])
        grads[0, at(i), :] = dy * conv[at(i), :]

    scale = 1.0 / math.sqrt(total_rows)

    def back_short(n):
        weights = taps_of(n)

        @pl.loop(0, seq // ROWS)
        def _(i):
            piece = grads[n, pl.ds(pl.multiple_of(i * ROWS, ROWS), ROWS + 8), :]
            total = weights[0] * piece[:ROWS]
            for j in range(1, taps):
                total = total + weights[j] * piece[j : j + ROWS]
            sent[n, at(i), :] = total.astype(BF16)

        back.append(send_back(n, grad_inputs.at[n, 0, :, cols_of(me)]))

    def short_grads(n):
        def body(i, acc):
            own = grads[n, at(i), :]
            inputs = branch[n, pl.ds(pl.multiple_of(i * ROWS, ROWS), ROWS + PAD), :].astype(F32)
            out = []
            for j in range(taps):
                prod = own * inputs[PAD - j : PAD - j + ROWS]
                part = acc[j]
                for r in range(ROWS // 8):
                    part = part + prod[r * 8 : (r + 1) * 8]
                out.append(part)
            return tuple(out)

        acc = lax.fori_loop(0, seq // ROWS, body, tuple(jnp.zeros((8, width), F32) for _ in range(taps)))
        for j in range(taps):
            short_sum[0, n, j : j + 1, :] = jnp.sum(acc[j], axis=0, keepdims=True) * scale

    back_short(0)

    forward(spec_g)
    multiply(spec_kv, spec_g, -1.0)

    def store_dfilt(rows, values):
        dfilt[0, rows, :] = values[:, :half] * scale
        dfilt[1, rows, :] = values[:, half:] * scale

    inverse(store_dfilt)
    df_copy = remote(dfilt.at[1 - dp], dfilt_in, df_send, df_recv, other)

    multiply(spec_f, spec_g, -1.0)

    def store_dkv(rows, values):
        grads[1, rows, :] = values * shorts[2, rows, :]
        grads[2, rows, :] = values * shorts[1, rows, :]

    inverse(store_dkv)
    back_short(1)
    df_copy.wait_recv()
    dfilt_sum[...] = (dfilt[dp] + dfilt_in[...]).astype(BF16)
    gl_target = grad_long.at[:, half_cols(me, dp)]
    gl_copies = [
        remote(
            dfilt_sum.at[rows_of(peer(off)), :],
            long_buf.at[off],
            gl_send.at[off],
            gl_recv.at[off],
            {"context": peer(off)},
        )
        for off in range(1, ctx)
    ]
    gl_own = [local(dfilt_sum.at[rows_of(me), :], gl_target, gl_local.at[0])]
    forwards = [remote(dfilt_sum.at[rows_of(me), :], gl_target, fw_send.at[0], fw_recv.at[0], other)]

    back_short(2)

    for n in range(3):
        short_grads(n)
    sh_copy = remote(short_sum.at[0], short_sum.at[1], sh_send, sh_recv, other)

    for off in range(1, ctx):
        gl_copies[off - 1].wait_recv()
        piece = grad_long.at[:, half_cols(source(off), dp)]
        forwards.append(remote(long_buf.at[off], piece, fw_send.at[off], fw_recv.at[off], other))
        gl_own.append(local(long_buf.at[off], piece, gl_local.at[off]))
    sh_copy.wait_recv()
    short_sum[2] = short_sum[0] + short_sum[1]
    gs_target = grad_short.at[:, :, cols_of(me)]
    gs_copies = [
        remote(short_sum.at[2], gs_target, gs_send.at[off], gs_recv.at[off], {"context": peer(off)})
        for off in range(1, ctx)
    ]
    gs_own = local(short_sum.at[2], gs_target, gs_local)
    for copies, own in back:
        own.wait()
        for copy in copies:
            copy.wait()
    for copy in gl_own:
        copy.wait()
    for copy in gl_copies:
        copy.wait_send()
    for copy in forwards:
        copy.wait()
    gs_own.wait()
    for copy in gs_copies:
        copy.wait()
    sh_copy.wait_send()
    df_copy.wait_send()
    f_hop.wait_send()
    for copy in f_copies + st_copies + prod_copies:
        copy.wait_send()
    for n in range(4):
        for copy in arrivals[n][:-1]:
            copy.wait_send()


def deliver_kernel(
    mixed, grad_inputs, grad_long, grad_short, mixed_out, inputs_out, long_out, short_out, held, narrow, wide, short, sem
):
    def move(n, src, dst):
        copy = pltpu.make_async_copy(src, dst, sem.at[n])
        copy.start()
        return copy

    loads = [move(0, grad_long, narrow), move(1, mixed.at[0], held.at[0])]
    loads += [move(2 + n, grad_inputs.at[n, 0], held.at[1 + n]) for n in range(3)]
    loads.append(move(5, grad_short, short))
    loads[0].wait()
    wide[...] = narrow[...].astype(F32)
    stores = [move(6, wide, long_out)]
    targets = [mixed_out.at[0]] + [inputs_out.at[n, 0] for n in range(3)]
    for n in range(4):
        loads[1 + n].wait()
        stores.append(move(7 + n, held.at[n], targets[n]))
    loads[5].wait()
    stores.append(move(11, short, short_out))
    for copy in stores:
        copy.wait()


def fused(q_in, k_in, v_in, short_filt, long_filt, norm_gain, grad_out):
    _, block, channels = q_in.shape
    ctx = lax.axis_size("context")
    tens = lax.axis_size("tensor")
    seq = block * ctx
    width = channels // ctx
    tables = [jnp.asarray(t) for t in odd_tables(seq)]
    dma = pltpu.SemaphoreType.DMA
    anywhere = pl.BlockSpec(memory_space=pl.ANY)
    in_hbm = pl.BlockSpec(memory_space=pltpu.HBM)
    outs = pl.pallas_call(
        functools.partial(operator_kernel, D, lax.axis_size("dp") * seq),
        out_shape=(
            jax.ShapeDtypeStruct((1, block, channels), BF16),
            jax.ShapeDtypeStruct((3, 1, block, channels), BF16),
            jax.ShapeDtypeStruct((block, channels), BF16),
            jax.ShapeDtypeStruct(short_filt.shape, F32),
        ),
        in_specs=[in_hbm] * 11,
        out_specs=(anywhere,) * 4,
        scratch_shapes=[
            pltpu.VMEM((4, block, channels), BF16),
            pltpu.VMEM((block, channels), F32),
            pltpu.VMEM((4, PAD + seq, width), BF16),
            pltpu.VMEM((2, seq, width // 2), F32),
            pltpu.VMEM((2 * seq, seq), BF16),
            pltpu.VMEM((2 * seq, seq), BF16),
            pltpu.VMEM((seq, 2 * seq), BF16),
            pltpu.VMEM((seq, 2 * seq), BF16),
            pltpu.VMEM(short_filt.shape, F32),
            pltpu.VMEM((1, channels), F32),
            pltpu.VMEM((3, seq, width), F32),
            pltpu.VMEM((seq, width), BF16),
            pltpu.VMEM((seq, width), BF16),
            pltpu.VMEM((2 * seq, width), F32),
            pltpu.VMEM((2 * seq, width), F32),
            pltpu.VMEM((2 * seq, width), F32),
            pltpu.VMEM((2 * seq, width), BF16),
            pltpu.VMEM((2 * seq, width), BF16),
            pltpu.VMEM((seq, width), F32),
            pltpu.VMEM((seq, width), F32),
            pltpu.VMEM((2, seq, 128), F32),
            pltpu.VMEM((2, tens * ctx, 8, 128), F32),
            pltpu.VMEM((3, seq + 8, width), F32),
            pltpu.VMEM((2, seq, width // 2), F32),
            pltpu.VMEM((seq, width // 2), F32),
            pltpu.VMEM((seq, width // 2), BF16),
            pltpu.VMEM((ctx, block, width // 2), BF16),
            pltpu.VMEM((3, 3, short_filt.shape[1], width), F32),
            pltpu.VMEM((4, seq, width), BF16),
            dma((5, ctx)),
            dma((5, ctx)),
            dma((5,)),
            dma((5,)),
            dma,
            dma,
            dma((6,)),
            dma((2, tens * ctx)),
            dma((2, tens * ctx)),
            dma((4, ctx)),
            dma((4, ctx)),
            dma((4,)),
            dma,
            dma,
            dma((ctx,)),
            dma((ctx,)),
            dma((ctx,)),
            dma((ctx,)),
            dma((ctx,)),
            dma,
            dma,
            dma((ctx,)),
            dma((ctx,)),
            dma,
        ],
        compiler_params=pltpu.CompilerParams(
            collective_id=0, has_side_effects=True, vmem_limit_bytes=60 * 2**20
        ),
    )(
        q_in[0],
        k_in[0],
        v_in[0],
        grad_out[0],
        long_filt,
        short_filt,
        norm_gain[None],
        *tables,
    )
    return pl.pallas_call(
        deliver_kernel,
        out_shape=(
            jax.ShapeDtypeStruct((1, block, channels), BF16),
            jax.ShapeDtypeStruct((3, 1, block, channels), BF16),
            jax.ShapeDtypeStruct((block, channels), F32),
            jax.ShapeDtypeStruct(short_filt.shape, F32),
        ),
        in_specs=[anywhere] * 4,
        out_specs=(anywhere,) * 4,
        scratch_shapes=[
            pltpu.VMEM((4, block, channels), BF16),
            pltpu.VMEM((block, channels), BF16),
            pltpu.VMEM((block, channels), F32),
            pltpu.VMEM(short_filt.shape, F32),
            dma((12,)),
        ],
        compiler_params=pltpu.CompilerParams(vmem_limit_bytes=60 * 2**20),
    )(*outs)


def operator(q_in, k_in, v_in, short_filt, long_filt, norm_gain, grad_out):
    _, block, channels = q_in.shape
    ctx = lax.axis_size("context")
    dense = block * ctx <= 1024 and block % 128 == 0 and channels % (256 * ctx) == 0
    form = fused if dense and lax.axis_size("dp") == 2 else shards
    return form(q_in, k_in, v_in, short_filt, long_filt, norm_gain, grad_out)


def solution(mesh):
    in_specs = (
        P("dp", "context", "tensor"),
        P("dp", "context", "tensor"),
        P("dp", "context", "tensor"),
        P(None, None, "tensor"),
        P("context", "tensor"),
        P("tensor"),
        P("dp", "context", "tensor"),
    )
    out_specs = (
        P("dp", "context", "tensor"),
        P(None, "dp", "context", "tensor"),
        P("context", "tensor"),
        P(None, None, "tensor"),
    )
    return jax.shard_map(operator, mesh=mesh, in_specs=in_specs, out_specs=out_specs, check_vma=False)
```

```python
import functools
import math

import jax
import jax.numpy as jnp
import numpy as np
from jax import lax
from jax.experimental import pallas as pl
from jax.experimental.pallas import tpu as pltpu
from jax.sharding import PartitionSpec as P

D = 4096
FILT = 7


EPS = 1e-06
HIGH = lax.Precision.HIGHEST


def passed_along(shard, axis, by):
    peers = lax.axis_size(axis)
    pairs = [(i, i + by) for i in range(peers) if 0 <= i + by < peers]
    return lax.ppermute(shard, axis, pairs)


def phases(first, second, modulus):
    product = first[:, None] * second[None, :] % modulus
    return product.astype(jnp.float32) * (2.0 * math.pi / modulus)


def block_table(block_len, sign):
    index = jnp.arange(block_len, dtype=jnp.int32)
    angle = phases(index, index, block_len)
    cosine = jnp.cos(angle)
    sine = jnp.sin(angle) * sign
    return jnp.stack([jnp.stack([cosine, sine]), jnp.stack([-sine, cosine])])


def forward_rows(values, modulus):
    count, block_len, width = values.shape
    ctx_size = lax.axis_size("context")
    sub_len = block_len // ctx_size
    spread = lax.all_to_all(
        values.reshape(count, 1, block_len, width),
        "context",
        split_axis=2,
        concat_axis=1,
        tiled=True,
    )
    freq = jnp.arange(2 * ctx_size, dtype=jnp.int32)
    place = (
        jnp.arange(ctx_size, dtype=jnp.int32)[:, None] * block_len
        + lax.axis_index("context") * sub_len
        + jnp.arange(sub_len, dtype=jnp.int32)[None, :]
    )
    angle = (freq[:, None, None] * place[None] % modulus).astype(jnp.float32) * (
        2.0 * math.pi / modulus
    )
    table = jnp.stack([jnp.cos(angle), -jnp.sin(angle)])
    turned = jnp.einsum("pkcs,ncsx->npksx", table, spread, precision=HIGH)
    moved = lax.all_to_all(turned, "context", split_axis=2, concat_axis=3, tiled=True)
    return jnp.einsum("pqmb,nqjbx->npjmx", block_table(block_len, 1.0), moved, precision=HIGH)


def inverse_rows(spec, modulus):
    rows = spec.shape[2]
    block_len = spec.shape[3]
    ctx_size = lax.axis_size("context")
    index = jnp.arange(block_len, dtype=jnp.int32)
    freq = 2 * lax.axis_index("context") + jnp.arange(rows, dtype=jnp.int32)
    total = freq[:, None, None] + 2 * ctx_size * index[None, :, None]
    angle = (total * index[None, None, :] % modulus).astype(jnp.float32) * (2.0 * math.pi / modulus)
    cosine = jnp.cos(angle)
    sine = jnp.sin(angle)
    table = jnp.stack([jnp.stack([cosine, -sine]), jnp.stack([sine, cosine])])
    turned = jnp.einsum("pqjmb,nqjmx->npjbx", table, spec, precision=HIGH)
    moved = lax.all_to_all(turned, "context", split_axis=3, concat_axis=2, tiled=True)
    outer = phases(
        jnp.arange(ctx_size, dtype=jnp.int32),
        jnp.arange(2 * ctx_size, dtype=jnp.int32),
        2 * ctx_size,
    )
    real_table = jnp.stack([jnp.cos(outer), -jnp.sin(outer)])
    values = jnp.einsum("qck,nqksx->ncsx", real_table, moved, precision=HIGH) / modulus
    back = lax.all_to_all(values, "context", split_axis=1, concat_axis=2, tiled=True)
    return back.reshape(back.shape[0], back.shape[2], back.shape[3])


def shards(q_in, k_in, v_in, short_filt, long_filt, norm_gain, grad_out):
    block_len = q_in.shape[1]
    channels = q_in.shape[2]
    edge_rows = FILT - 1
    modulus = 2 * lax.axis_size("context") * block_len
    branches = jnp.stack([q_in[0], k_in[0], v_in[0]])
    before = passed_along(branches[:, block_len - edge_rows :], "context", 1)
    inputs = jnp.concatenate([before, branches], 1).astype(jnp.float32)
    shorts = jnp.zeros((3, block_len, channels), jnp.float32)
    for lag in range(FILT):
        shorts = (
            shorts
            + short_filt[:, lag][:, None, :]
            * inputs[:, edge_rows - lag : edge_rows - lag + block_len]
        )
    q_short = shorts[0]
    k_short = shorts[1]
    v_short = shorts[2]
    kv_prod = k_short * v_short
    spectra = forward_rows(jnp.stack([kv_prod, long_filt]), modulus)
    kv_real, kv_imag = (spectra[0, 0], spectra[0, 1])
    filt_real, filt_imag = (spectra[1, 0], spectra[1, 1])
    conv_spec = jnp.stack(
        [kv_real * filt_real - kv_imag * filt_imag, kv_real * filt_imag + kv_imag * filt_real]
    )[None]
    conv = inverse_rows(conv_spec, modulus)[0]
    y_out = q_short * conv
    squares = lax.psum(jnp.sum(y_out * y_out, axis=-1), "tensor")
    rms = jnp.sqrt(squares / D + EPS)[:, None]
    mixed = (y_out / rms * norm_gain).astype(jnp.bfloat16)[None]
    grad_z = grad_out[0].astype(jnp.float32) * norm_gain
    prods = lax.psum(jnp.sum(grad_z * y_out, axis=-1), "tensor")[:, None]
    grad_y = grad_z / rms - y_out * prods / (D * rms**3)
    dconv = grad_y * q_short
    grad_q = grad_y * conv
    grad_spec = forward_rows(dconv[None], modulus)[0]
    grad_real = grad_spec[0]
    grad_imag = grad_spec[1]
    dkv_spec = jnp.stack(
        [
            filt_real * grad_real + filt_imag * grad_imag,
            filt_real * grad_imag - filt_imag * grad_real,
        ]
    )
    dfilt_spec = jnp.stack(
        [kv_real * grad_real + kv_imag * grad_imag, kv_real * grad_imag - kv_imag * grad_real]
    )
    results = inverse_rows(jnp.stack([dkv_spec, dfilt_spec]), modulus)
    dkv = results[0]
    dfilt_local = results[1]
    grads = jnp.stack([grad_q, dkv * v_short, dkv * k_short])
    after = passed_along(grads[:, :edge_rows].astype(jnp.bfloat16), "context", -1).astype(
        jnp.float32
    )
    extended = jnp.concatenate([grads, after], 1)
    grad_inputs = jnp.zeros((3, block_len, channels), jnp.float32)
    for lag in range(FILT):
        grad_inputs = (
            grad_inputs + short_filt[:, lag][:, None, :] * extended[:, lag : lag + block_len]
        )
    short_local = jnp.stack(
        [
            jnp.sum(grads * inputs[:, edge_rows - lag : edge_rows - lag + block_len], axis=1)
            for lag in range(FILT)
        ],
        1,
    )
    scale = 1.0 / math.sqrt(lax.axis_size("dp") * block_len * lax.axis_size("context"))
    grad_long = lax.psum(dfilt_local, "dp") * scale
    grad_short = lax.psum(short_local, ("dp", "context")) * scale
    return (mixed, grad_inputs.astype(jnp.bfloat16)[:, None], grad_long, grad_short)

MESH = pl.DeviceIdType.MESH
F32 = jnp.float32
BF16 = jnp.bfloat16
PAD = 16
ROWS = 32


def split_table(table):
    high = table.astype(jnp.bfloat16)
    low = (table - high.astype(np.float64)).astype(jnp.bfloat16)
    return high, low


def odd_tables(seq):
    freq = 2 * np.arange(seq)[:, None] + 1
    angle = (freq * np.arange(seq)[None, :] % (4 * seq)) * (np.pi / (2 * seq))
    groups = (seq // 128, 1, 128, seq)
    forward = np.concatenate([np.cos(angle).reshape(groups), -np.sin(angle).reshape(groups)], 1)
    forward = forward.reshape(2 * seq, seq)
    return split_table(forward) + split_table(np.ascontiguousarray(forward.T) / seq)


def halves(values):
    high = values.astype(BF16)
    return high, (values - high.astype(F32)).astype(BF16)


def dot(a, b):
    return jnp.dot(a, b, preferred_element_type=F32)


def dot3(ah, al, bh, bl):
    return dot(ah, bh) + (dot(ah, bl) + dot(al, bh))


def operator_kernel(
    model_width,
    total_rows,
    q_in,
    k_in,
    v_in,
    g_in,
    f_in,
    short_in,
    gains_in,
    wh_in,
    wl_in,
    vh_in,
    vl_in,
    mixed,
    grad_inputs,
    grad_long,
    grad_short,
    staged,
    f_staged,
    branch,
    filt,
    wh,
    wl,
    vh,
    vl,
    short_filt,
    gain_in,
    shorts,
    op_h,
    op_l,
    spec_kv,
    spec_f,
    prod_h,
    prod_l,
    conv,
    y_buf,
    sums,
    stats,
    grads,
    dfilt,
    dfilt_in,
    dfilt_sum,
    long_buf,
    short_sum,
    sent,
    in_send,
    in_recv,
    in_local,
    stage_sem,
    hop_send,
    hop_recv,
    tab_sem,
    st_send,
    st_recv,
    out_send,
    out_recv,
    out_local,
    df_send,
    df_recv,
    gl_send,
    gl_recv,
    gl_local,
    fw_send,
    fw_recv,
    sh_send,
    sh_recv,
    gs_send,
    gs_recv,
    gs_local,
):
    ctx = lax.axis_size("context")
    tens = lax.axis_size("tensor")
    dp = lax.axis_index("dp")
    me = lax.axis_index("context")
    row = lax.axis_index("tensor")
    block = q_in.shape[0]
    seq = block * ctx
    width = branch.shape[2]
    half = width // 2
    taps = short_filt.shape[1]
    other = {"dp": 1 - dp}

    def peer(off):
        return lax.rem(me + off, ctx)

    def source(off):
        return lax.rem(me + ctx - off, ctx)

    def rows_of(p):
        return pl.ds(pl.multiple_of(p * block, block), block)

    def cols_of(p):
        return pl.ds(pl.multiple_of(p * width, width), width)

    def half_cols(p, h):
        return pl.ds(pl.multiple_of(p * width + h * half, half), half)

    def remote(src, dst, send, recv, device):
        copy = pltpu.make_async_remote_copy(
            src_ref=src, dst_ref=dst, send_sem=send, recv_sem=recv, device_id=device, device_id_type=MESH
        )
        copy.start()
        return copy

    def local(src, dst, sem):
        copy = pltpu.make_async_copy(src, dst, sem)
        copy.start()
        return copy

    f_load = local(f_in, f_staged, stage_sem.at[4])
    loads = {n: local(ref, staged.at[n], stage_sem.at[n]) for n, ref in ((1, k_in), (2, v_in), (0, q_in), (3, g_in))}

    barrier = pltpu.get_barrier_semaphore()
    near = [(a, b) for a in range(tens) for b in range(ctx) if a + b > 0]
    for a, b in near:
        pl.semaphore_signal(
            barrier,
            inc=1,
            device_id={"tensor": lax.rem(row + a, tens), "context": peer(b)},
            device_id_type=MESH,
        )
    pl.semaphore_signal(barrier, inc=1, device_id=other, device_id_type=MESH)
    pl.semaphore_wait(barrier, len(near) + 1)

    f_load.wait()
    f_copies = [
        remote(
            f_staged.at[:, half_cols(peer(off), dp)],
            filt.at[dp, rows_of(me), :],
            in_send.at[4, off],
            in_recv.at[4, off],
            {"context": peer(off)},
        )
        for off in range(1, ctx)
    ]
    f_own = local(f_staged.at[:, half_cols(me, dp)], filt.at[dp, rows_of(me), :], in_local.at[4])
    land = pl.ds(pl.multiple_of(PAD + me * block, PAD), block)
    arrivals = {}

    def fetch(n):
        loads[n].wait()
        ref = staged.at[n]
        arrivals[n] = [
            remote(
                ref.at[:, cols_of(peer(off))],
                branch.at[n, land, :],
                in_send.at[n, off],
                in_recv.at[n, off],
                {"context": peer(off)},
            )
            for off in range(1, ctx)
        ]
        arrivals[n].append(local(ref.at[:, cols_of(me)], branch.at[n, land, :], in_local.at[n]))

    fetch(1)
    small = [local(short_in, short_filt, tab_sem.at[4]), local(gains_in, gain_in, tab_sem.at[5])]
    tables = [
        local(src, dst, tab_sem.at[n])
        for n, (src, dst) in enumerate([(wh_in, wh), (wl_in, wl), (vh_in, vh), (vl_in, vl)])
    ]

    def arrived(n):
        for copy in arrivals[n][:-1]:
            copy.wait_recv()
        arrivals[n][-1].wait()

    branch[:, :PAD, :] = jnp.zeros((4, PAD, width), BF16)
    grads[:, seq:, :] = jnp.zeros((3, 8, width), F32)

    for copy in small:
        copy.wait()

    def taps_of(n):
        return [short_filt[n, j : j + 1, cols_of(me)] for j in range(taps)]

    gain = gain_in[:, cols_of(me)]

    def at(i, rows=ROWS):
        return pl.ds(pl.multiple_of(i * rows, rows), rows)

    def short_conv(n, i, weights):
        piece = branch[n, pl.ds(pl.multiple_of(i * ROWS, ROWS), ROWS + PAD), :].astype(F32)
        total = weights[0] * piece[PAD : PAD + ROWS]
        for j in range(1, taps):
            total = total + weights[j] * piece[PAD - j : PAD - j + ROWS]
        return total

    def forward(use):
        @pl.loop(0, 2 * seq // 256, unroll=True)
        def _(m):
            rows = at(m, 256)
            use(rows, dot3(wh[rows, :], wl[rows, :], op_h[...], op_l[...]))

    def inverse(n, store):
        @pl.loop(0, seq // 256, unroll=True)
        def _(m):
            rows = at(m, 256)
            store(rows, dot3(vh[rows, :], vl[rows, :], prod_h[n], prod_l[n]))

    def multiply(n, rows, left, right, sign):
        a, b = left[:128], left[128:] * sign
        c, d = right[:128], right[128:]
        prod = jnp.concatenate([a * c - b * d, a * d + b * c], 0)
        prod_h[n, rows, :], prod_l[n, rows, :] = halves(prod)

    for copy in f_copies:
        copy.wait_recv()
    f_own.wait()
    f_hop = remote(filt.at[dp], filt.at[dp], hop_send, hop_recv, other)
    fetch(2)

    arrived(1)
    fetch(0)
    k_taps = taps_of(1)

    @pl.loop(0, seq // ROWS, unroll=2)
    def _(i):
        shorts[1, at(i), :] = short_conv(1, i, k_taps)

    arrived(2)
    fetch(3)
    v_taps = taps_of(2)

    @pl.loop(0, seq // ROWS, unroll=2)
    def _(i):
        vs = short_conv(2, i, v_taps)
        shorts[2, at(i), :] = vs
        op_h[at(i), :], op_l[at(i), :] = halves(shorts[1, at(i), :] * vs)

    for copy in tables:
        copy.wait()

    def keep_kv(rows, values):
        spec_kv[rows, :] = values

    forward(keep_kv)

    f_hop.wait_recv()

    @pl.loop(0, seq // ROWS, unroll=2)
    def _(i):
        op_h[at(i), :half], op_l[at(i), :half] = halves(filt[0, at(i), :])
        op_h[at(i), half:], op_l[at(i), half:] = halves(filt[1, at(i), :])

    def keep_f(rows, values):
        spec_f[rows, :] = values
        multiply(0, rows, spec_kv[rows, :], values, 1.0)

    forward(keep_f)

    def store_conv(rows, values):
        conv[rows, :] = values

    inverse(0, store_conv)

    arrived(0)
    q_taps = taps_of(0)

    def folded(values):
        total = values[:, :128]
        for n in range(1, width // 128):
            total = total + values[:, n * 128 : (n + 1) * 128]
        return total

    @pl.loop(0, seq // ROWS, unroll=2)
    def _(i):
        qs = short_conv(0, i, q_taps)
        shorts[0, at(i), :] = qs
        y = qs * conv[at(i), :]
        y_buf[at(i), :] = y
        sums[0, at(i), :] = folded(y * y)

    groups = seq // 128
    lane = lax.broadcasted_iota(jnp.int32, (128, 128), 1)

    def share(n):
        columns = jnp.zeros((128, 128), F32)
        for b in range(groups):
            part = jnp.sum(sums[n, b * 128 : (b + 1) * 128, :], axis=1, keepdims=True)
            columns = jnp.where(lane == b, part, columns)
        stats[n, 0] = columns.T[:8]
        return [
            remote(
                stats.at[n, 0],
                stats.at[n, a * ctx + b],
                st_send.at[n, a * ctx + b],
                st_recv.at[n, a * ctx + b],
                {"tensor": lax.rem(row + a, tens), "context": peer(b)},
            )
            for a, b in near
        ]

    def gathered(n, copies):
        for copy in copies:
            copy.wait_recv()
        total = stats[n, 0]
        for r in range(1, tens * ctx):
            total = total + stats[n, r]
        return total

    def widen(n, values):
        spread = jnp.concatenate([values, jnp.zeros((120, 128), F32)], 0).T
        for b in range(groups):
            sums[n, b * 128 : (b + 1) * 128, :] = jnp.broadcast_to(spread[:, b : b + 1], (128, 128))

    st_copies = share(0)
    arrived(3)

    @pl.loop(0, seq // ROWS, unroll=2)
    def _(i):
        gz = branch[3, pl.ds(pl.multiple_of(PAD + i * ROWS, PAD), ROWS), :].astype(F32) * gain
        sums[1, at(i), :] = folded(gz * y_buf[at(i), :])

    prod_copies = share(1)
    inv = 1.0 / jnp.sqrt(gathered(0, st_copies) / model_width + EPS)
    widen(0, inv)

    def wide(n, i):
        return jnp.concatenate([sums[n, at(i), :]] * (width // 128), 1)

    @pl.loop(0, seq // ROWS, unroll=2)
    def _(i):
        sent[3, at(i), :] = (y_buf[at(i), :] * wide(0, i) * gain).astype(BF16)

    def send_back(n, target):
        copies = [
            remote(
                sent.at[n, rows_of(peer(off)), :],
                target,
                out_send.at[n, off],
                out_recv.at[n, off],
                {"context": peer(off)},
            )
            for off in range(1, ctx)
        ]
        return copies, local(sent.at[n, rows_of(me), :], target, out_local.at[n])

    back = [send_back(3, mixed.at[0, :, cols_of(me)])]
    widen(1, gathered(1, prod_copies) * (inv * inv * inv / model_width))

    @pl.loop(0, seq // ROWS, unroll=2)
    def _(i):
        gz = branch[3, pl.ds(pl.multiple_of(PAD + i * ROWS, PAD), ROWS), :].astype(F32) * gain
        dy = gz * wide(0, i) - y_buf[at(i), :] * wide(1, i)
        op_h[at(i), :], op_l[at(i), :] = halves(dy * shorts[0, at(i), :])
        grads[0, at(i), :] = dy * conv[at(i), :]

    scale = 1.0 / math.sqrt(total_rows)

    def back_short(n):
        weights = taps_of(n)

        @pl.loop(0, seq // ROWS, unroll=2)
        def _(i):
            piece = grads[n, pl.ds(pl.multiple_of(i * ROWS, ROWS), ROWS + 8), :]
            total = weights[0] * piece[:ROWS]
            for j in range(1, taps):
                total = total + weights[j] * piece[j : j + ROWS]
            sent[n, at(i), :] = total.astype(BF16)

        back.append(send_back(n, grad_inputs.at[n, 0, :, cols_of(me)]))

    def short_grads(n):
        def body(i, acc):
            own = grads[n, at(i), :]
            inputs = branch[n, pl.ds(pl.multiple_of(i * ROWS, ROWS), ROWS + PAD), :].astype(F32)
            out = []
            for j in range(taps):
                prod = own * inputs[PAD - j : PAD - j + ROWS]
                part = acc[j]
                for r in range(ROWS // 8):
                    part = part + prod[r * 8 : (r + 1) * 8]
                out.append(part)
            return tuple(out)

        acc = lax.fori_loop(0, seq // ROWS, body, tuple(jnp.zeros((8, width), F32) for _ in range(taps)))
        for j in range(taps):
            short_sum[0, n, j : j + 1, :] = jnp.sum(acc[j], axis=0, keepdims=True) * scale

    back_short(0)

    def use_g(rows, values):
        multiply(0, rows, spec_kv[rows, :], values, -1.0)
        multiply(1, rows, spec_f[rows, :], values, -1.0)

    forward(use_g)

    def store_dfilt(rows, values):
        dfilt[0, rows, :] = values[:, :half] * scale
        dfilt[1, rows, :] = values[:, half:] * scale

    inverse(0, store_dfilt)
    df_copy = remote(dfilt.at[1 - dp], dfilt_in, df_send, df_recv, other)

    def store_dkv(rows, values):
        grads[1, rows, :] = values * shorts[2, rows, :]
        grads[2, rows, :] = values * shorts[1, rows, :]

    inverse(1, store_dkv)
    back_short(1)
    df_copy.wait_recv()
    dfilt_sum[...] = (dfilt[dp] + dfilt_in[...]).astype(BF16)
    gl_target = grad_long.at[:, half_cols(me, dp)]
    gl_copies = [
        remote(
            dfilt_sum.at[rows_of(peer(off)), :],
            long_buf.at[off],
            gl_send.at[off],
            gl_recv.at[off],
            {"context": peer(off)},
        )
        for off in range(1, ctx)
    ]
    gl_own = [local(dfilt_sum.at[rows_of(me), :], gl_target, gl_local.at[0])]
    forwards = [remote(dfilt_sum.at[rows_of(me), :], gl_target, fw_send.at[0], fw_recv.at[0], other)]

    back_short(2)

    for n in range(3):
        short_grads(n)
    sh_copy = remote(short_sum.at[0], short_sum.at[1], sh_send, sh_recv, other)

    for off in range(1, ctx):
        gl_copies[off - 1].wait_recv()
        piece = grad_long.at[:, half_cols(source(off), dp)]
        forwards.append(remote(long_buf.at[off], piece, fw_send.at[off], fw_recv.at[off], other))
        gl_own.append(local(long_buf.at[off], piece, gl_local.at[off]))
    sh_copy.wait_recv()
    short_sum[2] = short_sum[0] + short_sum[1]
    gs_target = grad_short.at[:, :, cols_of(me)]
    gs_copies = [
        remote(short_sum.at[2], gs_target, gs_send.at[off], gs_recv.at[off], {"context": peer(off)})
        for off in range(1, ctx)
    ]
    gs_own = local(short_sum.at[2], gs_target, gs_local)
    for copies, own in back:
        own.wait()
        for copy in copies:
            copy.wait()
    for copy in gl_own:
        copy.wait()
    for copy in gl_copies:
        copy.wait_send()
    for copy in forwards:
        copy.wait()
    gs_own.wait()
    for copy in gs_copies:
        copy.wait()
    sh_copy.wait_send()
    df_copy.wait_send()
    f_hop.wait_send()
    for copy in f_copies + st_copies + prod_copies:
        copy.wait_send()
    for n in range(4):
        for copy in arrivals[n][:-1]:
            copy.wait_send()


def deliver_kernel(
    mixed, grad_inputs, grad_long, grad_short, mixed_out, inputs_out, long_out, short_out, held, narrow, wide, short, sem
):
    def move(n, src, dst):
        copy = pltpu.make_async_copy(src, dst, sem.at[n])
        copy.start()
        return copy

    loads = [move(0, grad_long, narrow), move(1, mixed.at[0], held.at[0])]
    loads += [move(2 + n, grad_inputs.at[n, 0], held.at[1 + n]) for n in range(3)]
    loads.append(move(5, grad_short, short))
    loads[0].wait()
    wide[...] = narrow[...].astype(F32)
    stores = [move(6, wide, long_out)]
    targets = [mixed_out.at[0]] + [inputs_out.at[n, 0] for n in range(3)]
    for n in range(4):
        loads[1 + n].wait()
        stores.append(move(7 + n, held.at[n], targets[n]))
    loads[5].wait()
    stores.append(move(11, short, short_out))
    for copy in stores:
        copy.wait()


def fused(q_in, k_in, v_in, short_filt, long_filt, norm_gain, grad_out):
    _, block, channels = q_in.shape
    ctx = lax.axis_size("context")
    tens = lax.axis_size("tensor")
    seq = block * ctx
    width = channels // ctx
    tables = [jnp.asarray(t) for t in odd_tables(seq)]
    dma = pltpu.SemaphoreType.DMA
    anywhere = pl.BlockSpec(memory_space=pl.ANY)
    in_hbm = pl.BlockSpec(memory_space=pltpu.HBM)
    outs = pl.pallas_call(
        functools.partial(operator_kernel, D, lax.axis_size("dp") * seq),
        out_shape=(
            jax.ShapeDtypeStruct((1, block, channels), BF16),
            jax.ShapeDtypeStruct((3, 1, block, channels), BF16),
            jax.ShapeDtypeStruct((block, channels), BF16),
            jax.ShapeDtypeStruct(short_filt.shape, F32),
        ),
        in_specs=[in_hbm] * 11,
        out_specs=(anywhere,) * 4,
        scratch_shapes=[
            pltpu.VMEM((4, block, channels), BF16),
            pltpu.VMEM((block, channels), F32),
            pltpu.VMEM((4, PAD + seq, width), BF16),
            pltpu.VMEM((2, seq, width // 2), F32),
            pltpu.VMEM((2 * seq, seq), BF16),
            pltpu.VMEM((2 * seq, seq), BF16),
            pltpu.VMEM((seq, 2 * seq), BF16),
            pltpu.VMEM((seq, 2 * seq), BF16),
            pltpu.VMEM(short_filt.shape, F32),
            pltpu.VMEM((1, channels), F32),
            pltpu.VMEM((3, seq, width), F32),
            pltpu.VMEM((seq, width), BF16),
            pltpu.VMEM((seq, width), BF16),
            pltpu.VMEM((2 * seq, width), F32),
            pltpu.VMEM((2 * seq, width), F32),
            pltpu.VMEM((2, 2 * seq, width), BF16),
            pltpu.VMEM((2, 2 * seq, width), BF16),
            pltpu.VMEM((seq, width), F32),
            pltpu.VMEM((seq, width), F32),
            pltpu.VMEM((2, seq, 128), F32),
            pltpu.VMEM((2, tens * ctx, 8, 128), F32),
            pltpu.VMEM((3, seq + 8, width), F32),
            pltpu.VMEM((2, seq, width // 2), F32),
            pltpu.VMEM((seq, width // 2), F32),
            pltpu.VMEM((seq, width // 2), BF16),
            pltpu.VMEM((ctx, block, width // 2), BF16),
            pltpu.VMEM((3, 3, short_filt.shape[1], width), F32),
            pltpu.VMEM((4, seq, width), BF16),
            dma((5, ctx)),
            dma((5, ctx)),
            dma((5,)),
            dma((5,)),
            dma,
            dma,
            dma((6,)),
            dma((2, tens * ctx)),
            dma((2, tens * ctx)),
            dma((4, ctx)),
            dma((4, ctx)),
            dma((4,)),
            dma,
            dma,
            dma((ctx,)),
            dma((ctx,)),
            dma((ctx,)),
            dma((ctx,)),
            dma((ctx,)),
            dma,
            dma,
            dma((ctx,)),
            dma((ctx,)),
            dma,
        ],
        compiler_params=pltpu.CompilerParams(
            collective_id=0, has_side_effects=True, vmem_limit_bytes=60 * 2**20
        ),
    )(
        q_in[0],
        k_in[0],
        v_in[0],
        grad_out[0],
        long_filt,
        short_filt,
        norm_gain[None],
        *tables,
    )
    return pl.pallas_call(
        deliver_kernel,
        out_shape=(
            jax.ShapeDtypeStruct((1, block, channels), BF16),
            jax.ShapeDtypeStruct((3, 1, block, channels), BF16),
            jax.ShapeDtypeStruct((block, channels), F32),
            jax.ShapeDtypeStruct(short_filt.shape, F32),
        ),
        in_specs=[anywhere] * 4,
        out_specs=(anywhere,) * 4,
        scratch_shapes=[
            pltpu.VMEM((4, block, channels), BF16),
            pltpu.VMEM((block, channels), BF16),
            pltpu.VMEM((block, channels), F32),
            pltpu.VMEM(short_filt.shape, F32),
            dma((12,)),
        ],
        compiler_params=pltpu.CompilerParams(vmem_limit_bytes=60 * 2**20),
    )(*outs)


def operator(q_in, k_in, v_in, short_filt, long_filt, norm_gain, grad_out):
    _, block, channels = q_in.shape
    ctx = lax.axis_size("context")
    dense = block * ctx <= 1024 and block % 128 == 0 and channels % (256 * ctx) == 0
    form = fused if dense and lax.axis_size("dp") == 2 else shards
    return form(q_in, k_in, v_in, short_filt, long_filt, norm_gain, grad_out)


def solution(mesh):
    in_specs = (
        P("dp", "context", "tensor"),
        P("dp", "context", "tensor"),
        P("dp", "context", "tensor"),
        P(None, None, "tensor"),
        P("context", "tensor"),
        P("tensor"),
        P("dp", "context", "tensor"),
    )
    out_specs = (
        P("dp", "context", "tensor"),
        P(None, "dp", "context", "tensor"),
        P("context", "tensor"),
        P(None, None, "tensor"),
    )
    return jax.shard_map(operator, mesh=mesh, in_specs=in_specs, out_specs=out_specs, check_vma=False)
```

```python
import functools
import math

import jax
import jax.numpy as jnp
import numpy as np
from jax import lax
from jax.experimental import pallas as pl
from jax.experimental.pallas import tpu as pltpu
from jax.sharding import PartitionSpec as P

D = 4096
FILT = 7


EPS = 1e-06
HIGH = lax.Precision.HIGHEST


def passed_along(shard, axis, by):
    peers = lax.axis_size(axis)
    pairs = [(i, i + by) for i in range(peers) if 0 <= i + by < peers]
    return lax.ppermute(shard, axis, pairs)


def phases(first, second, modulus):
    product = first[:, None] * second[None, :] % modulus
    return product.astype(jnp.float32) * (2.0 * math.pi / modulus)


def block_table(block_len, sign):
    index = jnp.arange(block_len, dtype=jnp.int32)
    angle = phases(index, index, block_len)
    cosine = jnp.cos(angle)
    sine = jnp.sin(angle) * sign
    return jnp.stack([jnp.stack([cosine, sine]), jnp.stack([-sine, cosine])])


def forward_rows(values, modulus):
    count, block_len, width = values.shape
    ctx_size = lax.axis_size("context")
    sub_len = block_len // ctx_size
    spread = lax.all_to_all(
        values.reshape(count, 1, block_len, width),
        "context",
        split_axis=2,
        concat_axis=1,
        tiled=True,
    )
    freq = jnp.arange(2 * ctx_size, dtype=jnp.int32)
    place = (
        jnp.arange(ctx_size, dtype=jnp.int32)[:, None] * block_len
        + lax.axis_index("context") * sub_len
        + jnp.arange(sub_len, dtype=jnp.int32)[None, :]
    )
    angle = (freq[:, None, None] * place[None] % modulus).astype(jnp.float32) * (
        2.0 * math.pi / modulus
    )
    table = jnp.stack([jnp.cos(angle), -jnp.sin(angle)])
    turned = jnp.einsum("pkcs,ncsx->npksx", table, spread, precision=HIGH)
    moved = lax.all_to_all(turned, "context", split_axis=2, concat_axis=3, tiled=True)
    return jnp.einsum("pqmb,nqjbx->npjmx", block_table(block_len, 1.0), moved, precision=HIGH)


def inverse_rows(spec, modulus):
    rows = spec.shape[2]
    block_len = spec.shape[3]
    ctx_size = lax.axis_size("context")
    index = jnp.arange(block_len, dtype=jnp.int32)
    freq = 2 * lax.axis_index("context") + jnp.arange(rows, dtype=jnp.int32)
    total = freq[:, None, None] + 2 * ctx_size * index[None, :, None]
    angle = (total * index[None, None, :] % modulus).astype(jnp.float32) * (2.0 * math.pi / modulus)
    cosine = jnp.cos(angle)
    sine = jnp.sin(angle)
    table = jnp.stack([jnp.stack([cosine, -sine]), jnp.stack([sine, cosine])])
    turned = jnp.einsum("pqjmb,nqjmx->npjbx", table, spec, precision=HIGH)
    moved = lax.all_to_all(turned, "context", split_axis=3, concat_axis=2, tiled=True)
    outer = phases(
        jnp.arange(ctx_size, dtype=jnp.int32),
        jnp.arange(2 * ctx_size, dtype=jnp.int32),
        2 * ctx_size,
    )
    real_table = jnp.stack([jnp.cos(outer), -jnp.sin(outer)])
    values = jnp.einsum("qck,nqksx->ncsx", real_table, moved, precision=HIGH) / modulus
    back = lax.all_to_all(values, "context", split_axis=1, concat_axis=2, tiled=True)
    return back.reshape(back.shape[0], back.shape[2], back.shape[3])


def shards(q_in, k_in, v_in, short_filt, long_filt, norm_gain, grad_out):
    block_len = q_in.shape[1]
    channels = q_in.shape[2]
    edge_rows = FILT - 1
    modulus = 2 * lax.axis_size("context") * block_len
    branches = jnp.stack([q_in[0], k_in[0], v_in[0]])
    before = passed_along(branches[:, block_len - edge_rows :], "context", 1)
    inputs = jnp.concatenate([before, branches], 1).astype(jnp.float32)
    shorts = jnp.zeros((3, block_len, channels), jnp.float32)
    for lag in range(FILT):
        shorts = (
            shorts
            + short_filt[:, lag][:, None, :]
            * inputs[:, edge_rows - lag : edge_rows - lag + block_len]
        )
    q_short = shorts[0]
    k_short = shorts[1]
    v_short = shorts[2]
    kv_prod = k_short * v_short
    spectra = forward_rows(jnp.stack([kv_prod, long_filt]), modulus)
    kv_real, kv_imag = (spectra[0, 0], spectra[0, 1])
    filt_real, filt_imag = (spectra[1, 0], spectra[1, 1])
    conv_spec = jnp.stack(
        [kv_real * filt_real - kv_imag * filt_imag, kv_real * filt_imag + kv_imag * filt_real]
    )[None]
    conv = inverse_rows(conv_spec, modulus)[0]
    y_out = q_short * conv
    squares = lax.psum(jnp.sum(y_out * y_out, axis=-1), "tensor")
    rms = jnp.sqrt(squares / D + EPS)[:, None]
    mixed = (y_out / rms * norm_gain).astype(jnp.bfloat16)[None]
    grad_z = grad_out[0].astype(jnp.float32) * norm_gain
    prods = lax.psum(jnp.sum(grad_z * y_out, axis=-1), "tensor")[:, None]
    grad_y = grad_z / rms - y_out * prods / (D * rms**3)
    dconv = grad_y * q_short
    grad_q = grad_y * conv
    grad_spec = forward_rows(dconv[None], modulus)[0]
    grad_real = grad_spec[0]
    grad_imag = grad_spec[1]
    dkv_spec = jnp.stack(
        [
            filt_real * grad_real + filt_imag * grad_imag,
            filt_real * grad_imag - filt_imag * grad_real,
        ]
    )
    dfilt_spec = jnp.stack(
        [kv_real * grad_real + kv_imag * grad_imag, kv_real * grad_imag - kv_imag * grad_real]
    )
    results = inverse_rows(jnp.stack([dkv_spec, dfilt_spec]), modulus)
    dkv = results[0]
    dfilt_local = results[1]
    grads = jnp.stack([grad_q, dkv * v_short, dkv * k_short])
    after = passed_along(grads[:, :edge_rows].astype(jnp.bfloat16), "context", -1).astype(
        jnp.float32
    )
    extended = jnp.concatenate([grads, after], 1)
    grad_inputs = jnp.zeros((3, block_len, channels), jnp.float32)
    for lag in range(FILT):
        grad_inputs = (
            grad_inputs + short_filt[:, lag][:, None, :] * extended[:, lag : lag + block_len]
        )
    short_local = jnp.stack(
        [
            jnp.sum(grads * inputs[:, edge_rows - lag : edge_rows - lag + block_len], axis=1)
            for lag in range(FILT)
        ],
        1,
    )
    scale = 1.0 / math.sqrt(lax.axis_size("dp") * block_len * lax.axis_size("context"))
    grad_long = lax.psum(dfilt_local, "dp") * scale
    grad_short = lax.psum(short_local, ("dp", "context")) * scale
    return (mixed, grad_inputs.astype(jnp.bfloat16)[:, None], grad_long, grad_short)

MESH = pl.DeviceIdType.MESH
F32 = jnp.float32
BF16 = jnp.bfloat16
PAD = 16
ROWS = 32


def split_table(table):
    high = table.astype(jnp.bfloat16)
    low = (table - high.astype(np.float64)).astype(jnp.bfloat16)
    return high, low


def odd_tables(seq):
    freq = 2 * np.arange(seq)[:, None] + 1
    angle = (freq * np.arange(seq)[None, :] % (4 * seq)) * (np.pi / (2 * seq))
    groups = (seq // 128, 1, 128, seq)
    forward = np.concatenate([np.cos(angle).reshape(groups), -np.sin(angle).reshape(groups)], 1)
    forward = forward.reshape(2 * seq, seq)
    return split_table(forward) + split_table(np.ascontiguousarray(forward.T) / seq)


def halves(values):
    high = values.astype(BF16)
    return high, (values - high.astype(F32)).astype(BF16)


def dot(a, b):
    return jnp.dot(a, b, preferred_element_type=F32)


def dot3(ah, al, bh, bl):
    return dot(ah, bh) + (dot(ah, bl) + dot(al, bh))


def operator_kernel(
    model_width,
    total_rows,
    q_in,
    k_in,
    v_in,
    g_in,
    f_in,
    short_in,
    gains_in,
    wh_in,
    wl_in,
    vh_in,
    vl_in,
    mixed,
    grad_inputs,
    grad_long,
    grad_short,
    staged,
    f_staged,
    branch,
    filt,
    wh,
    wl,
    vh,
    vl,
    short_filt,
    gain_in,
    shorts,
    op_h,
    op_l,
    spec_kv,
    spec_f,
    prod_h,
    prod_l,
    conv,
    y_buf,
    sums,
    stats,
    grads,
    dfilt,
    dfilt_in,
    dfilt_sum,
    long_buf,
    short_sum,
    sent,
    in_send,
    in_recv,
    in_local,
    stage_sem,
    hop_send,
    hop_recv,
    tab_sem,
    st_send,
    st_recv,
    out_send,
    out_recv,
    out_local,
    df_send,
    df_recv,
    gl_send,
    gl_recv,
    gl_local,
    fw_send,
    fw_recv,
    sh_send,
    sh_recv,
    gs_send,
    gs_recv,
    gs_local,
):
    ctx = lax.axis_size("context")
    tens = lax.axis_size("tensor")
    dp = lax.axis_index("dp")
    me = lax.axis_index("context")
    row = lax.axis_index("tensor")
    block = q_in.shape[0]
    seq = block * ctx
    width = branch.shape[2]
    half = width // 2
    taps = short_filt.shape[1]
    other = {"dp": 1 - dp}

    steps = (2, 3, 1)

    def peer(step):
        if step == 1:
            return me + 1 - 2 * (me % 2)
        if step == 2:
            return lax.rem(me + 2, ctx)
        return 3 - me if step == 3 else me

    source = peer

    def rows_of(p):
        return pl.ds(pl.multiple_of(p * block, block), block)

    def cols_of(p):
        return pl.ds(pl.multiple_of(p * width, width), width)

    def half_cols(p, h):
        return pl.ds(pl.multiple_of(p * width + h * half, half), half)

    def remote(src, dst, send, recv, device):
        copy = pltpu.make_async_remote_copy(
            src_ref=src, dst_ref=dst, send_sem=send, recv_sem=recv, device_id=device, device_id_type=MESH
        )
        copy.start()
        return copy

    def local(src, dst, sem):
        copy = pltpu.make_async_copy(src, dst, sem)
        copy.start()
        return copy

    f_load = local(f_in, f_staged, stage_sem.at[4])
    loads = {n: local(ref, staged.at[n], stage_sem.at[n]) for n, ref in ((1, k_in), (2, v_in), (0, q_in), (3, g_in))}

    barrier = pltpu.get_barrier_semaphore()
    near = [(a, b) for a in range(tens) for b in range(ctx) if a + b > 0]
    for a, b in near:
        pl.semaphore_signal(
            barrier,
            inc=1,
            device_id={"tensor": lax.rem(row + a, tens), "context": peer(b)},
            device_id_type=MESH,
        )
    pl.semaphore_signal(barrier, inc=1, device_id=other, device_id_type=MESH)
    pl.semaphore_wait(barrier, len(near) + 1)

    f_load.wait()
    f_copies = [
        remote(
            f_staged.at[:, half_cols(peer(off), dp)],
            filt.at[dp, rows_of(me), :],
            in_send.at[4, off],
            in_recv.at[4, off],
            {"context": peer(off)},
        )
        for off in steps
    ]
    f_own = local(f_staged.at[:, half_cols(me, dp)], filt.at[dp, rows_of(me), :], in_local.at[4])
    land = pl.ds(pl.multiple_of(PAD + me * block, PAD), block)
    arrivals = {}

    def fetch(n):
        loads[n].wait()
        ref = staged.at[n]
        arrivals[n] = [
            remote(
                ref.at[:, cols_of(peer(off))],
                branch.at[n, land, :],
                in_send.at[n, off],
                in_recv.at[n, off],
                {"context": peer(off)},
            )
            for off in steps
        ]
        arrivals[n].append(local(ref.at[:, cols_of(me)], branch.at[n, land, :], in_local.at[n]))

    fetch(1)
    fetch(2)
    small = [local(short_in, short_filt, tab_sem.at[4]), local(gains_in, gain_in, tab_sem.at[5])]
    tables = [
        local(src, dst, tab_sem.at[n])
        for n, (src, dst) in enumerate([(wh_in, wh), (wl_in, wl), (vh_in, vh), (vl_in, vl)])
    ]

    def arrived(n):
        for copy in arrivals[n][:-1]:
            copy.wait_recv()
        arrivals[n][-1].wait()

    branch[:, :PAD, :] = jnp.zeros((4, PAD, width), BF16)
    grads[:, seq:, :] = jnp.zeros((3, 8, width), F32)

    for copy in small:
        copy.wait()

    def taps_of(n):
        return [short_filt[n, j : j + 1, cols_of(me)] for j in range(taps)]

    gain = gain_in[:, cols_of(me)]

    def at(i, rows=ROWS):
        return pl.ds(pl.multiple_of(i * rows, rows), rows)

    def short_conv(n, i, weights):
        piece = branch[n, pl.ds(pl.multiple_of(i * ROWS, ROWS), ROWS + PAD), :].astype(F32)
        total = weights[0] * piece[PAD : PAD + ROWS]
        for j in range(1, taps):
            total = total + weights[j] * piece[PAD - j : PAD - j + ROWS]
        return total

    def forward(use):
        @pl.loop(0, 2 * seq // 256, unroll=True)
        def _(m):
            rows = at(m, 256)
            use(rows, dot3(wh[rows, :], wl[rows, :], op_h[...], op_l[...]))

    def inverse(n, store):
        @pl.loop(0, seq // 256, unroll=True)
        def _(m):
            rows = at(m, 256)
            store(rows, dot3(vh[rows, :], vl[rows, :], prod_h[n], prod_l[n]))

    def multiply(n, rows, left, right, sign):
        a, b = left[:128], left[128:] * sign
        c, d = right[:128], right[128:]
        prod = jnp.concatenate([a * c - b * d, a * d + b * c], 0)
        prod_h[n, rows, :], prod_l[n, rows, :] = halves(prod)

    for copy in f_copies:
        copy.wait_recv()
    f_own.wait()
    f_hop = remote(filt.at[dp], filt.at[dp], hop_send, hop_recv, other)
    fetch(0)

    arrived(1)
    fetch(3)
    k_taps = taps_of(1)

    @pl.loop(0, seq // ROWS, unroll=2)
    def _(i):
        shorts[1, at(i), :] = short_conv(1, i, k_taps)

    arrived(2)
    v_taps = taps_of(2)

    @pl.loop(0, seq // ROWS, unroll=2)
    def _(i):
        vs = short_conv(2, i, v_taps)
        shorts[2, at(i), :] = vs
        op_h[at(i), :], op_l[at(i), :] = halves(shorts[1, at(i), :] * vs)

    for copy in tables:
        copy.wait()

    def keep_kv(rows, values):
        spec_kv[rows, :] = values

    forward(keep_kv)

    f_hop.wait_recv()

    @pl.loop(0, seq // ROWS, unroll=2)
    def _(i):
        op_h[at(i), :half], op_l[at(i), :half] = halves(filt[0, at(i), :])
        op_h[at(i), half:], op_l[at(i), half:] = halves(filt[1, at(i), :])

    def keep_f(rows, values):
        spec_f[rows, :] = values
        multiply(0, rows, spec_kv[rows, :], values, 1.0)

    forward(keep_f)

    def store_conv(rows, values):
        conv[rows, :] = values

    inverse(0, store_conv)

    arrived(0)
    q_taps = taps_of(0)

    def folded(values):
        total = values[:, :128]
        for n in range(1, width // 128):
            total = total + values[:, n * 128 : (n + 1) * 128]
        return total

    @pl.loop(0, seq // ROWS, unroll=2)
    def _(i):
        qs = short_conv(0, i, q_taps)
        shorts[0, at(i), :] = qs
        y = qs * conv[at(i), :]
        y_buf[at(i), :] = y
        sums[0, at(i), :] = folded(y * y)

    groups = seq // 128
    lane = lax.broadcasted_iota(jnp.int32, (128, 128), 1)

    def share(n):
        columns = jnp.zeros((128, 128), F32)
        for b in range(groups):
            part = jnp.sum(sums[n, b * 128 : (b + 1) * 128, :], axis=1, keepdims=True)
            columns = jnp.where(lane == b, part, columns)
        stats[n, 0] = columns.T[:8]
        return [
            remote(
                stats.at[n, 0],
                stats.at[n, a * ctx + b],
                st_send.at[n, a * ctx + b],
                st_recv.at[n, a * ctx + b],
                {"tensor": lax.rem(row + a, tens), "context": peer(b)},
            )
            for a, b in near
        ]

    def gathered(n, copies):
        for copy in copies:
            copy.wait_recv()
        total = stats[n, 0]
        for r in range(1, tens * ctx):
            total = total + stats[n, r]
        return total

    def widen(n, values):
        spread = jnp.concatenate([values, jnp.zeros((120, 128), F32)], 0).T
        for b in range(groups):
            sums[n, b * 128 : (b + 1) * 128, :] = jnp.broadcast_to(spread[:, b : b + 1], (128, 128))

    st_copies = share(0)
    arrived(3)

    @pl.loop(0, seq // ROWS, unroll=2)
    def _(i):
        gz = branch[3, pl.ds(pl.multiple_of(PAD + i * ROWS, PAD), ROWS), :].astype(F32) * gain
        sums[1, at(i), :] = folded(gz * y_buf[at(i), :])

    prod_copies = share(1)
    inv = 1.0 / jnp.sqrt(gathered(0, st_copies) / model_width + EPS)
    widen(0, inv)

    def wide(n, i):
        return jnp.concatenate([sums[n, at(i), :]] * (width // 128), 1)

    @pl.loop(0, seq // ROWS, unroll=2)
    def _(i):
        sent[3, at(i), :] = (y_buf[at(i), :] * wide(0, i) * gain).astype(BF16)

    def send_back(n, target):
        copies = [
            remote(
                sent.at[n, rows_of(peer(off)), :],
                target,
                out_send.at[n, off],
                out_recv.at[n, off],
                {"context": peer(off)},
            )
            for off in steps
        ]
        return copies, local(sent.at[n, rows_of(me), :], target, out_local.at[n])

    back = [send_back(3, mixed.at[0, :, cols_of(me)])]
    widen(1, gathered(1, prod_copies) * (inv * inv * inv / model_width))

    @pl.loop(0, seq // ROWS, unroll=2)
    def _(i):
        gz = branch[3, pl.ds(pl.multiple_of(PAD + i * ROWS, PAD), ROWS), :].astype(F32) * gain
        dy = gz * wide(0, i) - y_buf[at(i), :] * wide(1, i)
        op_h[at(i), :], op_l[at(i), :] = halves(dy * shorts[0, at(i), :])
        grads[0, at(i), :] = dy * conv[at(i), :]

    scale = 1.0 / math.sqrt(total_rows)

    def back_short(n):
        weights = taps_of(n)

        @pl.loop(0, seq // ROWS, unroll=2)
        def _(i):
            piece = grads[n, pl.ds(pl.multiple_of(i * ROWS, ROWS), ROWS + 8), :]
            total = weights[0] * piece[:ROWS]
            for j in range(1, taps):
                total = total + weights[j] * piece[j : j + ROWS]
            sent[n, at(i), :] = total.astype(BF16)

        back.append(send_back(n, grad_inputs.at[n, 0, :, cols_of(me)]))

    def short_grads(n):
        def body(i, acc):
            own = grads[n, at(i), :]
            inputs = branch[n, pl.ds(pl.multiple_of(i * ROWS, ROWS), ROWS + PAD), :].astype(F32)
            out = []
            for j in range(taps):
                prod = own * inputs[PAD - j : PAD - j + ROWS]
                part = acc[j]
                for r in range(ROWS // 8):
                    part = part + prod[r * 8 : (r + 1) * 8]
                out.append(part)
            return tuple(out)

        acc = lax.fori_loop(0, seq // ROWS, body, tuple(jnp.zeros((8, width), F32) for _ in range(taps)))
        for j in range(taps):
            short_sum[0, n, j : j + 1, :] = jnp.sum(acc[j], axis=0, keepdims=True) * scale

    back_short(0)

    def use_g(rows, values):
        multiply(0, rows, spec_kv[rows, :], values, -1.0)
        multiply(1, rows, spec_f[rows, :], values, -1.0)

    forward(use_g)

    def store_dfilt(rows, values):
        dfilt[0, rows, :] = values[:, :half] * scale
        dfilt[1, rows, :] = values[:, half:] * scale

    inverse(0, store_dfilt)
    df_copy = remote(dfilt.at[1 - dp], dfilt_in, df_send, df_recv, other)

    def store_dkv(rows, values):
        grads[1, rows, :] = values * shorts[2, rows, :]
        grads[2, rows, :] = values * shorts[1, rows, :]

    inverse(1, store_dkv)
    back_short(1)
    df_copy.wait_recv()
    dfilt_sum[...] = (dfilt[dp] + dfilt_in[...]).astype(BF16)
    gl_target = grad_long.at[:, half_cols(me, dp)]
    gl_copies = [
        remote(
            dfilt_sum.at[rows_of(peer(off)), :],
            long_buf.at[off],
            gl_send.at[off],
            gl_recv.at[off],
            {"context": peer(off)},
        )
        for off in steps
    ]
    gl_own = [local(dfilt_sum.at[rows_of(me), :], gl_target, gl_local.at[0])]
    forwards = [remote(dfilt_sum.at[rows_of(me), :], gl_target, fw_send.at[0], fw_recv.at[0], other)]

    back_short(2)

    for n in range(3):
        short_grads(n)
    sh_copy = remote(short_sum.at[0], short_sum.at[1], sh_send, sh_recv, other)

    for off in steps:
        gl_copies[steps.index(off)].wait_recv()
        piece = grad_long.at[:, half_cols(source(off), dp)]
        forwards.append(remote(long_buf.at[off], piece, fw_send.at[off], fw_recv.at[off], other))
        gl_own.append(local(long_buf.at[off], piece, gl_local.at[off]))
    sh_copy.wait_recv()
    short_sum[2] = short_sum[0] + short_sum[1]
    gs_target = grad_short.at[:, :, cols_of(me)]
    gs_copies = [
        remote(short_sum.at[2], gs_target, gs_send.at[off], gs_recv.at[off], {"context": peer(off)})
        for off in steps
    ]
    gs_own = local(short_sum.at[2], gs_target, gs_local)
    for copies, own in back:
        own.wait()
        for copy in copies:
            copy.wait()
    for copy in gl_own:
        copy.wait()
    for copy in gl_copies:
        copy.wait_send()
    for copy in forwards:
        copy.wait()
    gs_own.wait()
    for copy in gs_copies:
        copy.wait()
    sh_copy.wait_send()
    df_copy.wait_send()
    f_hop.wait_send()
    for copy in f_copies + st_copies + prod_copies:
        copy.wait_send()
    for n in range(4):
        for copy in arrivals[n][:-1]:
            copy.wait_send()


def deliver_kernel(
    mixed, grad_inputs, grad_long, grad_short, mixed_out, inputs_out, long_out, short_out, held, narrow, wide, short, sem
):
    def move(n, src, dst):
        copy = pltpu.make_async_copy(src, dst, sem.at[n])
        copy.start()
        return copy

    loads = [move(0, grad_long, narrow), move(1, mixed.at[0], held.at[0])]
    loads += [move(2 + n, grad_inputs.at[n, 0], held.at[1 + n]) for n in range(3)]
    loads.append(move(5, grad_short, short))
    loads[0].wait()
    wide[...] = narrow[...].astype(F32)
    stores = [move(6, wide, long_out)]
    targets = [mixed_out.at[0]] + [inputs_out.at[n, 0] for n in range(3)]
    for n in range(4):
        loads[1 + n].wait()
        stores.append(move(7 + n, held.at[n], targets[n]))
    loads[5].wait()
    stores.append(move(11, short, short_out))
    for copy in stores:
        copy.wait()


def fused(q_in, k_in, v_in, short_filt, long_filt, norm_gain, grad_out):
    _, block, channels = q_in.shape
    ctx = lax.axis_size("context")
    tens = lax.axis_size("tensor")
    seq = block * ctx
    width = channels // ctx
    tables = [jnp.asarray(t) for t in odd_tables(seq)]
    dma = pltpu.SemaphoreType.DMA
    anywhere = pl.BlockSpec(memory_space=pl.ANY)
    in_hbm = pl.BlockSpec(memory_space=pltpu.HBM)
    outs = pl.pallas_call(
        functools.partial(operator_kernel, D, lax.axis_size("dp") * seq),
        out_shape=(
            jax.ShapeDtypeStruct((1, block, channels), BF16),
            jax.ShapeDtypeStruct((3, 1, block, channels), BF16),
            jax.ShapeDtypeStruct((block, channels), BF16),
            jax.ShapeDtypeStruct(short_filt.shape, F32),
        ),
        in_specs=[in_hbm] * 11,
        out_specs=(anywhere,) * 4,
        scratch_shapes=[
            pltpu.VMEM((4, block, channels), BF16),
            pltpu.VMEM((block, channels), F32),
            pltpu.VMEM((4, PAD + seq, width), BF16),
            pltpu.VMEM((2, seq, width // 2), F32),
            pltpu.VMEM((2 * seq, seq), BF16),
            pltpu.VMEM((2 * seq, seq), BF16),
            pltpu.VMEM((seq, 2 * seq), BF16),
            pltpu.VMEM((seq, 2 * seq), BF16),
            pltpu.VMEM(short_filt.shape, F32),
            pltpu.VMEM((1, channels), F32),
            pltpu.VMEM((3, seq, width), F32),
            pltpu.VMEM((seq, width), BF16),
            pltpu.VMEM((seq, width), BF16),
            pltpu.VMEM((2 * seq, width), F32),
            pltpu.VMEM((2 * seq, width), F32),
            pltpu.VMEM((2, 2 * seq, width), BF16),
            pltpu.VMEM((2, 2 * seq, width), BF16),
            pltpu.VMEM((seq, width), F32),
            pltpu.VMEM((seq, width), F32),
            pltpu.VMEM((2, seq, 128), F32),
            pltpu.VMEM((2, tens * ctx, 8, 128), F32),
            pltpu.VMEM((3, seq + 8, width), F32),
            pltpu.VMEM((2, seq, width // 2), F32),
            pltpu.VMEM((seq, width // 2), F32),
            pltpu.VMEM((seq, width // 2), BF16),
            pltpu.VMEM((ctx, block, width // 2), BF16),
            pltpu.VMEM((3, 3, short_filt.shape[1], width), F32),
            pltpu.VMEM((4, seq, width), BF16),
            dma((5, ctx)),
            dma((5, ctx)),
            dma((5,)),
            dma((5,)),
            dma,
            dma,
            dma((6,)),
            dma((2, tens * ctx)),
            dma((2, tens * ctx)),
            dma((4, ctx)),
            dma((4, ctx)),
            dma((4,)),
            dma,
            dma,
            dma((ctx,)),
            dma((ctx,)),
            dma((ctx,)),
            dma((ctx,)),
            dma((ctx,)),
            dma,
            dma,
            dma((ctx,)),
            dma((ctx,)),
            dma,
        ],
        compiler_params=pltpu.CompilerParams(
            collective_id=0, has_side_effects=True, vmem_limit_bytes=60 * 2**20
        ),
    )(
        q_in[0],
        k_in[0],
        v_in[0],
        grad_out[0],
        long_filt,
        short_filt,
        norm_gain[None],
        *tables,
    )
    return pl.pallas_call(
        deliver_kernel,
        out_shape=(
            jax.ShapeDtypeStruct((1, block, channels), BF16),
            jax.ShapeDtypeStruct((3, 1, block, channels), BF16),
            jax.ShapeDtypeStruct((block, channels), F32),
            jax.ShapeDtypeStruct(short_filt.shape, F32),
        ),
        in_specs=[anywhere] * 4,
        out_specs=(anywhere,) * 4,
        scratch_shapes=[
            pltpu.VMEM((4, block, channels), BF16),
            pltpu.VMEM((block, channels), BF16),
            pltpu.VMEM((block, channels), F32),
            pltpu.VMEM(short_filt.shape, F32),
            dma((12,)),
        ],
        compiler_params=pltpu.CompilerParams(vmem_limit_bytes=60 * 2**20),
    )(*outs)


def operator(q_in, k_in, v_in, short_filt, long_filt, norm_gain, grad_out):
    _, block, channels = q_in.shape
    ctx = lax.axis_size("context")
    dense = block * ctx <= 1024 and block % 128 == 0 and channels % (256 * ctx) == 0
    form = fused if dense and lax.axis_size("dp") == 2 and ctx == 4 else shards
    return form(q_in, k_in, v_in, short_filt, long_filt, norm_gain, grad_out)


def solution(mesh):
    in_specs = (
        P("dp", "context", "tensor"),
        P("dp", "context", "tensor"),
        P("dp", "context", "tensor"),
        P(None, None, "tensor"),
        P("context", "tensor"),
        P("tensor"),
        P("dp", "context", "tensor"),
    )
    out_specs = (
        P("dp", "context", "tensor"),
        P(None, "dp", "context", "tensor"),
        P("context", "tensor"),
        P(None, None, "tensor"),
    )
    return jax.shard_map(operator, mesh=mesh, in_specs=in_specs, out_specs=out_specs, check_vma=False)
```

```python
import functools
import math

import jax
import jax.numpy as jnp
import numpy as np
from jax import lax
from jax.experimental import pallas as pl
from jax.experimental.pallas import tpu as pltpu
from jax.sharding import PartitionSpec as P

D = 4096
FILT = 7


EPS = 1e-06
HIGH = lax.Precision.HIGHEST


def passed_along(shard, axis, by):
    peers = lax.axis_size(axis)
    pairs = [(i, i + by) for i in range(peers) if 0 <= i + by < peers]
    return lax.ppermute(shard, axis, pairs)


def phases(first, second, modulus):
    product = first[:, None] * second[None, :] % modulus
    return product.astype(jnp.float32) * (2.0 * math.pi / modulus)


def block_table(block_len, sign):
    index = jnp.arange(block_len, dtype=jnp.int32)
    angle = phases(index, index, block_len)
    cosine = jnp.cos(angle)
    sine = jnp.sin(angle) * sign
    return jnp.stack([jnp.stack([cosine, sine]), jnp.stack([-sine, cosine])])


def forward_rows(values, modulus):
    count, block_len, width = values.shape
    ctx_size = lax.axis_size("context")
    sub_len = block_len // ctx_size
    spread = lax.all_to_all(
        values.reshape(count, 1, block_len, width),
        "context",
        split_axis=2,
        concat_axis=1,
        tiled=True,
    )
    freq = jnp.arange(2 * ctx_size, dtype=jnp.int32)
    place = (
        jnp.arange(ctx_size, dtype=jnp.int32)[:, None] * block_len
        + lax.axis_index("context") * sub_len
        + jnp.arange(sub_len, dtype=jnp.int32)[None, :]
    )
    angle = (freq[:, None, None] * place[None] % modulus).astype(jnp.float32) * (
        2.0 * math.pi / modulus
    )
    table = jnp.stack([jnp.cos(angle), -jnp.sin(angle)])
    turned = jnp.einsum("pkcs,ncsx->npksx", table, spread, precision=HIGH)
    moved = lax.all_to_all(turned, "context", split_axis=2, concat_axis=3, tiled=True)
    return jnp.einsum("pqmb,nqjbx->npjmx", block_table(block_len, 1.0), moved, precision=HIGH)


def inverse_rows(spec, modulus):
    rows = spec.shape[2]
    block_len = spec.shape[3]
    ctx_size = lax.axis_size("context")
    index = jnp.arange(block_len, dtype=jnp.int32)
    freq = 2 * lax.axis_index("context") + jnp.arange(rows, dtype=jnp.int32)
    total = freq[:, None, None] + 2 * ctx_size * index[None, :, None]
    angle = (total * index[None, None, :] % modulus).astype(jnp.float32) * (2.0 * math.pi / modulus)
    cosine = jnp.cos(angle)
    sine = jnp.sin(angle)
    table = jnp.stack([jnp.stack([cosine, -sine]), jnp.stack([sine, cosine])])
    turned = jnp.einsum("pqjmb,nqjmx->npjbx", table, spec, precision=HIGH)
    moved = lax.all_to_all(turned, "context", split_axis=3, concat_axis=2, tiled=True)
    outer = phases(
        jnp.arange(ctx_size, dtype=jnp.int32),
        jnp.arange(2 * ctx_size, dtype=jnp.int32),
        2 * ctx_size,
    )
    real_table = jnp.stack([jnp.cos(outer), -jnp.sin(outer)])
    values = jnp.einsum("qck,nqksx->ncsx", real_table, moved, precision=HIGH) / modulus
    back = lax.all_to_all(values, "context", split_axis=1, concat_axis=2, tiled=True)
    return back.reshape(back.shape[0], back.shape[2], back.shape[3])


def shards(q_in, k_in, v_in, short_filt, long_filt, norm_gain, grad_out):
    block_len = q_in.shape[1]
    channels = q_in.shape[2]
    edge_rows = FILT - 1
    modulus = 2 * lax.axis_size("context") * block_len
    branches = jnp.stack([q_in[0], k_in[0], v_in[0]])
    before = passed_along(branches[:, block_len - edge_rows :], "context", 1)
    inputs = jnp.concatenate([before, branches], 1).astype(jnp.float32)
    shorts = jnp.zeros((3, block_len, channels), jnp.float32)
    for lag in range(FILT):
        shorts = (
            shorts
            + short_filt[:, lag][:, None, :]
            * inputs[:, edge_rows - lag : edge_rows - lag + block_len]
        )
    q_short = shorts[0]
    k_short = shorts[1]
    v_short = shorts[2]
    kv_prod = k_short * v_short
    spectra = forward_rows(jnp.stack([kv_prod, long_filt]), modulus)
    kv_real, kv_imag = (spectra[0, 0], spectra[0, 1])
    filt_real, filt_imag = (spectra[1, 0], spectra[1, 1])
    conv_spec = jnp.stack(
        [kv_real * filt_real - kv_imag * filt_imag, kv_real * filt_imag + kv_imag * filt_real]
    )[None]
    conv = inverse_rows(conv_spec, modulus)[0]
    y_out = q_short * conv
    squares = lax.psum(jnp.sum(y_out * y_out, axis=-1), "tensor")
    rms = jnp.sqrt(squares / D + EPS)[:, None]
    mixed = (y_out / rms * norm_gain).astype(jnp.bfloat16)[None]
    grad_z = grad_out[0].astype(jnp.float32) * norm_gain
    prods = lax.psum(jnp.sum(grad_z * y_out, axis=-1), "tensor")[:, None]
    grad_y = grad_z / rms - y_out * prods / (D * rms**3)
    dconv = grad_y * q_short
    grad_q = grad_y * conv
    grad_spec = forward_rows(dconv[None], modulus)[0]
    grad_real = grad_spec[0]
    grad_imag = grad_spec[1]
    dkv_spec = jnp.stack(
        [
            filt_real * grad_real + filt_imag * grad_imag,
            filt_real * grad_imag - filt_imag * grad_real,
        ]
    )
    dfilt_spec = jnp.stack(
        [kv_real * grad_real + kv_imag * grad_imag, kv_real * grad_imag - kv_imag * grad_real]
    )
    results = inverse_rows(jnp.stack([dkv_spec, dfilt_spec]), modulus)
    dkv = results[0]
    dfilt_local = results[1]
    grads = jnp.stack([grad_q, dkv * v_short, dkv * k_short])
    after = passed_along(grads[:, :edge_rows].astype(jnp.bfloat16), "context", -1).astype(
        jnp.float32
    )
    extended = jnp.concatenate([grads, after], 1)
    grad_inputs = jnp.zeros((3, block_len, channels), jnp.float32)
    for lag in range(FILT):
        grad_inputs = (
            grad_inputs + short_filt[:, lag][:, None, :] * extended[:, lag : lag + block_len]
        )
    short_local = jnp.stack(
        [
            jnp.sum(grads * inputs[:, edge_rows - lag : edge_rows - lag + block_len], axis=1)
            for lag in range(FILT)
        ],
        1,
    )
    scale = 1.0 / math.sqrt(lax.axis_size("dp") * block_len * lax.axis_size("context"))
    grad_long = lax.psum(dfilt_local, "dp") * scale
    grad_short = lax.psum(short_local, ("dp", "context")) * scale
    return (mixed, grad_inputs.astype(jnp.bfloat16)[:, None], grad_long, grad_short)

MESH = pl.DeviceIdType.MESH
F32 = jnp.float32
BF16 = jnp.bfloat16
PAD = 16
ROWS = 32


def split_table(table):
    high = table.astype(jnp.bfloat16)
    low = (table - high.astype(np.float64)).astype(jnp.bfloat16)
    return high, low


def odd_tables(seq):
    freq = 2 * np.arange(seq)[:, None] + 1
    angle = (freq * np.arange(seq)[None, :] % (4 * seq)) * (np.pi / (2 * seq))
    groups = (seq // 128, 1, 128, seq)
    forward = np.concatenate([np.cos(angle).reshape(groups), -np.sin(angle).reshape(groups)], 1)
    forward = forward.reshape(2 * seq, seq)
    return split_table(forward) + split_table(np.ascontiguousarray(forward.T) / seq)


def halves(values):
    high = values.astype(BF16)
    return high, (values - high.astype(F32)).astype(BF16)


def dot(a, b):
    return jnp.dot(a, b, preferred_element_type=F32)


def dot3(ah, al, bh, bl):
    return dot(ah, bh) + (dot(ah, bl) + dot(al, bh))


def operator_kernel(
    model_width,
    total_rows,
    q_in,
    k_in,
    v_in,
    g_in,
    f_in,
    short_in,
    gains_in,
    wh_in,
    wl_in,
    vh_in,
    vl_in,
    mixed,
    grad_inputs,
    grad_long,
    grad_short,
    staged,
    f_staged,
    branch,
    filt,
    wh,
    wl,
    vh,
    vl,
    short_filt,
    gain_in,
    shorts,
    op_h,
    op_l,
    spec_kv,
    spec_f,
    prod_h,
    prod_l,
    conv,
    y_buf,
    sums,
    stats,
    grads,
    dfilt,
    dfilt_in,
    dfilt_sum,
    long_buf,
    short_sum,
    sent,
    in_send,
    in_recv,
    in_local,
    stage_sem,
    hop_send,
    hop_recv,
    tab_sem,
    st_send,
    st_recv,
    out_send,
    out_recv,
    out_local,
    df_send,
    df_recv,
    gl_send,
    gl_recv,
    gl_local,
    fw_send,
    fw_recv,
    sh_send,
    sh_recv,
    gs_send,
    gs_recv,
    gs_local,
):
    ctx = lax.axis_size("context")
    tens = lax.axis_size("tensor")
    dp = lax.axis_index("dp")
    me = lax.axis_index("context")
    row = lax.axis_index("tensor")
    block = q_in.shape[0]
    seq = block * ctx
    width = branch.shape[2]
    half = width // 2
    taps = short_filt.shape[1]
    other = {"dp": 1 - dp}

    steps = (2, 3, 1)

    def peer(step):
        if step == 1:
            return me + 1 - 2 * (me % 2)
        if step == 2:
            return lax.rem(me + 2, ctx)
        return 3 - me if step == 3 else me

    source = peer

    def rows_of(p):
        return pl.ds(pl.multiple_of(p * block, block), block)

    def cols_of(p):
        return pl.ds(pl.multiple_of(p * width, width), width)

    def half_cols(p, h):
        return pl.ds(pl.multiple_of(p * width + h * half, half), half)

    def remote(src, dst, send, recv, device):
        copy = pltpu.make_async_remote_copy(
            src_ref=src, dst_ref=dst, send_sem=send, recv_sem=recv, device_id=device, device_id_type=MESH
        )
        copy.start()
        return copy

    def local(src, dst, sem):
        copy = pltpu.make_async_copy(src, dst, sem)
        copy.start()
        return copy

    f_load = local(f_in, f_staged, stage_sem.at[4])
    loads = {n: local(ref, staged.at[n], stage_sem.at[n]) for n, ref in ((1, k_in), (2, v_in), (0, q_in), (3, g_in))}

    barrier = pltpu.get_barrier_semaphore()
    near = [(a, b) for a in range(tens) for b in range(ctx) if a + b > 0]
    for a, b in near:
        pl.semaphore_signal(
            barrier,
            inc=1,
            device_id={"tensor": lax.rem(row + a, tens), "context": peer(b)},
            device_id_type=MESH,
        )
    pl.semaphore_signal(barrier, inc=1, device_id=other, device_id_type=MESH)
    pl.semaphore_wait(barrier, len(near) + 1)

    f_load.wait()
    f_copies = [
        remote(
            f_staged.at[:, half_cols(peer(off), dp)],
            filt.at[dp, rows_of(me), :],
            in_send.at[4, off],
            in_recv.at[4, off],
            {"context": peer(off)},
        )
        for off in steps
    ]
    f_own = local(f_staged.at[:, half_cols(me, dp)], filt.at[dp, rows_of(me), :], in_local.at[4])
    land = pl.ds(pl.multiple_of(PAD + me * block, PAD), block)
    arrivals = {}

    def fetch(n):
        loads[n].wait()
        ref = staged.at[n]
        arrivals[n] = [
            remote(
                ref.at[:, cols_of(peer(off))],
                branch.at[n, land, :],
                in_send.at[n, off],
                in_recv.at[n, off],
                {"context": peer(off)},
            )
            for off in steps
        ]
        arrivals[n].append(local(ref.at[:, cols_of(me)], branch.at[n, land, :], in_local.at[n]))

    fetch(1)
    fetch(2)
    small = [local(short_in, short_filt, tab_sem.at[4]), local(gains_in, gain_in, tab_sem.at[5])]
    tables = [
        local(src, dst, tab_sem.at[n])
        for n, (src, dst) in enumerate([(wh_in, wh), (wl_in, wl), (vh_in, vh), (vl_in, vl)])
    ]

    def arrived(n):
        for copy in arrivals[n][:-1]:
            copy.wait_recv()
        arrivals[n][-1].wait()

    branch[:, :PAD, :] = jnp.zeros((4, PAD, width), BF16)
    grads[:, seq:, :] = jnp.zeros((3, 8, width), F32)

    for copy in small:
        copy.wait()

    def taps_of(n):
        return [short_filt[n, j : j + 1, cols_of(me)] for j in range(taps)]

    gain = gain_in[:, cols_of(me)]

    def at(i, rows=ROWS):
        return pl.ds(pl.multiple_of(i * rows, rows), rows)

    def short_conv(n, i, weights):
        piece = branch[n, pl.ds(pl.multiple_of(i * ROWS, ROWS), ROWS + PAD), :].astype(F32)
        total = weights[0] * piece[PAD : PAD + ROWS]
        for j in range(1, taps):
            total = total + weights[j] * piece[PAD - j : PAD - j + ROWS]
        return total

    def forward(use):
        @pl.loop(0, 2 * seq // 256, unroll=True)
        def _(m):
            rows = at(m, 256)
            use(rows, dot3(wh[rows, :], wl[rows, :], op_h[...], op_l[...]))

    def inverse(n, store):
        @pl.loop(0, seq // 256, unroll=True)
        def _(m):
            rows = at(m, 256)
            store(rows, dot3(vh[rows, :], vl[rows, :], prod_h[n], prod_l[n]))

    def multiply(n, rows, left, right, sign):
        a, b = left[:128], left[128:] * sign
        c, d = right[:128], right[128:]
        prod = jnp.concatenate([a * c - b * d, a * d + b * c], 0)
        prod_h[n, rows, :], prod_l[n, rows, :] = halves(prod)

    for copy in f_copies:
        copy.wait_recv()
    f_own.wait()
    f_hop = remote(filt.at[dp], filt.at[dp], hop_send, hop_recv, other)
    fetch(0)

    arrived(1)
    fetch(3)
    k_taps = taps_of(1)

    @pl.loop(0, seq // ROWS, unroll=2)
    def _(i):
        shorts[1, at(i), :] = short_conv(1, i, k_taps)

    arrived(2)
    v_taps = taps_of(2)

    @pl.loop(0, seq // ROWS, unroll=2)
    def _(i):
        vs = short_conv(2, i, v_taps)
        shorts[2, at(i), :] = vs
        op_h[at(i), :], op_l[at(i), :] = halves(shorts[1, at(i), :] * vs)

    for copy in tables:
        copy.wait()

    def keep_kv(rows, values):
        spec_kv[rows, :] = values

    forward(keep_kv)

    f_hop.wait_recv()

    @pl.loop(0, seq // ROWS, unroll=2)
    def _(i):
        op_h[at(i), :half], op_l[at(i), :half] = halves(filt[0, at(i), :])
        op_h[at(i), half:], op_l[at(i), half:] = halves(filt[1, at(i), :])

    def keep_f(rows, values):
        spec_f[rows, :] = values
        multiply(0, rows, spec_kv[rows, :], values, 1.0)

    forward(keep_f)

    def store_conv(rows, values):
        conv[rows, :] = values

    inverse(0, store_conv)

    arrived(0)
    q_taps = taps_of(0)

    def folded(values):
        total = values[:, :128]
        for n in range(1, width // 128):
            total = total + values[:, n * 128 : (n + 1) * 128]
        return total

    @pl.loop(0, seq // ROWS, unroll=2)
    def _(i):
        qs = short_conv(0, i, q_taps)
        shorts[0, at(i), :] = qs
        y = qs * conv[at(i), :]
        y_buf[at(i), :] = y
        sums[0, at(i), :] = folded(y * y)

    groups = seq // 128
    lane = lax.broadcasted_iota(jnp.int32, (128, 128), 1)

    def share(n):
        columns = jnp.zeros((128, 128), F32)
        for b in range(groups):
            part = jnp.sum(sums[n, b * 128 : (b + 1) * 128, :], axis=1, keepdims=True)
            columns = jnp.where(lane == b, part, columns)
        stats[n, 0] = columns.T[:8]
        return [
            remote(
                stats.at[n, 0],
                stats.at[n, a * ctx + b],
                st_send.at[n, a * ctx + b],
                st_recv.at[n, a * ctx + b],
                {"tensor": lax.rem(row + a, tens), "context": peer(b)},
            )
            for a, b in near
        ]

    def gathered(n, copies):
        for copy in copies:
            copy.wait_recv()
        total = stats[n, 0]
        for r in range(1, tens * ctx):
            total = total + stats[n, r]
        return total

    def widen(n, values):
        spread = jnp.concatenate([values, jnp.zeros((120, 128), F32)], 0).T
        for b in range(groups):
            sums[n, b * 128 : (b + 1) * 128, :] = jnp.broadcast_to(spread[:, b : b + 1], (128, 128))

    st_copies = share(0)
    arrived(3)

    @pl.loop(0, seq // ROWS, unroll=2)
    def _(i):
        gz = branch[3, pl.ds(pl.multiple_of(PAD + i * ROWS, PAD), ROWS), :].astype(F32) * gain
        sums[1, at(i), :] = folded(gz * y_buf[at(i), :])

    prod_copies = share(1)
    inv = 1.0 / jnp.sqrt(gathered(0, st_copies) / model_width + EPS)
    widen(0, inv)

    def wide(n, i):
        return jnp.concatenate([sums[n, at(i), :]] * (width // 128), 1)

    @pl.loop(0, seq // ROWS, unroll=2)
    def _(i):
        sent[3, at(i), :] = (y_buf[at(i), :] * wide(0, i) * gain).astype(BF16)

    def send_back(n, target):
        copies = [
            remote(
                sent.at[n, rows_of(peer(off)), :],
                target,
                out_send.at[n, off],
                out_recv.at[n, off],
                {"context": peer(off)},
            )
            for off in steps
        ]
        return copies, local(sent.at[n, rows_of(me), :], target, out_local.at[n])

    back = [send_back(3, mixed.at[0, :, cols_of(me)])]
    widen(1, gathered(1, prod_copies) * (inv * inv * inv / model_width))

    @pl.loop(0, seq // ROWS, unroll=2)
    def _(i):
        gz = branch[3, pl.ds(pl.multiple_of(PAD + i * ROWS, PAD), ROWS), :].astype(F32) * gain
        dy = gz * wide(0, i) - y_buf[at(i), :] * wide(1, i)
        op_h[at(i), :], op_l[at(i), :] = halves(dy * shorts[0, at(i), :])
        grads[0, at(i), :] = dy * conv[at(i), :]

    scale = 1.0 / math.sqrt(total_rows)

    def back_short(n):
        weights = taps_of(n)

        @pl.loop(0, seq // ROWS, unroll=2)
        def _(i):
            piece = grads[n, pl.ds(pl.multiple_of(i * ROWS, ROWS), ROWS + 8), :]
            total = weights[0] * piece[:ROWS]
            for j in range(1, taps):
                total = total + weights[j] * piece[j : j + ROWS]
            sent[n, at(i), :] = total.astype(BF16)

        back.append(send_back(n, grad_inputs.at[n, 0, :, cols_of(me)]))

    def short_grads(n):
        def body(i, acc):
            own = grads[n, at(i), :]
            inputs = branch[n, pl.ds(pl.multiple_of(i * ROWS, ROWS), ROWS + PAD), :].astype(F32)
            out = []
            for j in range(taps):
                prod = own * inputs[PAD - j : PAD - j + ROWS]
                part = acc[j]
                for r in range(ROWS // 8):
                    part = part + prod[r * 8 : (r + 1) * 8]
                out.append(part)
            return tuple(out)

        acc = lax.fori_loop(0, seq // ROWS, body, tuple(jnp.zeros((8, width), F32) for _ in range(taps)))
        for j in range(taps):
            short_sum[0, n, j : j + 1, :] = jnp.sum(acc[j], axis=0, keepdims=True) * scale

    back_short(0)

    def use_g(rows, values):
        multiply(0, rows, spec_kv[rows, :], values, -1.0)
        multiply(1, rows, spec_f[rows, :], values, -1.0)

    forward(use_g)

    def store_dfilt(rows, values):
        dfilt[0, rows, :] = values[:, :half] * scale
        dfilt[1, rows, :] = values[:, half:] * scale

    inverse(0, store_dfilt)
    df_copy = remote(dfilt.at[1 - dp], dfilt_in, df_send, df_recv, other)

    def store_dkv(rows, values):
        grads[1, rows, :] = values * shorts[2, rows, :]
        grads[2, rows, :] = values * shorts[1, rows, :]

    inverse(1, store_dkv)
    back_short(1)
    back_short(2)
    short_grads(0)
    df_copy.wait_recv()
    dfilt_sum[...] = (dfilt[dp] + dfilt_in[...]).astype(BF16)
    gl_target = grad_long.at[:, half_cols(me, dp)]
    gl_copies = [
        remote(
            dfilt_sum.at[rows_of(peer(off)), :],
            long_buf.at[off],
            gl_send.at[off],
            gl_recv.at[off],
            {"context": peer(off)},
        )
        for off in steps
    ]
    gl_own = [local(dfilt_sum.at[rows_of(me), :], gl_target, gl_local.at[0])]
    forwards = [remote(dfilt_sum.at[rows_of(me), :], gl_target, fw_send.at[0], fw_recv.at[0], other)]

    for n in (1, 2):
        short_grads(n)
    sh_copy = remote(short_sum.at[0], short_sum.at[1], sh_send, sh_recv, other)

    for off in steps:
        gl_copies[steps.index(off)].wait_recv()
        piece = grad_long.at[:, half_cols(source(off), dp)]
        forwards.append(remote(long_buf.at[off], piece, fw_send.at[off], fw_recv.at[off], other))
        gl_own.append(local(long_buf.at[off], piece, gl_local.at[off]))
    sh_copy.wait_recv()
    short_sum[2] = short_sum[0] + short_sum[1]
    gs_target = grad_short.at[:, :, cols_of(me)]
    gs_copies = [
        remote(short_sum.at[2], gs_target, gs_send.at[off], gs_recv.at[off], {"context": peer(off)})
        for off in steps
    ]
    gs_own = local(short_sum.at[2], gs_target, gs_local)
    for copies, own in back:
        own.wait()
        for copy in copies:
            copy.wait()
    for copy in gl_own:
        copy.wait()
    for copy in gl_copies:
        copy.wait_send()
    for copy in forwards:
        copy.wait()
    gs_own.wait()
    for copy in gs_copies:
        copy.wait()
    sh_copy.wait_send()
    df_copy.wait_send()
    f_hop.wait_send()
    for copy in f_copies + st_copies + prod_copies:
        copy.wait_send()
    for n in range(4):
        for copy in arrivals[n][:-1]:
            copy.wait_send()


def deliver_kernel(
    mixed, grad_inputs, grad_long, grad_short, mixed_out, inputs_out, long_out, short_out, held, narrow, wide, short, sem
):
    def move(n, src, dst):
        copy = pltpu.make_async_copy(src, dst, sem.at[n])
        copy.start()
        return copy

    loads = [move(0, grad_long, narrow), move(1, mixed.at[0], held.at[0])]
    loads += [move(2 + n, grad_inputs.at[n, 0], held.at[1 + n]) for n in range(3)]
    loads.append(move(5, grad_short, short))
    loads[0].wait()
    wide[...] = narrow[...].astype(F32)
    stores = [move(6, wide, long_out)]
    targets = [mixed_out.at[0]] + [inputs_out.at[n, 0] for n in range(3)]
    for n in range(4):
        loads[1 + n].wait()
        stores.append(move(7 + n, held.at[n], targets[n]))
    loads[5].wait()
    stores.append(move(11, short, short_out))
    for copy in stores:
        copy.wait()


def fused(q_in, k_in, v_in, short_filt, long_filt, norm_gain, grad_out):
    _, block, channels = q_in.shape
    ctx = lax.axis_size("context")
    tens = lax.axis_size("tensor")
    seq = block * ctx
    width = channels // ctx
    tables = [jnp.asarray(t) for t in odd_tables(seq)]
    dma = pltpu.SemaphoreType.DMA
    anywhere = pl.BlockSpec(memory_space=pl.ANY)
    in_hbm = pl.BlockSpec(memory_space=pltpu.HBM)
    outs = pl.pallas_call(
        functools.partial(operator_kernel, D, lax.axis_size("dp") * seq),
        out_shape=(
            jax.ShapeDtypeStruct((1, block, channels), BF16),
            jax.ShapeDtypeStruct((3, 1, block, channels), BF16),
            jax.ShapeDtypeStruct((block, channels), BF16),
            jax.ShapeDtypeStruct(short_filt.shape, F32),
        ),
        in_specs=[in_hbm] * 11,
        out_specs=(anywhere,) * 4,
        scratch_shapes=[
            pltpu.VMEM((4, block, channels), BF16),
            pltpu.VMEM((block, channels), F32),
            pltpu.VMEM((4, PAD + seq, width), BF16),
            pltpu.VMEM((2, seq, width // 2), F32),
            pltpu.VMEM((2 * seq, seq), BF16),
            pltpu.VMEM((2 * seq, seq), BF16),
            pltpu.VMEM((seq, 2 * seq), BF16),
            pltpu.VMEM((seq, 2 * seq), BF16),
            pltpu.VMEM(short_filt.shape, F32),
            pltpu.VMEM((1, channels), F32),
            pltpu.VMEM((3, seq, width), F32),
            pltpu.VMEM((seq, width), BF16),
            pltpu.VMEM((seq, width), BF16),
            pltpu.VMEM((2 * seq, width), F32),
            pltpu.VMEM((2 * seq, width), F32),
            pltpu.VMEM((2, 2 * seq, width), BF16),
            pltpu.VMEM((2, 2 * seq, width), BF16),
            pltpu.VMEM((seq, width), F32),
            pltpu.VMEM((seq, width), F32),
            pltpu.VMEM((2, seq, 128), F32),
            pltpu.VMEM((2, tens * ctx, 8, 128), F32),
            pltpu.VMEM((3, seq + 8, width), F32),
            pltpu.VMEM((2, seq, width // 2), F32),
            pltpu.VMEM((seq, width // 2), F32),
            pltpu.VMEM((seq, width // 2), BF16),
            pltpu.VMEM((ctx, block, width // 2), BF16),
            pltpu.VMEM((3, 3, short_filt.shape[1], width), F32),
            pltpu.VMEM((4, seq, width), BF16),
            dma((5, ctx)),
            dma((5, ctx)),
            dma((5,)),
            dma((5,)),
            dma,
            dma,
            dma((6,)),
            dma((2, tens * ctx)),
            dma((2, tens * ctx)),
            dma((4, ctx)),
            dma((4, ctx)),
            dma((4,)),
            dma,
            dma,
            dma((ctx,)),
            dma((ctx,)),
            dma((ctx,)),
            dma((ctx,)),
            dma((ctx,)),
            dma,
            dma,
            dma((ctx,)),
            dma((ctx,)),
            dma,
        ],
        compiler_params=pltpu.CompilerParams(
            collective_id=0, has_side_effects=True, vmem_limit_bytes=60 * 2**20
        ),
    )(
        q_in[0],
        k_in[0],
        v_in[0],
        grad_out[0],
        long_filt,
        short_filt,
        norm_gain[None],
        *tables,
    )
    return pl.pallas_call(
        deliver_kernel,
        out_shape=(
            jax.ShapeDtypeStruct((1, block, channels), BF16),
            jax.ShapeDtypeStruct((3, 1, block, channels), BF16),
            jax.ShapeDtypeStruct((block, channels), F32),
            jax.ShapeDtypeStruct(short_filt.shape, F32),
        ),
        in_specs=[anywhere] * 4,
        out_specs=(anywhere,) * 4,
        scratch_shapes=[
            pltpu.VMEM((4, block, channels), BF16),
            pltpu.VMEM((block, channels), BF16),
            pltpu.VMEM((block, channels), F32),
            pltpu.VMEM(short_filt.shape, F32),
            dma((12,)),
        ],
        compiler_params=pltpu.CompilerParams(vmem_limit_bytes=60 * 2**20),
    )(*outs)


def operator(q_in, k_in, v_in, short_filt, long_filt, norm_gain, grad_out):
    _, block, channels = q_in.shape
    ctx = lax.axis_size("context")
    dense = block * ctx <= 1024 and block % 128 == 0 and channels % (256 * ctx) == 0
    form = fused if dense and lax.axis_size("dp") == 2 and ctx == 4 else shards
    return form(q_in, k_in, v_in, short_filt, long_filt, norm_gain, grad_out)


def solution(mesh):
    in_specs = (
        P("dp", "context", "tensor"),
        P("dp", "context", "tensor"),
        P("dp", "context", "tensor"),
        P(None, None, "tensor"),
        P("context", "tensor"),
        P("tensor"),
        P("dp", "context", "tensor"),
    )
    out_specs = (
        P("dp", "context", "tensor"),
        P(None, "dp", "context", "tensor"),
        P("context", "tensor"),
        P(None, None, "tensor"),
    )
    return jax.shard_map(operator, mesh=mesh, in_specs=in_specs, out_specs=out_specs, check_vma=False)
```
